256 devices in a mesh: pair: 16 (over y, x), side: 2 (over core), grp: 8 (over z).
Axes of the slice: x: 4, y: 4, z: 8, core: 2. Of those that a mesh axis runs over, the one named last changes fastest.
Arguments:
- coeffs: bfloat16 [16, 2, 8, 20, 64, 576], P('pair', 'side', 'grp'), may hold values from -6 to 6
- lengths: int32 [16, 4], replicated, may hold values from 1 to 8, 20 in all within a row
- owners: int32 [64, 1], replicated, may hold values from 0 to 15; in each aligned block of 4 rows (0 to 3, 4 to 7, ...) no two rows name the same one
- row_pick: int32 [128], P('pair'), may hold values from 0 to 1048575
- queries: bfloat16 [128, 4, 128, 576], P('pair', None, 'side'), may hold values from -400 to 400
- new_latent: bfloat16 [128, 4, 576], P('pair'), may hold values from -6 to 6
Outputs:
- attended: bfloat16 [128, 4, 128, 512], P('pair', None, 'side')
The draws below stay inside these ranges and needn't reach their ends.
Inputs may be any that keep to these rules, and one draw needn't show every extreme that they name: `lengths`: each pair's row sums to 20, and its largest entry is 8. `owners`: each aligned block of 4 requests (those of one pair) names no owner more than 1 times, some block names one owner exactly 1 times, and every owner is named.
All inputs are finite; a program needn't handle non-finite values.
Results may differ from the reference program's by a relative error of at most 0.0018.
The reference program's roundings to bfloat16 on the way count: a program that leaves them out, or rounds other values in their place, can miss the bound.
Values may be sent and summed in bfloat16 or wider, within the bound.
No kernel may reach another device: no remote copies, remote signals or barrier semaphores. Data moves between devices by JAX's collectives and lax.ppermute only.
A program may use at most 128 MiB of HBM per device.

```python
import math
import jax
import jax.numpy as jnp
import numpy as np
from jax import lax

H = 128
LAT = 512
KV = 576
BLK = 64
STEPS = 4
ROWS = 8
MOST_M = 8
CAPR = 1
REQ_PAIR = 4
STORE = 20
REQS = 64
N_PAIR = 16
N_SIDE = 2
N_GRP = 8


def draw_queries(key, part):
    key = jax.random.fold_in(key, 11)
    base_key = jax.random.fold_in(key, 0)
    values = jax.random.normal(base_key, (N_PAIR * ROWS, STEPS, H, KV), jnp.float32)
    return jnp.clip(values, -400.0, 400.0).astype(jnp.bfloat16)


def with_ends(entries, stream_key, least, top_value):
    shape = entries.shape
    spot = [jax.random.randint(jax.random.fold_in(stream_key, axis), (), 0, shape[axis]) for axis in range(len(shape))]
    entries = entries.at[tuple(spot)].set(least)
    longest = shape.index(max(shape))
    spot[longest] = (spot[longest] + 1) % shape[longest]
    return entries.at[tuple(spot)].set(top_value)


def levels(rng, shape, shards, smallest, largest):
    level, own = 1.0, jax.random.fold_in(rng, 6)
    for axis_at, parts in shards:
        draws = jnp.exp(jax.random.uniform(jax.random.fold_in(own, axis_at), (parts,), jnp.float32, smallest / len(shards), largest / len(shards)))
        level = level * jnp.repeat(draws, shape[axis_at] // parts).reshape([-1 if axis == axis_at else 1 for axis in range(len(shape))])
    return level


def profile(number_of, total, limit, slope):
    weights = [(1 << 20) // math.isqrt(grade ** slope) + 1 for grade in range(2, number_of + 1)]
    surplus, counts = total - limit - (number_of - 1), [1] * (number_of - 1)
    while surplus > 0:
        candidates = [i for i in range(number_of - 1) if counts[i] < limit]
        mass, left = sum([weights[i] for i in candidates]), surplus
        for i in candidates:
            extra = min(limit - counts[i], max(1, left * weights[i] // mass), surplus)
            counts[i] = counts[i] + extra
            surplus = surplus - extra
    return np.array([limit] + counts)


def uneven(own_key, count, total, bound, skew):
    if count == 2:
        one = jax.random.randint(own_key, (), max(1, total - bound), min(bound, total - 1) + 1)
        return jnp.stack([one, total - one])
    tallies = jnp.asarray(profile(count, total, bound, skew), jnp.int32)
    pairs = (count - 1) // 2
    giver, receiver = tallies[1:1 + 2 * pairs:2], tallies[2:2 + 2 * pairs:2]
    slack = jnp.minimum(giver - 1, bound - receiver)
    moved = jax.random.randint(jax.random.fold_in(own_key, 1), (pairs,), 0, 1 << 20) % (slack + 1)
    tallies = tallies.at[1:1 + 2 * pairs:2].set(giver - moved).at[2:2 + 2 * pairs:2].set(receiver + moved)
    return tallies[jax.random.permutation(jax.random.fold_in(own_key, 2), count)]


def deal_out(stream_key, own, number, rows, number_of, top, most, slope):
    order = jax.random.permutation(stream_key, number_of)
    crowded, usual = shares(number_of, rows * top, most, slope, True), shares(number_of, rows * top, most, slope, False)
    places = jnp.arange(number_of)

    def named(sizes, offset_by):
        used = int((sizes > 0).sum())
        fixed = max(1, used // 4)
        shifted = fixed + (places - fixed + offset_by * (used - fixed)) % max(1, number_of - fixed)
        return jnp.zeros((number_of,), jnp.int32).at[order[jnp.where(places < fixed, places, shifted)]].set(jnp.asarray(sizes, jnp.int32))

    sizes = jnp.where(number % 4 == 0, named(crowded, number // 4), named(usual, number - number // 4 - 1))
    mixed = jax.random.permutation(jax.random.fold_in(own, 3), number_of)
    donor, receiver = mixed[0:number_of // 2 * 2:2], mixed[1:number_of // 2 * 2:2]
    margin = jnp.minimum(sizes[donor] - 1, most - sizes[receiver]) // 2
    margin = jnp.where((donor == order[0]) | (receiver == order[0]) | (sizes[receiver] == 0), 0, jnp.maximum(margin, 0))
    shifted = jax.random.randint(jax.random.fold_in(own, 4), (number_of // 2,), 0, 1 << 20) % (margin + 1)
    sizes = sizes.at[donor].add(-shifted).at[receiver].add(shifted)
    members = jnp.searchsorted(jnp.cumsum(sizes), jnp.arange(rows * top), side="right").astype(jnp.int32)
    grid = members.reshape(top, rows).T
    grid = grid[jax.random.permutation(jax.random.fold_in(own, 1), rows)]
    offset_by = jax.random.randint(jax.random.fold_in(own, 2), (rows, 1), 0, top)
    return jnp.take_along_axis(grid, (jnp.arange(top)[None, :] + offset_by) % top, axis=1)


def shares(number_of, total, reach, skew, full):
    weights = [(1 << 20) // math.isqrt(rank ** skew) + 1 for rank in range(1, number_of + 1)]
    largest = reach if full else min(reach, max(-(-total // number_of), total * weights[0] // sum(weights)))
    least = 1 if total - largest >= number_of - 1 else 0
    given, spare = [largest] + [least] * (number_of - 1), total - largest - least * (number_of - 1)
    while spare > 0:
        movable = [i for i in range(1, number_of) if given[i] < largest] or [i for i in range(1, number_of) if given[i] < reach]
        pool, budget = sum([weights[i] for i in movable]), spare
        for i in movable:
            extra = min(reach - given[i], max(1, budget * weights[i] // pool), spare)
            given[i] = given[i] + extra
            spare = spare - extra
    return np.array(given)


def gaussian(own_key, shape, scale, limit, cuts=(), kind=jnp.bfloat16):
    array = scale * jax.random.normal(own_key, shape, jnp.float32)
    if cuts:
        array = array * levels(own_key, shape, cuts, -0.22, 0.18)
    return jnp.clip(array, -limit, limit).astype(kind)


def setup_inputs(seed: int = 0) -> dict:
    arg_keys = jax.random.split(jax.random.key(seed), 7)
    coeffs = gaussian(arg_keys[0], (N_PAIR, N_SIDE, N_GRP, STORE, BLK, KV), 1.0, 6.0, ((0, 16), (1, 2), (2, 8)))
    lengths = jax.vmap(lambda own: uneven(own, REQ_PAIR, STORE, MOST_M, 2))(jax.random.split(arg_keys[1], N_PAIR)).reshape((N_PAIR, REQ_PAIR)).astype(jnp.int32)
    owners_keys = jax.random.split(jax.random.fold_in(arg_keys[2], 1), REQS // REQ_PAIR)
    owners_turns = jax.random.permutation(jax.random.fold_in(arg_keys[2], 3), REQS // REQ_PAIR)
    owners = jax.vmap(lambda own, number: deal_out(jax.random.fold_in(arg_keys[2], 2), own, number, REQ_PAIR, N_PAIR, 1, CAPR, 2))(owners_keys, owners_turns).reshape((REQS, 1))
    row_pick = with_ends(jax.random.randint(arg_keys[3], (N_PAIR * ROWS,), 0, 1048576), jax.random.fold_in(arg_keys[3], 1), 0, 1048575).astype(jnp.int32)
    queries = draw_queries(jax.random.fold_in(arg_keys[6], 71), 0)
    new_latent = gaussian(arg_keys[5], (N_PAIR * ROWS, STEPS, KV), 1.0, 6.0, ((0, 16),))
    return {"coeffs": coeffs, "lengths": lengths, "owners": owners, "row_pick": row_pick, "queries": queries, "new_latent": new_latent}


score_scale = 192.0 ** (-0.5)

def dct_table_of(length_blocks):
    frequency = jnp.arange(length_blocks, dtype=jnp.float32)[:, None]
    position = jnp.arange(length_blocks, dtype=jnp.float32)[None, :]
    factor = jnp.where(frequency > 0, jnp.sqrt(2.0 / length_blocks), jnp.sqrt(1.0 / length_blocks))
    return (factor * jnp.cos(math.pi * (2.0 * position + 1.0) * frequency / (2.0 * length_blocks))).astype(jnp.bfloat16)

def owned_request(owner_list, pair_index, pick_value):
    mine_mask = (owner_list == pair_index).astype(jnp.int32)
    owned = jnp.sum(mine_mask)
    wanted = pick_value % owned
    ranking = jnp.cumsum(mine_mask) - mine_mask
    hit_mask = mine_mask * (ranking == wanted).astype(jnp.int32)
    return jnp.sum(hit_mask * jnp.arange(owner_list.shape[0], dtype=jnp.int32)).astype(jnp.int32)

def reference(coeffs, lengths, owners, row_pick, queries, new_latent):
    dct_table = dct_table_of(BLK).astype(jnp.float32)
    owner_list = owners[:, 0]
    offsets = jnp.cumsum(lengths, axis=1) - lengths
    causal = jnp.arange(STEPS)[None, :] <= jnp.arange(STEPS)[:, None]

    def one_row(row_index):
        pair_index = (row_index // ROWS).astype(jnp.int32)
        request = owned_request(owner_list, pair_index, row_pick[row_index])
        source = request // REQ_PAIR
        within = request % REQ_PAIR
        filled = lengths[source, within]
        offset = offsets[source, within]
        spot_rows = jnp.minimum(offset + jnp.arange(MOST_M, dtype=jnp.int32), STORE - 1).astype(jnp.int32)
        blocks = coeffs[source][:, :, spot_rows]
        latent = jnp.einsum('ft,sgifk->sgitk', dct_table, blocks.astype(jnp.float32)).astype(jnp.bfloat16)
        usable = jnp.broadcast_to((jnp.arange(MOST_M) < filled)[None, None, :, None], (N_SIDE, N_GRP, MOST_M, BLK)).reshape(-1)
        key_rows = latent.reshape(-1, KV).astype(jnp.float32)
        query_row = queries[row_index].astype(jnp.float32)
        scores = jnp.einsum('thk,nk->thn', query_row, key_rows) * score_scale
        scores = jnp.where(usable[None, None, :], scores, -jnp.inf)
        new_keys = new_latent[row_index].astype(jnp.float32)
        new_scores = jnp.einsum('thk,uk->thu', query_row, new_keys) * score_scale
        new_scores = jnp.where(causal[:, None, :], new_scores, -jnp.inf)
        row_top = jnp.maximum(lax.optimization_barrier(jnp.max(scores, axis=2)), lax.optimization_barrier(jnp.max(new_scores, axis=2)))
        weights = jnp.exp(scores - row_top[:, :, None])
        new_weights = jnp.exp(new_scores - row_top[:, :, None])
        denominator = lax.optimization_barrier(jnp.sum(weights, axis=2)) + lax.optimization_barrier(jnp.sum(new_weights, axis=2))
        weights_low = lax.optimization_barrier(weights.astype(jnp.bfloat16)).astype(jnp.float32)
        new_low = lax.optimization_barrier(new_weights.astype(jnp.bfloat16)).astype(jnp.float32)
        numerator = jnp.einsum('thn,nk->thk', weights_low, key_rows[:, :LAT])
        numerator = numerator + jnp.einsum('thu,uk->thk', new_low, new_keys[:, :LAT])
        return (numerator / denominator[:, :, None]).astype(jnp.bfloat16)
    return lax.map(one_row, jnp.arange(N_PAIR * ROWS, dtype=jnp.int32))
```

```python
import functools
import math

import jax
import jax.numpy as jnp
from jax import lax
from jax.experimental import pallas as pl
from jax.experimental.pallas import tpu as pltpu
from jax.sharding import PartitionSpec as P

LAT = 512
KV = 576
BLK = 64
HALF = 32
QUARTER = 16
STEPS = 4
MOST_M = 8
STORE = 20
ROWS = 8
HEADS = 64
QS = STEPS * HEADS
SIDE_LEN = 4
CAP = SIDE_LEN * MOST_M
GRP = 8
GROUP = 4
CHUNK = GROUP * BLK
VMEM_LIMIT = 56 * 1024 * 1024
RED = QS + 8
FLAG = STORE

score_scale = 192.0 ** (-0.5)
BF = jnp.bfloat16
F32 = jnp.float32
I32 = jnp.int32
RELS = (0, 1, 3, 2)


def dct_table_of(length_blocks):
    frequency = jnp.arange(length_blocks, dtype=jnp.float32)[:, None]
    position = jnp.arange(length_blocks, dtype=jnp.float32)[None, :]
    factor = jnp.where(frequency > 0, jnp.sqrt(2.0 / length_blocks), jnp.sqrt(1.0 / length_blocks))
    return (
        factor * jnp.cos(math.pi * (2.0 * position + 1.0) * frequency / (2.0 * length_blocks))
    ).astype(jnp.bfloat16)


def x_perm(shift):
    return [(y * 4 + x, y * 4 + (x + shift) % 4) for y in range(4) for x in range(4)]


def y_perm(shift):
    return [(y * 4 + x, (y + shift) % 4 * 4 + x) for y in range(4) for x in range(4)]


def ring(shift):
    return [(i, (i + shift) % GRP) for i in range(GRP)]


def pick4(index, values):
    out = values[3]
    for i in (2, 1, 0):
        out = jnp.where(index == i, values[i], out)
    return out


ANY = pl.BlockSpec(memory_space=pl.ANY)


def pack_kernel(place_ref, flags_ref, len_ref, off_ref, *refs):
    ins, outs = refs[:10], refs[10:16]
    y, x = place_ref[0], place_ref[1]
    low, high, tail = pl.ds(0, QUARTER), pl.ds(QUARTER, QUARTER), pl.ds(HALF, QUARTER)
    for path in range(2):
        src0, src_next, src_prev, src_lo, src_hi = ins[path * 5 : path * 5 + 5]
        out_own, out_next, out_prev = outs[path * 3 : path * 3 + 3]
        along, across = (x, y) if path == 0 else (y, x)
        for kd, shift in enumerate(RELS):
            there = lax.rem(across + shift, 4)
            dest = there * 4 + x if path == 0 else y * 4 + there
            counts, offsets, starts = [], [], []
            total = jnp.int32(0)
            for s in range(4):
                p = y * 4 + s if path == 0 else s * 4 + x
                n = flags_ref[path * 4 + kd, p] * len_ref[p, dest]
                counts.append(n)
                offsets.append(off_ref[p, dest])
                starts.append(total)
                total = total + n
            for ks, near in enumerate(RELS):
                s = lax.rem(along + near, 4)
                n, o, d = pick4(s, counts), pick4(s, offsets), pick4(s, starts)
                source = (src0, src_next, src_prev, None)[ks]

                def move(i, carry):
                    if ks < 3:
                        first, second = source[o + i, low], source[o + i, high]
                    else:
                        first, second = src_lo[o + i], src_hi[o + i]
                    if kd < 3:
                        out = (out_own, out_next, out_prev)[kd]
                        out[d + i, low] = first
                        out[d + i, high] = second
                    else:
                        out_next[d + i, tail] = first
                        out_prev[d + i, tail] = second
                    return carry

                lax.fori_loop(0, n, move, 0)


def pack(place, flags, len_of, off_of, arrays):
    own = jax.ShapeDtypeStruct((CAP, HALF, KV), BF)
    sent = jax.ShapeDtypeStruct((CAP, HALF + QUARTER, KV), BF)
    smem = pl.BlockSpec(memory_space=pltpu.SMEM)
    vmem = pl.BlockSpec(memory_space=pltpu.VMEM)
    return pl.pallas_call(
        pack_kernel,
        out_shape=[own, sent, sent] * 2,
        in_specs=[smem] * 4 + [vmem] * 10,
        out_specs=[vmem] * 6,
        compiler_params=pltpu.CompilerParams(vmem_limit_bytes=40 * 1024 * 1024),
        name="pack",
    )(place, flags, len_of, off_of, *arrays)


def column_of(row, width=128):
    return jnp.transpose(jnp.broadcast_to(row, (width, QS)))


def row_of(column):
    return jnp.transpose(jnp.broadcast_to(column, (QS, 128)))[:8]


def draft_scores(query, fresh):
    raw = (
        lax.dot_general(query, fresh, (((1,), (1,)), ((), ())), preferred_element_type=F32)
        * score_scale
    )
    step = lax.broadcasted_iota(I32, raw.shape, 0) // HEADS
    token = lax.broadcasted_iota(I32, raw.shape, 1)
    return jnp.where(token <= step, raw, -jnp.inf)


def token_live(shape, group, filled):
    token = lax.rem(lax.broadcasted_iota(I32, shape, 1), CHUNK)
    return token // BLK + group * GROUP < filled


def cache_scores(query, keys, group, filled, other):
    raw = (
        lax.dot_general(query, keys, (((1,), (1,)), ((), ())), preferred_element_type=F32)
        * score_scale
    )
    return jnp.where(token_live(raw.shape, group, filled), raw, other)


def fold(op, wide):
    return op(op(wide[:, :128], wide[:, 128:256]), op(wide[:, 256:384], wide[:, 384:]))


def keys_kernel(meta_ref, place_ref, filled_ref, table_ref, query_ref, fresh_ref, *refs):
    ins = refs[:20]
    keys_ref, top_ref, hold, best, sems = refs[20:]
    row = pl.program_id(0)
    y, x = place_ref[0], place_ref[1]

    def spots(n):
        p = meta_ref[n]
        sy, sx = p // 4, lax.rem(p, 4)
        found = []
        for path in range(2):
            line, inner = (sy, sx) if path == 0 else (sx, sy)
            start = jnp.int32(0)
            for s in range(3):
                other = sy * 4 + s if path == 0 else s * 4 + sx
                start = start + jnp.where(s < inner, filled_ref[other], 0)
            rel = lax.rem(line - (y if path == 0 else x) + 4, 4)
            first = jnp.minimum(start, CAP - MOST_M)
            found.append((rel, first, start - first))
        return found

    def each_copy(n, act):
        slot = lax.rem(n, 2)
        found = spots(n)
        for side in range(2):
            for path in range(2):
                own, nxt, prv, low, high = ins[(side * 2 + path) * 5 : (side * 2 + path) * 5 + 5]
                rel, first, _ = found[path]
                there = hold.at[slot, side, path, pl.ds(0, MOST_M)]
                block = pl.ds(first, MOST_M)
                for ref, shift in ((own, 0), (nxt, 1), (prv, 3)):
                    @pl.when(rel == shift)
                    def _():
                        act(
                            pltpu.make_async_copy(
                                ref.at[block, pl.ds(0, HALF)], there, sems.at[slot, side, path, 0]
                            )
                        )

                @pl.when(rel == 2)
                def _():
                    for part, ref in enumerate((low, high)):
                        act(
                            pltpu.make_async_copy(
                                ref.at[block],
                                there.at[:, pl.ds(part * QUARTER, QUARTER)],
                                sems.at[slot, side, path, part],
                            )
                        )

    @pl.when(row == 0)
    def _():
        each_copy(jnp.int32(0), lambda c: c.start())

    @pl.when(row + 1 < ROWS)
    def _():
        each_copy(row + 1, lambda c: c.start())

    each_copy(row, lambda c: c.wait())
    slot = lax.rem(row, 2)
    found = spots(row)
    filled = meta_ref[ROWS + row]
    query = query_ref[0]
    draft = draft_scores(query, fresh_ref[0])
    best[...] = jnp.broadcast_to(jnp.max(draft, axis=1, keepdims=True), (QS, 128))
    for group in range(2):
        @pl.when(group * GROUP < filled)
        def _():
            for side in range(2):
                parts = []
                for path in range(2):
                    at = found[path][2] + group * GROUP
                    parts.append(
                        hold[slot, side, path, pl.ds(at, GROUP)].reshape(GROUP * HALF, KV)
                    )
                packed = jnp.concatenate(parts, axis=0)
                block = lax.rem(lax.broadcasted_iota(I32, packed.shape, 0), GROUP * HALF) // HALF
                packed = jnp.where(block + group * GROUP < filled, packed, jnp.zeros_like(packed))
                keys_ref[0, group, side * CHUNK : side * CHUNK + CHUNK] = jnp.dot(
                    table_ref[...], packed, preferred_element_type=F32
                ).astype(BF)
            raw = cache_scores(query, keys_ref[0, group], group, filled, -jnp.inf)
            best[...] = jnp.maximum(best[...], fold(jnp.maximum, raw))
    top_ref[0] = row_of(jnp.max(best[...], axis=1, keepdims=True))[:1]


def keys_and_top(meta, place, filled, table, queries, fresh, arrays):
    row = lambda *tail: pl.BlockSpec((1,) + tail, lambda i, *_: (i,) + (0,) * len(tail))
    return pl.pallas_call(
        keys_kernel,
        out_shape=[
            jax.ShapeDtypeStruct((ROWS, 2, 2 * CHUNK, KV), BF),
            jax.ShapeDtypeStruct((ROWS, 1, QS), F32),
        ],
        grid_spec=pltpu.PrefetchScalarGridSpec(
            num_scalar_prefetch=3,
            grid=(ROWS,),
            in_specs=[
                pl.BlockSpec((CHUNK, CHUNK), lambda i, *_: (0, 0)),
                row(QS, KV),
                row(QUARTER, KV),
            ]
            + [ANY] * 20,
            out_specs=[row(2, 2 * CHUNK, KV), row(1, QS)],
            scratch_shapes=[
                pltpu.VMEM((2, 2, 2, 2 * MOST_M, HALF, KV), BF),
                pltpu.VMEM((QS, 128), F32),
                pltpu.SemaphoreType.DMA((2, 2, 2, 2)),
            ],
        ),
        compiler_params=pltpu.CompilerParams(vmem_limit_bytes=VMEM_LIMIT),
        name="keys",
    )(meta, place, filled, table, queries, fresh, *arrays)


def sums_kernel(last, meta_ref, order_ref, keys_ref, query_ref, fresh_ref, *refs):
    tops, out_ref, total = refs[:-2], refs[-2], refs[-1]
    step = pl.program_id(0)
    row = order_ref[step]
    filled = meta_ref[ROWS + row]
    query = query_ref[0]
    peak_row = tops[0][0]
    for top in tops[1:]:
        peak_row = jnp.maximum(peak_row, top[0])
    peak = column_of(peak_row)
    for group in range(2):
        def add():
            keys = keys_ref[0, group]
            raw = cache_scores(query, keys, group, filled, -jnp.inf)
            weights = jnp.exp(raw - jnp.concatenate([peak] * 4, axis=1))
            part = jnp.dot(weights.astype(BF), keys[:, :LAT], preferred_element_type=F32)
            if group == 0:
                total[...] = fold(jnp.add, weights)
                out_ref[0, :QS] = part
            else:
                total[...] += fold(jnp.add, weights)
                out_ref[0, :QS] += part

        if group == 0:
            add()
        else:
            pl.when(group * GROUP < filled)(add)

    if last:
        @pl.when(step == pl.num_programs(0) - 1)
        def _():
            fresh = fresh_ref[0]
            weights = jnp.exp(draft_scores(query, fresh) - peak[:, :QUARTER])
            out_ref[0, :QS] += jnp.dot(
                weights.astype(BF), fresh[:, :LAT], preferred_element_type=F32
            )
            lane = lax.broadcasted_iota(I32, (QS, 128), 1)
            extra = jnp.sum(weights, axis=1, keepdims=True)
            total[...] += jnp.where(lane == 0, extra, 0.0)

    out_ref[0, QS:, :QS] = row_of(jnp.sum(total[...], axis=1, keepdims=True))
    out_ref[0, QS:, QS:] = jnp.zeros((RED - QS, LAT - QS), F32)


def sums(places, grp, meta, keys, queries, fresh, tops):
    count = len(places)
    order = (grp + jnp.array(places, I32)) % ROWS
    row = lambda *tail: pl.BlockSpec((1,) + tail, lambda i, m, o: (o[i],) + (0,) * len(tail))
    return pl.pallas_call(
        functools.partial(sums_kernel, places[-1] == 0),
        out_shape=jax.ShapeDtypeStruct((count, RED, LAT), F32),
        grid_spec=pltpu.PrefetchScalarGridSpec(
            num_scalar_prefetch=2,
            grid=(count,),
            in_specs=[row(2, 2 * CHUNK, KV), row(QS, KV), row(QUARTER, KV)]
            + [row(1, QS)] * len(tops),
            out_specs=pl.BlockSpec((1, RED, LAT), lambda i, m, o: (i, 0, 0)),
            scratch_shapes=[pltpu.VMEM((QS, 128), F32)],
        ),
        compiler_params=pltpu.CompilerParams(vmem_limit_bytes=VMEM_LIMIT),
        name="sums",
    )(meta, order, keys, queries, fresh, *tops)


def finish_kernel(a_ref, b_ref, c_ref, out_ref):
    whole = a_ref[0] + (b_ref[...] + c_ref[...])
    total = jnp.transpose(jnp.broadcast_to(whole[QS : QS + 1, :QS], (128, QS)))
    total = jnp.concatenate([total] * 4, axis=1)
    out_ref[...] = (whole[:QS] / total).astype(BF)


def finish(own, left, right):
    vmem = pl.BlockSpec(memory_space=pltpu.VMEM)
    return pl.pallas_call(
        finish_kernel,
        out_shape=jax.ShapeDtypeStruct((QS, LAT), BF),
        in_specs=[vmem] * 3,
        out_specs=vmem,
        compiler_params=pltpu.CompilerParams(vmem_limit_bytes=24 * 1024 * 1024),
        name="finish",
    )(own, left, right)


def place_kernel(grp_ref, *refs):
    ins, out_ref = refs[:9], refs[9]
    step = pl.program_id(0)
    for d in range(8):
        @pl.when(step == d)
        def _():
            if d == 4:
                out_ref[0, : QS // 2] = ins[4][...]
                out_ref[0, QS // 2 :] = ins[8][...]
            else:
                out_ref[0] = ins[d][...]


def put_in_place(grp, pieces):
    return pl.pallas_call(
        place_kernel,
        out_shape=jax.ShapeDtypeStruct((ROWS, QS, LAT), BF),
        grid_spec=pltpu.PrefetchScalarGridSpec(
            num_scalar_prefetch=1,
            grid=(ROWS,),
            in_specs=[pl.BlockSpec(memory_space=pltpu.VMEM)] * 9,
            out_specs=pl.BlockSpec((1, QS, LAT), lambda i, g: (lax.rem(g[0] + i, GRP), 0, 0)),
        ),
        compiler_params=pltpu.CompilerParams(vmem_limit_bytes=16 * 1024 * 1024),
        name="place",
    )(grp, *pieces)


def body(coeffs, lengths, owners, row_pick, queries, new_latent):
    stored = coeffs[0, 0, 0]
    pair = lax.axis_index("pair").astype(I32)
    grp = lax.axis_index("grp").astype(I32)
    place = jnp.stack([pair // 4, pair % 4])

    owner = owners[:, 0]
    requests = jnp.arange(owner.shape[0], dtype=I32)
    mine = (owner == pair).astype(I32)
    before = jnp.sum(jnp.where(requests[None, :] < requests[:, None], mine[None, :], 0), axis=1)
    wanted = row_pick % jnp.sum(mine)
    hit = mine[None, :] * (before[None, :] == wanted[:, None]).astype(I32)
    request = jnp.sum(hit * requests[None, :], axis=1)
    flags = jnp.max(hit.reshape(ROWS, 16, 4), axis=(0, 2))

    flag_block = jnp.zeros((1, HALF, KV), BF).at[0, :, :16].set(flags.astype(BF)[None, :])
    a0 = jnp.concatenate([stored[:, :HALF], flag_block], axis=0)
    b0 = jnp.concatenate([stored[:, HALF:], flag_block], axis=0)

    send = lambda v, perm: lax.ppermute(v, "pair", perm)
    a_prev, a_next = send(a0, x_perm(1)), send(a0, x_perm(-1))
    b_prev, b_next = send(b0, y_perm(1)), send(b0, y_perm(-1))
    a_lo, a_hi = send(a_prev[:, :QUARTER], x_perm(1)), send(a_next[:, QUARTER:], x_perm(-1))
    b_lo, b_hi = send(b_prev[:, :QUARTER], y_perm(1)), send(b_next[:, QUARTER:], y_perm(-1))

    named = owner.reshape(16, 4)[:, :, None] == jnp.arange(16, dtype=I32)[None, None, :]
    earlier = jnp.arange(4)[None, :] < jnp.arange(4)[:, None]
    offsets = jnp.sum(jnp.where(earlier[None], lengths[:, None, :], 0), axis=2)
    len_of = jnp.sum(jnp.where(named, lengths[:, :, None], 0), axis=1)
    off_of = jnp.sum(jnp.where(named, offsets[:, :, None], 0), axis=1)
    filled = flags * jnp.sum(
        jnp.where(owner.reshape(16, 4) == pair, lengths, 0), axis=1
    )
    request_len = jnp.sum(
        jnp.where(request[:, None] == requests[None, :], lengths.reshape(1, -1), 0), axis=1
    )
    meta = jnp.concatenate([request // 4, request_len])

    heard = lambda v: v[FLAG, 0, :16]
    all_flags = jnp.stack(
        [heard(v) for v in (b0, b_next, b_prev, b_hi, a0, a_next, a_prev, a_hi)]
    ).astype(I32)
    o_a, n_a, p_a, o_b, n_b, p_b = pack(
        place,
        all_flags,
        len_of,
        off_of,
        (a0, a_next, a_prev, a_lo, a_hi, b0, b_next, b_prev, b_lo, b_hi),
    )

    across = lambda v: lax.ppermute(v, "side", [(0, 1), (1, 0)])
    ra_prev, ra_next = send(n_a, y_perm(1)), send(p_a, y_perm(-1))
    rb_prev, rb_next = send(n_b, x_perm(1)), send(p_b, x_perm(-1))
    ra_lo = send(ra_prev[:, HALF:], y_perm(1))
    ra_hi = send(ra_next[:, HALF:], y_perm(-1))
    rb_lo = send(rb_prev[:, HALF:], x_perm(1))
    rb_hi = send(rb_next[:, HALF:], x_perm(-1))
    here = (o_a, ra_next, ra_prev, ra_lo, ra_hi, o_b, rb_next, rb_prev, rb_lo, rb_hi)
    there = tuple(across(v) for v in here)

    table = dct_table_of(BLK)
    same = jnp.eye(GROUP, dtype=BF)
    spread = jnp.einsum("bc,hft->bthcf", same, table.reshape(2, HALF, BLK)).reshape(CHUNK, CHUNK)
    flat_queries = queries.reshape(ROWS, QS, KV)
    fresh = jnp.concatenate(
        [new_latent, jnp.zeros((ROWS, QUARTER - STEPS, KV), BF)], axis=1
    )
    keys, top = keys_and_top(meta, place, filled, spread, flat_queries, fresh, here + there)

    turn = lambda v, shift: lax.ppermute(v, "grp", ring(shift))
    near = jnp.maximum(top, jnp.maximum(turn(top, 1), turn(top, -1)))
    tops = (near, turn(near, 3), turn(near, -3))

    part = lambda *places: sums(places, grp, meta, keys, flat_queries, fresh, tops)
    far = part(4)
    third = part(3, 5)
    second = part(2, 6)
    first = part(1, 7, 0)

    cut = QS // 2
    up, down = turn(far[0, :cut], 1), turn(far[0, cut:], -1)
    up = turn(jnp.concatenate([third[0, :cut] + up, third[0, cut:]]), 1)
    down = turn(jnp.concatenate([third[1, :cut], third[1, cut:] + down]), -1)
    up, down = turn(second[0] + up, 1), turn(second[1] + down, -1)
    up, down = turn(first[0] + up, 1), turn(first[1] + down, -1)
    mine_out = finish(first[2:3], up, down)

    got = [None] * 9
    got[0] = mine_out
    for d in (1, 2, 3):
        got[8 - d] = turn(got[(9 - d) % 8], 1)
        got[d] = turn(got[d - 1], -1)
    low, high = turn(got[5][:cut], 1), turn(got[3][cut:], -1)
    got[4], got[8] = low, high
    out = put_in_place(grp[None], got)
    return out.reshape(ROWS, STEPS, HEADS, LAT)


def solution(mesh):
    return jax.shard_map(
        body,
        mesh=mesh,
        in_specs=(
            P("pair", "side", "grp", None, None, None),
            P(),
            P(),
            P("pair"),
            P("pair", None, "side", None),
            P("pair", None, None),
        ),
        out_specs=P("pair", None, "side", None),
        check_vma=False,
    )
```

```python
import functools
import math

import jax
import jax.numpy as jnp
import numpy as np
from jax import lax
from jax.experimental import pallas as pl
from jax.experimental.pallas import tpu as pltpu
from jax.sharding import PartitionSpec as P

LAT = 512
KV = 576
BLK = 64
HALF = 32
QUARTER = 16
STEPS = 4
MOST_M = 8
STORE = 20
ROWS = 8
HEADS = 64
QS = STEPS * HEADS
SIDE_LEN = 4
CAP = SIDE_LEN * MOST_M
GRP = 8
GROUP = 4
CHUNK = GROUP * BLK
VMEM_LIMIT = 56 * 1024 * 1024
RED = QS + 8
FLAG = STORE

score_scale = 192.0 ** (-0.5)
BF = jnp.bfloat16
F32 = jnp.float32
I32 = jnp.int32
RELS = (0, 1, 3, 2)


def spread_table():
    frequency = np.arange(BLK, dtype=np.float64)[:, None]
    position = np.arange(BLK, dtype=np.float64)[None, :]
    factor = np.sqrt(np.where(frequency > 0, 2.0, 1.0) / BLK)
    table = factor * np.cos(math.pi * (2.0 * position + 1.0) * frequency / (2.0 * BLK))
    table = table.reshape(2, HALF, BLK)
    spread = np.einsum("bc,hft->bthcf", np.eye(GROUP), table).reshape(CHUNK, CHUNK)
    return jnp.asarray(spread, BF)


def x_perm(shift):
    return [(y * 4 + x, y * 4 + (x + shift) % 4) for y in range(4) for x in range(4)]


def y_perm(shift):
    return [(y * 4 + x, (y + shift) % 4 * 4 + x) for y in range(4) for x in range(4)]


def ring(shift):
    return [(i, (i + shift) % GRP) for i in range(GRP)]


def pick4(index, values):
    out = values[3]
    for i in (2, 1, 0):
        out = jnp.where(index == i, values[i], out)
    return out


ANY = pl.BlockSpec(memory_space=pl.ANY)


def pack_kernel(place_ref, flags_ref, len_ref, off_ref, *refs):
    ins, outs = refs[:16], refs[16:26]
    y, x = place_ref[0], place_ref[1]
    low, high = pl.ds(0, QUARTER), pl.ds(QUARTER, QUARTER)
    for path in range(2):
        sources = ins[path * 8 : path * 8 + 8]
        out_own, out_next, out_prev, out_lo, out_hi = outs[path * 5 : path * 5 + 5]
        along, across = (x, y) if path == 0 else (y, x)
        for kd, shift in enumerate(RELS):
            there = lax.rem(across + shift, 4)
            dest = there * 4 + x if path == 0 else y * 4 + there
            counts, offsets, starts = [], [], []
            total = jnp.int32(0)
            for s in range(4):
                p = y * 4 + s if path == 0 else s * 4 + x
                n = flags_ref[path * 4 + kd, p] * len_ref[p, dest]
                counts.append(n)
                offsets.append(off_ref[p, dest])
                starts.append(total)
                total = total + n
            for ks, near in enumerate(RELS):
                s = lax.rem(along + near, 4)
                n, o, d = pick4(s, counts), pick4(s, offsets), pick4(s, starts)
                source_lo, source_hi = sources[2 * ks : 2 * ks + 2]

                def move(i, carry):
                    if kd < 3:
                        out = (out_own, out_next, out_prev)[kd]
                        out[d + i, low] = source_lo[o + i]
                        out[d + i, high] = source_hi[o + i]
                    else:
                        out_lo[d + i] = source_lo[o + i]
                        out_hi[d + i] = source_hi[o + i]
                    return carry

                lax.fori_loop(0, n, move, 0)


def pack(place, flags, len_of, off_of, arrays):
    half = jax.ShapeDtypeStruct((CAP, HALF, KV), BF)
    quarter = jax.ShapeDtypeStruct((CAP, QUARTER, KV), BF)
    smem = pl.BlockSpec(memory_space=pltpu.SMEM)
    vmem = pl.BlockSpec(memory_space=pltpu.VMEM)
    return pl.pallas_call(
        pack_kernel,
        out_shape=[half, half, half, quarter, quarter] * 2,
        in_specs=[smem] * 4 + [vmem] * 16,
        out_specs=[vmem] * 10,
        compiler_params=pltpu.CompilerParams(vmem_limit_bytes=40 * 1024 * 1024),
        name="pack",
    )(place, flags, len_of, off_of, *arrays)


def column_of(row, width=128):
    return jnp.transpose(jnp.broadcast_to(row, (width, QS)))


def row_of(column):
    return jnp.transpose(jnp.broadcast_to(column, (QS, 128)))[:8]


def draft_scores(query, fresh):
    raw = (
        lax.dot_general(query, fresh, (((1,), (1,)), ((), ())), preferred_element_type=F32)
        * score_scale
    )
    step = lax.broadcasted_iota(I32, raw.shape, 0) // HEADS
    token = lax.broadcasted_iota(I32, raw.shape, 1)
    return jnp.where(token <= step, raw, -jnp.inf)


def token_live(shape, group, filled):
    token = lax.rem(lax.broadcasted_iota(I32, shape, 1), CHUNK)
    return token // BLK + group * GROUP < filled


def cache_scores(query, keys, group, filled, other):
    raw = (
        lax.dot_general(query, keys, (((1,), (1,)), ((), ())), preferred_element_type=F32)
        * score_scale
    )
    return jnp.where(token_live(raw.shape, group, filled), raw, other)


def fold(op, wide):
    return op(op(wide[:, :128], wide[:, 128:256]), op(wide[:, 256:384], wide[:, 384:]))


def keys_kernel(meta_ref, place_ref, filled_ref, table_ref, query_ref, fresh_ref, *refs):
    ins = refs[:20]
    keys_ref, top_ref, hold, best, sems = refs[20:]
    row = pl.program_id(0)
    y, x = place_ref[0], place_ref[1]

    def spots(n):
        p = meta_ref[n]
        sy, sx = p // 4, lax.rem(p, 4)
        found = []
        for path in range(2):
            line, inner = (sy, sx) if path == 0 else (sx, sy)
            start = jnp.int32(0)
            for s in range(3):
                other = sy * 4 + s if path == 0 else s * 4 + sx
                start = start + jnp.where(s < inner, filled_ref[other], 0)
            rel = lax.rem(line - (y if path == 0 else x) + 4, 4)
            first = jnp.minimum(start, CAP - MOST_M)
            found.append((rel, first, start - first))
        return found

    def each_copy(n, act):
        slot = lax.rem(n, 2)
        found = spots(n)
        for side in range(2):
            for path in range(2):
                own, nxt, prv, low, high = ins[(side * 2 + path) * 5 : (side * 2 + path) * 5 + 5]
                rel, first, _ = found[path]
                there = hold.at[slot, side, path, pl.ds(0, MOST_M)]
                block = pl.ds(first, MOST_M)
                for ref, shift in ((own, 0), (nxt, 1), (prv, 3)):
                    @pl.when(rel == shift)
                    def _():
                        act(
                            pltpu.make_async_copy(
                                ref.at[block], there, sems.at[slot, side, path, 0]
                            )
                        )

                @pl.when(rel == 2)
                def _():
                    for part, ref in enumerate((low, high)):
                        act(
                            pltpu.make_async_copy(
                                ref.at[block],
                                there.at[:, pl.ds(part * QUARTER, QUARTER)],
                                sems.at[slot, side, path, part],
                            )
                        )

    @pl.when(row == 0)
    def _():
        each_copy(jnp.int32(0), lambda c: c.start())

    @pl.when(row + 1 < ROWS)
    def _():
        each_copy(row + 1, lambda c: c.start())

    each_copy(row, lambda c: c.wait())
    slot = lax.rem(row, 2)
    found = spots(row)
    filled = meta_ref[ROWS + row]
    query = query_ref[0]
    draft = draft_scores(query, fresh_ref[0])
    best[...] = jnp.broadcast_to(jnp.max(draft, axis=1, keepdims=True), (QS, 128))
    for group in range(2):
        @pl.when(group * GROUP < filled)
        def _():
            for side in range(2):
                parts = []
                for path in range(2):
                    at = found[path][2] + group * GROUP
                    parts.append(
                        hold[slot, side, path, pl.ds(at, GROUP)].reshape(GROUP * HALF, KV)
                    )
                packed = jnp.concatenate(parts, axis=0)
                block = lax.rem(lax.broadcasted_iota(I32, packed.shape, 0), GROUP * HALF) // HALF
                packed = jnp.where(block + group * GROUP < filled, packed, jnp.zeros_like(packed))
                keys_ref[0, group, side * CHUNK : side * CHUNK + CHUNK] = jnp.dot(
                    table_ref[...], packed, preferred_element_type=F32
                ).astype(BF)
            raw = cache_scores(query, keys_ref[0, group], group, filled, -jnp.inf)
            best[...] = jnp.maximum(best[...], fold(jnp.maximum, raw))
    top_ref[0] = row_of(jnp.max(best[...], axis=1, keepdims=True))[:1]


def keys_and_top(meta, place, filled, table, queries, fresh, arrays):
    row = lambda *tail: pl.BlockSpec((1,) + tail, lambda i, *_: (i,) + (0,) * len(tail))
    return pl.pallas_call(
        keys_kernel,
        out_shape=[
            jax.ShapeDtypeStruct((ROWS, 2, 2 * CHUNK, KV), BF),
            jax.ShapeDtypeStruct((ROWS, 1, QS), F32),
        ],
        grid_spec=pltpu.PrefetchScalarGridSpec(
            num_scalar_prefetch=3,
            grid=(ROWS,),
            in_specs=[
                pl.BlockSpec((CHUNK, CHUNK), lambda i, *_: (0, 0)),
                row(QS, KV),
                row(QUARTER, KV),
            ]
            + [ANY] * 20,
            out_specs=[row(2, 2 * CHUNK, KV), row(1, QS)],
            scratch_shapes=[
                pltpu.VMEM((2, 2, 2, 2 * MOST_M, HALF, KV), BF),
                pltpu.VMEM((QS, 128), F32),
                pltpu.SemaphoreType.DMA((2, 2, 2, 2)),
            ],
        ),
        compiler_params=pltpu.CompilerParams(vmem_limit_bytes=VMEM_LIMIT),
        name="keys",
    )(meta, place, filled, table, queries, fresh, *arrays)


def sums_kernel(places, meta_ref, order_ref, keys_ref, query_ref, fresh_ref, *refs):
    tops, outs, acc, total = refs[:3], refs[3:-2], refs[-2], refs[-1]
    step = pl.program_id(0)
    row = order_ref[step]
    filled = meta_ref[ROWS + row]
    query = query_ref[0]
    peak_row = tops[0][0]
    for top in tops[1:]:
        peak_row = jnp.maximum(peak_row, top[0])
    peak = column_of(peak_row)
    for group in range(2):
        def add():
            keys = keys_ref[0, group]
            raw = cache_scores(query, keys, group, filled, -jnp.inf)
            weights = jnp.exp(raw - jnp.concatenate([peak] * 4, axis=1))
            part = jnp.dot(weights.astype(BF), keys[:, :LAT], preferred_element_type=F32)
            if group == 0:
                total[...] = fold(jnp.add, weights)
                acc[...] = part
            else:
                total[...] += fold(jnp.add, weights)
                acc[...] += part

        if group == 0:
            add()
        else:
            pl.when(group * GROUP < filled)(add)

    if places[-1] == 0:
        @pl.when(step == len(places) - 1)
        def _():
            fresh = fresh_ref[0]
            weights = jnp.exp(draft_scores(query, fresh) - peak[:, :QUARTER])
            acc[...] += jnp.dot(weights.astype(BF), fresh[:, :LAT], preferred_element_type=F32)
            lane = lax.broadcasted_iota(I32, (QS, 128), 1)
            extra = jnp.sum(weights, axis=1, keepdims=True)
            total[...] += jnp.where(lane == 0, extra, 0.0)

    shares = row_of(jnp.sum(total[...], axis=1, keepdims=True))
    for i in range(len(places)):
        @pl.when(step == i)
        def _():
            outs[i][:QS] = acc[...]
            outs[i][QS:, :QS] = shares
            outs[i][QS:, QS:] = jnp.zeros((RED - QS, LAT - QS), F32)


def sums(places, grp, meta, keys, queries, fresh, tops):
    count = len(places)
    order = (grp + jnp.array(places, I32)) % ROWS
    row = lambda *tail: pl.BlockSpec((1,) + tail, lambda i, m, o: (o[i],) + (0,) * len(tail))
    return pl.pallas_call(
        functools.partial(sums_kernel, places),
        out_shape=[jax.ShapeDtypeStruct((RED, LAT), F32)] * count,
        grid_spec=pltpu.PrefetchScalarGridSpec(
            num_scalar_prefetch=2,
            grid=(count,),
            in_specs=[row(2, 2 * CHUNK, KV), row(QS, KV), row(QUARTER, KV)]
            + [row(1, QS)] * len(tops),
            out_specs=[pl.BlockSpec((RED, LAT), lambda i, m, o: (0, 0))] * count,
            scratch_shapes=[pltpu.VMEM((QS, LAT), F32), pltpu.VMEM((QS, 128), F32)],
        ),
        compiler_params=pltpu.CompilerParams(vmem_limit_bytes=VMEM_LIMIT),
        name="sums",
    )(meta, order, keys, queries, fresh, *tops)


def finish_kernel(a_ref, b_ref, c_ref, top_ref, bottom_ref):
    whole = a_ref[...] + (b_ref[...] + c_ref[...])
    total = jnp.transpose(jnp.broadcast_to(whole[QS : QS + 1, :QS], (128, QS)))
    total = jnp.concatenate([total] * 4, axis=1)
    out = (whole[:QS] / total).astype(BF)
    top_ref[...] = out[: QS // 2]
    bottom_ref[...] = out[QS // 2 :]


def finish(own, left, right):
    vmem = pl.BlockSpec(memory_space=pltpu.VMEM)
    return pl.pallas_call(
        finish_kernel,
        out_shape=[jax.ShapeDtypeStruct((QS // 2, LAT), BF)] * 2,
        in_specs=[vmem] * 3,
        out_specs=[vmem] * 2,
        compiler_params=pltpu.CompilerParams(vmem_limit_bytes=24 * 1024 * 1024),
        name="finish",
    )(own, left, right)


def place_kernel(grp_ref, *refs):
    ins, out_ref = refs[:16], refs[16]
    step = pl.program_id(0)
    for d in range(8):
        @pl.when(step == d)
        def _():
            out_ref[0, : QS // 2] = ins[2 * d][...]
            out_ref[0, QS // 2 :] = ins[2 * d + 1][...]


def put_in_place(grp, pieces):
    return pl.pallas_call(
        place_kernel,
        out_shape=jax.ShapeDtypeStruct((ROWS, QS, LAT), BF),
        grid_spec=pltpu.PrefetchScalarGridSpec(
            num_scalar_prefetch=1,
            grid=(ROWS,),
            in_specs=[pl.BlockSpec(memory_space=pltpu.VMEM)] * 16,
            out_specs=pl.BlockSpec((1, QS, LAT), lambda i, g: (lax.rem(g[0] + i, GRP), 0, 0)),
        ),
        compiler_params=pltpu.CompilerParams(vmem_limit_bytes=16 * 1024 * 1024),
        name="place",
    )(grp, *pieces)


def body(coeffs, lengths, owners, row_pick, queries, new_latent):
    stored = coeffs[0, 0, 0]
    pair = lax.axis_index("pair").astype(I32)
    grp = lax.axis_index("grp").astype(I32)
    place = jnp.stack([pair // 4, pair % 4])

    owner = owners[:, 0]
    requests = jnp.arange(owner.shape[0], dtype=I32)
    mine = (owner == pair).astype(I32)
    before = jnp.sum(jnp.where(requests[None, :] < requests[:, None], mine[None, :], 0), axis=1)
    wanted = row_pick % jnp.sum(mine)
    hit = mine[None, :] * (before[None, :] == wanted[:, None]).astype(I32)
    request = jnp.sum(hit * requests[None, :], axis=1)
    flags = jnp.max(hit.reshape(ROWS, 16, 4), axis=(0, 2))

    flag_block = jnp.zeros((1, QUARTER, KV), BF).at[0, :, :16].set(flags.astype(BF)[None, :])
    quarter = lambda i: stored[:, i * QUARTER : (i + 1) * QUARTER]
    flagged = lambda v: jnp.concatenate([v, flag_block], axis=0)
    a_lo, a_hi = flagged(quarter(0)), quarter(1)
    b_lo, b_hi = flagged(quarter(2)), quarter(3)

    send = lambda v, perm: lax.ppermute(v, "pair", perm)

    def gather_line(lo, hi, perm):
        from_prev = send(lo, perm(1)), send(hi, perm(1))
        from_next = send(lo, perm(-1)), send(hi, perm(-1))
        return (lo, hi) + from_next + from_prev, from_prev[0], from_next[1]

    line_a, a_prev_lo, a_next_hi = gather_line(a_lo, a_hi, x_perm)
    line_b, b_prev_lo, b_next_hi = gather_line(b_lo, b_hi, y_perm)

    named = owner.reshape(16, 4)[:, :, None] == jnp.arange(16, dtype=I32)[None, None, :]
    earlier = jnp.arange(4)[None, :] < jnp.arange(4)[:, None]
    offsets = jnp.sum(jnp.where(earlier[None], lengths[:, None, :], 0), axis=2)
    len_of = jnp.sum(jnp.where(named, lengths[:, :, None], 0), axis=1)
    off_of = jnp.sum(jnp.where(named, offsets[:, :, None], 0), axis=1)
    filled = flags * jnp.sum(
        jnp.where(owner.reshape(16, 4) == pair, lengths, 0), axis=1
    )
    request_len = jnp.sum(
        jnp.where(request[:, None] == requests[None, :], lengths.reshape(1, -1), 0), axis=1
    )
    meta = jnp.concatenate([request // 4, request_len])
    fresh = jnp.concatenate([new_latent, jnp.zeros((ROWS, QUARTER - STEPS, KV), BF)], axis=1)
    table = spread_table()

    a_prev_lo, b_prev_lo, place, len_of, off_of, filled, meta, fresh, table = (
        lax.optimization_barrier(
            (a_prev_lo, b_prev_lo, place, len_of, off_of, filled, meta, fresh, table)
        )
    )
    line_a = line_a + (send(a_prev_lo, x_perm(1)), send(a_next_hi, x_perm(-1)))
    line_b = line_b + (send(b_prev_lo, y_perm(1)), send(b_next_hi, y_perm(-1)))

    heard = lambda v: v[FLAG, 0, :16]
    all_flags = jnp.stack([heard(v) for v in line_b[::2] + line_a[::2]]).astype(I32)
    o_a, n_a, p_a, l_a, h_a, o_b, n_b, p_b, l_b, h_b = pack(
        place, all_flags, len_of, off_of, line_a + line_b
    )

    across = lambda v: lax.ppermute(v, "side", [(0, 1), (1, 0)])

    def second_hop(own, nxt, prv, lo, hi, perm):
        lo, hi = send(lo, perm(1)), send(hi, perm(-1))
        prv, nxt = send(nxt, perm(1)), send(prv, perm(-1))
        return own, nxt, prv, send(lo, perm(1)), send(hi, perm(-1))

    here = second_hop(o_a, n_a, p_a, l_a, h_a, y_perm) + second_hop(
        o_b, n_b, p_b, l_b, h_b, x_perm
    )
    there = tuple(across(v) for v in here)

    flat_queries = queries.reshape(ROWS, QS, KV)
    keys, top = keys_and_top(meta, place, filled, table, flat_queries, fresh, here + there)

    turn = lambda v, shift: lax.ppermute(v, "grp", ring(shift))
    near = jnp.maximum(top, jnp.maximum(turn(top, 1), turn(top, -1)))
    tops = (near, turn(near, 3), turn(near, -3))

    part = lambda *places: sums(places, grp, meta, keys, flat_queries, fresh, tops)
    (far,) = part(4)
    up3, down3 = part(3, 5)
    up2, down2 = part(2, 6)
    up1, down1, own = part(1, 7, 0)

    cut = QS // 2
    up, down = turn(far[:cut], 1), turn(far[cut:], -1)
    up = turn(jnp.concatenate([up3[:cut] + up, up3[cut:]]), 1)
    down = turn(jnp.concatenate([down3[:cut], down3[cut:] + down]), -1)
    up, down = turn(up2 + up, 1), turn(down2 + down, -1)
    up, down = turn(up1 + up, 1), turn(down1 + down, -1)
    top_half, bottom_half = finish(own, up, down)

    got = [[top_half, bottom_half]] + [[None, None] for _ in range(7)]
    for d in (1, 2, 3):
        for h in range(2):
            got[8 - d][h] = turn(got[(9 - d) % 8][h], 1)
            got[d][h] = turn(got[d - 1][h], -1)
    got[4] = [turn(got[5][0], 1), turn(got[3][1], -1)]
    out = put_in_place(grp[None], [half for pieces in got for half in pieces])
    return out.reshape(ROWS, STEPS, HEADS, LAT)


def solution(mesh):
    return jax.shard_map(
        body,
        mesh=mesh,
        in_specs=(
            P("pair", "side", "grp", None, None, None),
            P(),
            P(),
            P("pair"),
            P("pair", None, "side", None),
            P("pair", None, None),
        ),
        out_specs=P("pair", None, "side", None),
        check_vma=False,
    )
```

```python
import functools
import math

import jax
import jax.numpy as jnp
import numpy as np
from jax import lax
from jax.experimental import pallas as pl
from jax.experimental.pallas import tpu as pltpu
from jax.sharding import PartitionSpec as P

LAT = 512
KV = 576
BLK = 64
HALF = 32
QUARTER = 16
STEPS = 4
MOST_M = 8
STORE = 20
ROWS = 8
HEADS = 64
QS = STEPS * HEADS
SIDE_LEN = 4
MOST_CAP = SIDE_LEN * MOST_M
USUAL_CAP = 24
GRP = 8
GROUP = 4
CHUNK = GROUP * BLK
VMEM_LIMIT = 56 * 1024 * 1024
RED = QS + 8
FLAG = STORE

score_scale = 192.0 ** (-0.5)
BF = jnp.bfloat16
F32 = jnp.float32
I32 = jnp.int32
RELS = (0, 1, 3, 2)


def spread_table():
    frequency = np.arange(BLK, dtype=np.float64)[:, None]
    position = np.arange(BLK, dtype=np.float64)[None, :]
    factor = np.sqrt(np.where(frequency > 0, 2.0, 1.0) / BLK)
    table = factor * np.cos(math.pi * (2.0 * position + 1.0) * frequency / (2.0 * BLK))
    table = table.reshape(2, HALF, BLK)
    spread = np.einsum("bc,hft->bthcf", np.eye(GROUP), table).reshape(CHUNK, CHUNK)
    return jnp.asarray(spread, BF)


def x_perm(shift):
    return [(y * 4 + x, y * 4 + (x + shift) % 4) for y in range(4) for x in range(4)]


def y_perm(shift):
    return [(y * 4 + x, (y + shift) % 4 * 4 + x) for y in range(4) for x in range(4)]


def ring(shift):
    return [(i, (i + shift) % GRP) for i in range(GRP)]


def pick4(index, values):
    out = values[3]
    for i in (2, 1, 0):
        out = jnp.where(index == i, values[i], out)
    return out


ANY = pl.BlockSpec(memory_space=pl.ANY)


def pack_kernel(cap, place_ref, flags_ref, len_ref, off_ref, over_ref, *refs):
    ins, outs = refs[:16], refs[16:22]
    y, x = place_ref[0], place_ref[1]
    low, high, tail = pl.ds(0, QUARTER), pl.ds(QUARTER, QUARTER), pl.ds(HALF, QUARTER)
    for path in range(2):
        sources = ins[path * 8 : path * 8 + 8]
        out_own, out_next, out_prev = outs[path * 3 : path * 3 + 3]
        for out in (out_next, out_prev):
            out[cap, low] = over_ref[...]
            out[cap, tail] = over_ref[...]
        along, across = (x, y) if path == 0 else (y, x)
        for kd, shift in enumerate(RELS):
            there = lax.rem(across + shift, 4)
            dest = there * 4 + x if path == 0 else y * 4 + there
            counts, offsets, starts = [], [], []
            total = jnp.int32(0)
            for s in range(4):
                p = y * 4 + s if path == 0 else s * 4 + x
                n = flags_ref[path * 4 + kd, p] * len_ref[p, dest]
                counts.append(n)
                offsets.append(off_ref[p, dest])
                starts.append(total)
                total = total + n
            for ks, near in enumerate(RELS):
                s = lax.rem(along + near, 4)
                n, o, d = pick4(s, counts), pick4(s, offsets), pick4(s, starts)
                source_lo, source_hi = sources[2 * ks : 2 * ks + 2]

                def move(i, carry):
                    if kd < 3:
                        out = (out_own, out_next, out_prev)[kd]
                        out[d + i, low] = source_lo[o + i]
                        out[d + i, high] = source_hi[o + i]
                    else:
                        out_next[d + i, tail] = source_lo[o + i]
                        out_prev[d + i, tail] = source_hi[o + i]
                    return carry

                lax.fori_loop(0, jnp.minimum(n, jnp.maximum(cap - d, 0)), move, 0)


def pack(cap, place, flags, len_of, off_of, over, arrays):
    own = jax.ShapeDtypeStruct((cap, HALF, KV), BF)
    sent = jax.ShapeDtypeStruct((cap + 1, HALF + QUARTER, KV), BF)
    smem = pl.BlockSpec(memory_space=pltpu.SMEM)
    vmem = pl.BlockSpec(memory_space=pltpu.VMEM)
    return pl.pallas_call(
        functools.partial(pack_kernel, cap),
        out_shape=[own, sent, sent] * 2,
        in_specs=[smem] * 4 + [vmem] * 17,
        out_specs=[vmem] * 6,
        compiler_params=pltpu.CompilerParams(vmem_limit_bytes=40 * 1024 * 1024),
        name="pack",
    )(place, flags, len_of, off_of, over, *arrays)


def column_of(row, width=128):
    return jnp.transpose(jnp.broadcast_to(row, (width, QS)))


def row_of(column):
    return jnp.transpose(jnp.broadcast_to(column, (QS, 128)))[:8]


def draft_scores(query, fresh):
    raw = (
        lax.dot_general(query, fresh, (((1,), (1,)), ((), ())), preferred_element_type=F32)
        * score_scale
    )
    step = lax.broadcasted_iota(I32, raw.shape, 0) // HEADS
    token = lax.broadcasted_iota(I32, raw.shape, 1)
    return jnp.where(token <= step, raw, -jnp.inf)


def bias_row(group, filled):
    token = lax.rem(lax.broadcasted_iota(I32, (1, 2 * CHUNK), 1), CHUNK)
    return jnp.where(token // BLK + group * GROUP < filled, 0.0, -jnp.inf)


def products(query, keys):
    return lax.dot_general(query, keys, (((1,), (1,)), ((), ())), preferred_element_type=F32)


def fold(op, wide):
    return op(op(wide[:, :128], wide[:, 128:256]), op(wide[:, 256:384], wide[:, 384:]))


def keys_kernel(cap, meta_ref, place_ref, filled_ref, table_ref, query_ref, fresh_ref, *refs):
    ins = refs[:20]
    keys_ref, top_ref, hold, best, sems = refs[20:]
    row = pl.program_id(0)
    y, x = place_ref[0], place_ref[1]

    def spots(n):
        p = meta_ref[n]
        sy, sx = p // 4, lax.rem(p, 4)
        found = []
        for path in range(2):
            line, inner = (sy, sx) if path == 0 else (sx, sy)
            start = jnp.int32(0)
            for s in range(3):
                other = sy * 4 + s if path == 0 else s * 4 + sx
                start = start + jnp.where(s < inner, filled_ref[other], 0)
            rel = lax.rem(line - (y if path == 0 else x) + 4, 4)
            first = jnp.minimum(start, cap - MOST_M)
            found.append((rel, first, start - first))
        return found

    def each_copy(n, act):
        slot = lax.rem(n, 2)
        found = spots(n)
        for side in range(2):
            for path in range(2):
                own, nxt, prv, low, high = ins[(side * 2 + path) * 5 : (side * 2 + path) * 5 + 5]
                rel, first, _ = found[path]
                there = hold.at[slot, side, path, pl.ds(0, MOST_M)]
                block = pl.ds(first, MOST_M)
                for ref, shift in ((own, 0), (nxt, 1), (prv, 3)):
                    @pl.when(rel == shift)
                    def _():
                        act(
                            pltpu.make_async_copy(
                                ref.at[block, pl.ds(0, HALF)], there, sems.at[slot, side, path, 0]
                            )
                        )

                @pl.when(rel == 2)
                def _():
                    for part, ref in enumerate((low, high)):
                        act(
                            pltpu.make_async_copy(
                                ref.at[block],
                                there.at[:, pl.ds(part * QUARTER, QUARTER)],
                                sems.at[slot, side, path, part],
                            )
                        )

    @pl.when(row == 0)
    def _():
        each_copy(jnp.int32(0), lambda c: c.start())

    @pl.when(row + 1 < ROWS)
    def _():
        each_copy(row + 1, lambda c: c.start())

    each_copy(row, lambda c: c.wait())
    slot = lax.rem(row, 2)
    found = spots(row)
    filled = meta_ref[ROWS + row]
    query = query_ref[0]
    draft = draft_scores(query, fresh_ref[0])
    best[...] = jnp.full((QS, 128), -jnp.inf, F32)
    for group in range(2):
        @pl.when(group * GROUP < filled)
        def _():
            for side in range(2):
                parts = []
                for path in range(2):
                    at = found[path][2] + group * GROUP
                    for i in range(GROUP):
                        block = hold[slot, side, path, at + i]
                        live = i + group * GROUP < filled
                        parts.append(jnp.where(live, block, jnp.zeros_like(block)))
                packed = jnp.concatenate(parts, axis=0)
                keys_ref[0, group, side * CHUNK : side * CHUNK + CHUNK] = jnp.dot(
                    table_ref[...], packed, preferred_element_type=F32
                ).astype(BF)
            raw = products(query, keys_ref[0, group]) + bias_row(group, filled)
            best[...] = jnp.maximum(best[...], fold(jnp.maximum, raw))
    cached = jnp.max(best[...], axis=1, keepdims=True) * score_scale
    top_ref[0] = row_of(jnp.maximum(cached, jnp.max(draft, axis=1, keepdims=True)))[:1]


def keys_and_top(cap, meta, place, filled, table, queries, fresh, arrays):
    row = lambda *tail: pl.BlockSpec((1,) + tail, lambda i, *_: (i,) + (0,) * len(tail))
    return pl.pallas_call(
        functools.partial(keys_kernel, cap),
        out_shape=[
            jax.ShapeDtypeStruct((ROWS, 2, 2 * CHUNK, KV), BF),
            jax.ShapeDtypeStruct((ROWS, 1, QS), F32),
        ],
        grid_spec=pltpu.PrefetchScalarGridSpec(
            num_scalar_prefetch=3,
            grid=(ROWS,),
            in_specs=[
                pl.BlockSpec((CHUNK, CHUNK), lambda i, *_: (0, 0)),
                row(QS, KV),
                row(QUARTER, KV),
            ]
            + [ANY] * 20,
            out_specs=[row(2, 2 * CHUNK, KV), row(1, QS)],
            scratch_shapes=[
                pltpu.VMEM((2, 2, 2, 2 * MOST_M, HALF, KV), BF),
                pltpu.VMEM((QS, 128), F32),
                pltpu.SemaphoreType.DMA((2, 2, 2, 2)),
            ],
        ),
        compiler_params=pltpu.CompilerParams(vmem_limit_bytes=VMEM_LIMIT),
        name="keys",
    )(meta, place, filled, table, queries, fresh, *arrays)


def sums_kernel(places, meta_ref, order_ref, keys_ref, query_ref, fresh_ref, *refs):
    top_ref, outs, acc, total = refs[0], refs[1:-2], refs[-2], refs[-1]
    step = pl.program_id(0)
    row = order_ref[step]
    filled = meta_ref[ROWS + row]
    query = query_ref[0]
    peak = column_of(top_ref[0])
    for group in range(2):
        def add():
            keys = keys_ref[0, group]
            raw = products(query, keys) * score_scale + bias_row(group, filled)
            weights = jnp.exp(raw - jnp.concatenate([peak] * 4, axis=1))
            part = jnp.dot(weights.astype(BF), keys[:, :LAT], preferred_element_type=F32)
            if group == 0:
                total[...] = fold(jnp.add, weights)
                acc[...] = part
            else:
                total[...] += fold(jnp.add, weights)
                acc[...] += part

        if group == 0:
            add()
        else:
            pl.when(group * GROUP < filled)(add)

    if places[-1] == 0:
        @pl.when(step == len(places) - 1)
        def _():
            fresh = fresh_ref[0]
            weights = jnp.exp(draft_scores(query, fresh) - peak[:, :QUARTER])
            acc[...] += jnp.dot(weights.astype(BF), fresh[:, :LAT], preferred_element_type=F32)
            lane = lax.broadcasted_iota(I32, (QS, 128), 1)
            extra = jnp.sum(weights, axis=1, keepdims=True)
            total[...] += jnp.where(lane == 0, extra, 0.0)

    shares = row_of(jnp.sum(total[...], axis=1, keepdims=True))
    if len(places) == 1:
        cut = QS // 2
        outs[0][...] = acc[:cut]
        outs[1][:cut] = acc[cut:]
        outs[1][cut:, :QS] = shares
        outs[1][cut:, QS:] = jnp.zeros((RED - QS, LAT - QS), F32)
        return
    for i in range(len(places)):
        @pl.when(step == i)
        def _():
            outs[i][:QS] = acc[...]
            outs[i][QS:, :QS] = shares
            outs[i][QS:, QS:] = jnp.zeros((RED - QS, LAT - QS), F32)


def sums(places, grp, meta, keys, queries, fresh, top):
    count = len(places)
    heights = [QS // 2, RED - QS // 2] if count == 1 else [RED] * count
    order = (grp + jnp.array(places, I32)) % ROWS
    row = lambda *tail: pl.BlockSpec((1,) + tail, lambda i, m, o: (o[i],) + (0,) * len(tail))
    return pl.pallas_call(
        functools.partial(sums_kernel, places),
        out_shape=[jax.ShapeDtypeStruct((n, LAT), F32) for n in heights],
        grid_spec=pltpu.PrefetchScalarGridSpec(
            num_scalar_prefetch=2,
            grid=(count,),
            in_specs=[row(2, 2 * CHUNK, KV), row(QS, KV), row(QUARTER, KV)]
            + [row(1, QS)],
            out_specs=[pl.BlockSpec((n, LAT), lambda i, m, o: (0, 0)) for n in heights],
            scratch_shapes=[pltpu.VMEM((QS, LAT), F32), pltpu.VMEM((QS, 128), F32)],
        ),
        compiler_params=pltpu.CompilerParams(vmem_limit_bytes=VMEM_LIMIT),
        name="sums",
    )(meta, order, keys, queries, fresh, top)


def finish_kernel(a_ref, b_ref, c_ref, top_ref, bottom_ref):
    whole = a_ref[...] + (b_ref[...] + c_ref[...])
    total = jnp.transpose(jnp.broadcast_to(whole[QS : QS + 1, :QS], (128, QS)))
    total = jnp.concatenate([total] * 4, axis=1)
    out = (whole[:QS] / total).astype(BF)
    top_ref[...] = out[: QS // 2]
    bottom_ref[...] = out[QS // 2 :]


def finish(own, left, right):
    vmem = pl.BlockSpec(memory_space=pltpu.VMEM)
    return pl.pallas_call(
        finish_kernel,
        out_shape=[jax.ShapeDtypeStruct((QS // 2, LAT), BF)] * 2,
        in_specs=[vmem] * 3,
        out_specs=[vmem] * 2,
        compiler_params=pltpu.CompilerParams(vmem_limit_bytes=24 * 1024 * 1024),
        name="finish",
    )(own, left, right)


def place_kernel(grp_ref, *refs):
    ins, out_ref = refs[:16], refs[16]
    step = pl.program_id(0)
    for d in range(8):
        @pl.when(step == d)
        def _():
            out_ref[0, : QS // 2] = ins[2 * d][...]
            out_ref[0, QS // 2 :] = ins[2 * d + 1][...]


def put_in_place(grp, pieces):
    return pl.pallas_call(
        place_kernel,
        out_shape=jax.ShapeDtypeStruct((ROWS, QS, LAT), BF),
        grid_spec=pltpu.PrefetchScalarGridSpec(
            num_scalar_prefetch=1,
            grid=(ROWS,),
            in_specs=[pl.BlockSpec(memory_space=pltpu.VMEM)] * 16,
            out_specs=pl.BlockSpec((1, QS, LAT), lambda i, g: (lax.rem(g[0] + i, GRP), 0, 0)),
        ),
        compiler_params=pltpu.CompilerParams(vmem_limit_bytes=16 * 1024 * 1024),
        name="place",
    )(grp, *pieces)


def attention(cap, turn, grp, place, filled, meta, table, queries, fresh, arrays):
    keys, top = keys_and_top(cap, meta, place, filled, table, queries, fresh, arrays)

    every = jnp.broadcast_to(top[None], (GRP,) + top.shape)
    top = jnp.max(lax.all_to_all(every, "grp", 0, 0, tiled=True), axis=0)

    part = lambda *places: sums(places, grp, meta, keys, queries, fresh, top)
    far_top, far_bottom = part(4)
    up3, down3 = part(3, 5)
    up2, down2 = part(2, 6)
    up1, down1, own = part(1, 7, 0)

    cut = QS // 2
    up, down = turn(far_top, 1), turn(far_bottom, -1)
    up = turn(jnp.concatenate([up3[:cut] + up, up3[cut:]]), 1)
    down = turn(jnp.concatenate([down3[:cut], down3[cut:] + down]), -1)
    up, down = turn(up2 + up, 1), turn(down2 + down, -1)
    up, down = turn(up1 + up, 1), turn(down1 + down, -1)
    top_half, bottom_half = finish(own, up, down)

    got = [[top_half, bottom_half]] + [[None, None] for _ in range(7)]
    for d in (1, 2, 3):
        for h in range(2):
            got[8 - d][h] = turn(got[(9 - d) % 8][h], 1)
            got[d][h] = turn(got[d - 1][h], -1)
    got[4] = [turn(got[5][0], 1), turn(got[3][1], -1)]
    return put_in_place(grp[None], [half for pieces in got for half in pieces])


def body(coeffs, lengths, owners, row_pick, queries, new_latent):
    stored = coeffs[0, 0, 0]
    pair = lax.axis_index("pair").astype(I32)
    grp = lax.axis_index("grp").astype(I32)
    place = jnp.stack([pair // 4, pair % 4])

    owner = owners[:, 0]
    requests = jnp.arange(owner.shape[0], dtype=I32)
    mine = (owner == pair).astype(I32)
    before = jnp.sum(jnp.where(requests[None, :] < requests[:, None], mine[None, :], 0), axis=1)
    wanted = row_pick % jnp.sum(mine)
    hit = mine[None, :] * (before[None, :] == wanted[:, None]).astype(I32)
    request = jnp.sum(hit * requests[None, :], axis=1)
    flags = jnp.max(hit.reshape(ROWS, 16, 4), axis=(0, 2))

    filled = flags * jnp.sum(jnp.where(owner.reshape(16, 4) == pair, lengths, 0), axis=1)
    grid = filled.reshape(4, 4)
    most = jnp.maximum(jnp.max(jnp.sum(grid, axis=0)), jnp.max(jnp.sum(grid, axis=1)))
    over = (most > USUAL_CAP).astype(I32)
    flag_row = jnp.concatenate([flags, over[None]]).astype(BF)
    flag_block = jnp.zeros((1, QUARTER, KV), BF).at[0, :, :17].set(flag_row[None, :])
    quarter = lambda i: stored[:, i * QUARTER : (i + 1) * QUARTER]
    flagged = lambda v: jnp.concatenate([v, flag_block], axis=0)
    a_lo, a_hi = flagged(quarter(0)), quarter(1)
    b_lo, b_hi = flagged(quarter(2)), quarter(3)

    send = lambda v, perm: lax.ppermute(v, "pair", perm)

    def gather_line(lo, hi, perm):
        from_prev = send(lo, perm(1)), send(hi, perm(1))
        from_next = send(lo, perm(-1)), send(hi, perm(-1))
        return (lo, hi) + from_next + from_prev, from_prev[0], from_next[1]

    line_a, a_prev_lo, a_next_hi = gather_line(a_lo, a_hi, x_perm)
    line_b, b_prev_lo, b_next_hi = gather_line(b_lo, b_hi, y_perm)

    named = owner.reshape(16, 4)[:, :, None] == jnp.arange(16, dtype=I32)[None, None, :]
    earlier = jnp.arange(4)[None, :] < jnp.arange(4)[:, None]
    offsets = jnp.sum(jnp.where(earlier[None], lengths[:, None, :], 0), axis=2)
    len_of = jnp.sum(jnp.where(named, lengths[:, :, None], 0), axis=1)
    off_of = jnp.sum(jnp.where(named, offsets[:, :, None], 0), axis=1)
    request_len = jnp.sum(
        jnp.where(request[:, None] == requests[None, :], lengths.reshape(1, -1), 0), axis=1
    )
    meta = jnp.concatenate([request // 4, request_len])
    fresh = jnp.concatenate([new_latent, jnp.zeros((ROWS, QUARTER - STEPS, KV), BF)], axis=1)
    table = spread_table()

    a_prev_lo, b_prev_lo, place, len_of, off_of, filled, meta, fresh, table = (
        lax.optimization_barrier(
            (a_prev_lo, b_prev_lo, place, len_of, off_of, filled, meta, fresh, table)
        )
    )
    line_a = line_a + (send(a_prev_lo, x_perm(1)), send(a_next_hi, x_perm(-1)))
    line_b = line_b + (send(b_prev_lo, y_perm(1)), send(b_next_hi, y_perm(-1)))

    heard = lambda v: v[FLAG, 0, :17]
    told = jnp.stack([heard(v) for v in line_b[::2] + line_a[::2]])
    all_flags = told[:, :16].astype(I32)
    line_over = jnp.broadcast_to(jnp.max(told[4:, 16]), (QUARTER, KV))

    across = lambda v: lax.ppermute(v, "side", [(0, 1), (1, 0)])

    def second_hop(own, nxt, prv, perm):
        prv, nxt = send(nxt, perm(1)), send(prv, perm(-1))
        return own, nxt, prv, send(prv[:, HALF:], perm(1)), send(nxt[:, HALF:], perm(-1))

    def exchange(cap):
        packed = pack(cap, place, all_flags, len_of, off_of, line_over, line_a + line_b)
        here = second_hop(*packed[:3], y_perm) + second_hop(*packed[3:], x_perm)
        return here + tuple(across(v) for v in here)

    arrays = exchange(USUAL_CAP)
    seen = jnp.stack([line_over[0, 0]] + [arrays[i][USUAL_CAP, 0, 0] for i in (1, 2, 3)])
    turn = lambda v, shift: lax.ppermute(v, "grp", ring(shift))
    flat_queries = queries.reshape(ROWS, QS, KV)

    def attend(cap, arrays):
        return attention(
            cap, turn, grp, place, filled, meta, table, flat_queries, fresh, arrays
        )

    out = lax.cond(
        jnp.max(seen) > 0,
        lambda: attend(MOST_CAP, exchange(MOST_CAP)),
        lambda: attend(USUAL_CAP, arrays),
    )
    return out.reshape(ROWS, STEPS, HEADS, LAT)


def solution(mesh):
    return jax.shard_map(
        body,
        mesh=mesh,
        in_specs=(
            P("pair", "side", "grp", None, None, None),
            P(),
            P(),
            P("pair"),
            P("pair", None, "side", None),
            P("pair", None, None),
        ),
        out_specs=P("pair", None, "side", None),
        check_vma=False,
    )
```

```python
import functools
import math

import jax
import jax.numpy as jnp
import numpy as np
from jax import lax
from jax.experimental import pallas as pl
from jax.experimental.pallas import tpu as pltpu
from jax.sharding import PartitionSpec as P

LAT = 512
KV = 576
BLK = 64
HALF = 32
QUARTER = 16
STEPS = 4
MOST_M = 8
STORE = 20
ROWS = 8
HEADS = 64
QS = STEPS * HEADS
SIDE_LEN = 4
CAP = SIDE_LEN * MOST_M
GRP = 8
GROUP = 4
CHUNK = GROUP * BLK
VMEM_LIMIT = 56 * 1024 * 1024
RED = QS + 8
FLAG = STORE

score_scale = 192.0 ** (-0.5)
BF = jnp.bfloat16
F32 = jnp.float32
I32 = jnp.int32
RELS = (0, 1, 3, 2)


def spread_table():
    frequency = np.arange(BLK, dtype=np.float64)[:, None]
    position = np.arange(BLK, dtype=np.float64)[None, :]
    factor = np.sqrt(np.where(frequency > 0, 2.0, 1.0) / BLK)
    table = factor * np.cos(math.pi * (2.0 * position + 1.0) * frequency / (2.0 * BLK))
    table = table.reshape(2, HALF, BLK)
    spread = np.einsum("bc,hft->bthcf", np.eye(GROUP), table).reshape(CHUNK, CHUNK)
    return jnp.asarray(spread, BF)


def x_perm(shift):
    return [(y * 4 + x, y * 4 + (x + shift) % 4) for y in range(4) for x in range(4)]


def y_perm(shift):
    return [(y * 4 + x, (y + shift) % 4 * 4 + x) for y in range(4) for x in range(4)]


def ring(shift):
    return [(i, (i + shift) % GRP) for i in range(GRP)]


def pick4(index, values):
    out = values[3]
    for i in (2, 1, 0):
        out = jnp.where(index == i, values[i], out)
    return out


ANY = pl.BlockSpec(memory_space=pl.ANY)


def pack_kernel(place_ref, flags_ref, len_ref, off_ref, *refs):
    ins, outs = refs[:16], refs[16:24]
    y, x = place_ref[0], place_ref[1]
    low, high = pl.ds(0, QUARTER), pl.ds(QUARTER, QUARTER)
    for path in range(2):
        sources = ins[path * 8 : path * 8 + 8]
        along, across = (x, y) if path == 0 else (y, x)
        for kd, shift in enumerate(RELS):
            there = lax.rem(across + shift, 4)
            dest = there * 4 + x if path == 0 else y * 4 + there
            counts, offsets, starts = [], [], []
            total = jnp.int32(0)
            for s in range(4):
                p = y * 4 + s if path == 0 else s * 4 + x
                n = flags_ref[path * 4 + kd, p] * len_ref[p, dest]
                counts.append(n)
                offsets.append(off_ref[p, dest])
                starts.append(total)
                total = total + n
            for ks, near in enumerate(RELS):
                s = lax.rem(along + near, 4)
                n, o, d = pick4(s, counts), pick4(s, offsets), pick4(s, starts)
                source_lo, source_hi = sources[2 * ks : 2 * ks + 2]

                def move(i, carry):
                    out = outs[path * 4 + kd]
                    out[d + i, low] = source_lo[o + i]
                    out[d + i, high] = source_hi[o + i]
                    return carry

                lax.fori_loop(0, n, move, 0)


def pack(place, flags, len_of, off_of, arrays):
    half = jax.ShapeDtypeStruct((CAP, HALF, KV), BF)
    smem = pl.BlockSpec(memory_space=pltpu.SMEM)
    vmem = pl.BlockSpec(memory_space=pltpu.VMEM)
    return pl.pallas_call(
        pack_kernel,
        out_shape=[half] * 8,
        in_specs=[smem] * 4 + [vmem] * 16,
        out_specs=[vmem] * 8,
        compiler_params=pltpu.CompilerParams(vmem_limit_bytes=40 * 1024 * 1024),
        name="pack",
    )(place, flags, len_of, off_of, *arrays)


def column_of(row, width=128):
    return jnp.transpose(jnp.broadcast_to(row, (width, QS)))


def row_of(column):
    return jnp.transpose(jnp.broadcast_to(column, (QS, 128)))[:8]


def draft_scores(query, fresh):
    raw = (
        lax.dot_general(query, fresh, (((1,), (1,)), ((), ())), preferred_element_type=F32)
        * score_scale
    )
    step = lax.broadcasted_iota(I32, raw.shape, 0) // HEADS
    token = lax.broadcasted_iota(I32, raw.shape, 1)
    return jnp.where(token <= step, raw, -jnp.inf)


def bias_row(group, filled):
    token = lax.broadcasted_iota(I32, (1, CHUNK), 1)
    return jnp.where(token // BLK + group * GROUP < filled, 0.0, -jnp.inf)


def products(query, keys):
    return lax.dot_general(query, keys, (((1,), (1,)), ((), ())), preferred_element_type=F32)


def fold(op, wide):
    return op(wide[:, :128], wide[:, 128:])


def keys_kernel(meta_ref, place_ref, filled_ref, table_ref, query_ref, fresh_ref, *refs):
    ins = refs[:8]
    keys_ref, top_ref, hold, best, sems = refs[8:]
    row = pl.program_id(0)
    y, x = place_ref[0], place_ref[1]

    def spots(n):
        p = meta_ref[n]
        sy, sx = p // 4, lax.rem(p, 4)
        found = []
        for path in range(2):
            line, inner = (sy, sx) if path == 0 else (sx, sy)
            start = jnp.int32(0)
            for s in range(3):
                other = sy * 4 + s if path == 0 else s * 4 + sx
                start = start + jnp.where(s < inner, filled_ref[other], 0)
            rel = lax.rem(line - (y if path == 0 else x) + 4, 4)
            first = jnp.minimum(start, CAP - MOST_M)
            found.append((rel, first, start - first))
        return found

    def each_copy(n, act):
        slot = lax.rem(n, 2)
        found = spots(n)
        for path in range(2):
            rel, first, _ = found[path]
            for ref, shift in zip(ins[path * 4 : path * 4 + 4], RELS):
                @pl.when(rel == shift)
                def _():
                    act(
                        pltpu.make_async_copy(
                            ref.at[pl.ds(first, MOST_M)],
                            hold.at[slot, path, pl.ds(0, MOST_M)],
                            sems.at[slot, path],
                        )
                    )

    @pl.when(row == 0)
    def _():
        each_copy(jnp.int32(0), lambda c: c.start())

    @pl.when(row + 1 < ROWS)
    def _():
        each_copy(row + 1, lambda c: c.start())

    each_copy(row, lambda c: c.wait())
    slot = lax.rem(row, 2)
    found = spots(row)
    filled = meta_ref[ROWS + row]
    query = query_ref[0]
    draft = draft_scores(query, fresh_ref[0])
    best[...] = jnp.full((QS, 128), -jnp.inf, F32)
    for group in range(2):
        @pl.when(group * GROUP < filled)
        def _():
            parts = []
            for path in range(2):
                at = found[path][2] + group * GROUP
                for i in range(GROUP):
                    block = hold[slot, path, at + i]
                    live = i + group * GROUP < filled
                    parts.append(jnp.where(live, block, jnp.zeros_like(block)))
            packed = jnp.concatenate(parts, axis=0)
            keys = jnp.dot(table_ref[...], packed, preferred_element_type=F32).astype(BF)
            keys_ref[0, group] = keys
            raw = products(query, keys) + bias_row(group, filled)
            best[...] = jnp.maximum(best[...], fold(jnp.maximum, raw))
    cached = jnp.max(best[...], axis=1, keepdims=True) * score_scale
    top_ref[0] = row_of(jnp.maximum(cached, jnp.max(draft, axis=1, keepdims=True)))[:1]


def keys_and_top(meta, place, filled, table, queries, fresh, arrays):
    row = lambda *tail: pl.BlockSpec((1,) + tail, lambda i, *_: (i,) + (0,) * len(tail))
    return pl.pallas_call(
        keys_kernel,
        out_shape=[
            jax.ShapeDtypeStruct((ROWS, 2, CHUNK, KV), BF),
            jax.ShapeDtypeStruct((ROWS, 1, QS), F32),
        ],
        grid_spec=pltpu.PrefetchScalarGridSpec(
            num_scalar_prefetch=3,
            grid=(ROWS,),
            in_specs=[
                pl.BlockSpec((CHUNK, CHUNK), lambda i, *_: (0, 0)),
                row(QS, KV),
                row(QUARTER, KV),
            ]
            + [ANY] * 8,
            out_specs=[row(2, CHUNK, KV), row(1, QS)],
            scratch_shapes=[
                pltpu.VMEM((2, 2, 2 * MOST_M, HALF, KV), BF),
                pltpu.VMEM((QS, 128), F32),
                pltpu.SemaphoreType.DMA((2, 2)),
            ],
        ),
        compiler_params=pltpu.CompilerParams(vmem_limit_bytes=VMEM_LIMIT),
        name="keys",
    )(meta, place, filled, table, queries, fresh, *arrays)


def sums_kernel(places, meta_ref, order_ref, here_ref, there_ref, query_ref, fresh_ref, *refs):
    top_ref, outs, acc, total = refs[0], refs[1:-2], refs[-2], refs[-1]
    step = pl.program_id(0)
    row = order_ref[step]
    filled = meta_ref[ROWS + row]
    query = query_ref[0]
    peak = column_of(top_ref[0])
    for group in range(2):
        def add():
            part = share = None
            for keys_ref in (here_ref, there_ref):
                keys = keys_ref[0, group]
                raw = products(query, keys) * score_scale + bias_row(group, filled)
                weights = jnp.exp(raw - jnp.concatenate([peak] * 2, axis=1))
                more = jnp.dot(weights.astype(BF), keys[:, :LAT], preferred_element_type=F32)
                part = more if part is None else part + more
                more = fold(jnp.add, weights)
                share = more if share is None else share + more
            if group == 0:
                total[...] = share
                acc[...] = part
            else:
                total[...] += share
                acc[...] += part

        if group == 0:
            add()
        else:
            pl.when(group * GROUP < filled)(add)

    if places[-1] == 0:
        @pl.when(step == len(places) - 1)
        def _():
            fresh = fresh_ref[0]
            weights = jnp.exp(draft_scores(query, fresh) - peak[:, :QUARTER])
            acc[...] += jnp.dot(weights.astype(BF), fresh[:, :LAT], preferred_element_type=F32)
            lane = lax.broadcasted_iota(I32, (QS, 128), 1)
            extra = jnp.sum(weights, axis=1, keepdims=True)
            total[...] += jnp.where(lane == 0, extra, 0.0)

    shares = row_of(jnp.sum(total[...], axis=1, keepdims=True))
    if len(places) == 1:
        cut = QS // 2
        outs[0][...] = acc[:cut]
        outs[1][:cut] = acc[cut:]
        outs[1][cut:, :QS] = shares
        outs[1][cut:, QS:] = jnp.zeros((RED - QS, LAT - QS), F32)
        return
    for i in range(len(places)):
        @pl.when(step == i)
        def _():
            outs[i][:QS] = acc[...]
            outs[i][QS:, :QS] = shares
            outs[i][QS:, QS:] = jnp.zeros((RED - QS, LAT - QS), F32)


def sums(places, grp, meta, keys, queries, fresh, top):
    count = len(places)
    heights = [QS // 2, RED - QS // 2] if count == 1 else [RED] * count
    order = (grp + jnp.array(places, I32)) % ROWS
    row = lambda *tail: pl.BlockSpec((1,) + tail, lambda i, m, o: (o[i],) + (0,) * len(tail))
    return pl.pallas_call(
        functools.partial(sums_kernel, places),
        out_shape=[jax.ShapeDtypeStruct((n, LAT), F32) for n in heights],
        grid_spec=pltpu.PrefetchScalarGridSpec(
            num_scalar_prefetch=2,
            grid=(count,),
            in_specs=[row(2, CHUNK, KV)] * 2 + [row(QS, KV), row(QUARTER, KV)]
            + [row(1, QS)],
            out_specs=[pl.BlockSpec((n, LAT), lambda i, m, o: (0, 0)) for n in heights],
            scratch_shapes=[pltpu.VMEM((QS, LAT), F32), pltpu.VMEM((QS, 128), F32)],
        ),
        compiler_params=pltpu.CompilerParams(vmem_limit_bytes=VMEM_LIMIT),
        name="sums",
    )(meta, order, *keys, queries, fresh, top)


def finish_kernel(a_ref, b_ref, c_ref, top_ref, bottom_ref):
    whole = a_ref[...] + (b_ref[...] + c_ref[...])
    total = jnp.transpose(jnp.broadcast_to(whole[QS : QS + 1, :QS], (128, QS)))
    total = jnp.concatenate([total] * 4, axis=1)
    out = (whole[:QS] / total).astype(BF)
    top_ref[...] = out[: QS // 2]
    bottom_ref[...] = out[QS // 2 :]


def finish(own, left, right):
    vmem = pl.BlockSpec(memory_space=pltpu.VMEM)
    return pl.pallas_call(
        finish_kernel,
        out_shape=[jax.ShapeDtypeStruct((QS // 2, LAT), BF)] * 2,
        in_specs=[vmem] * 3,
        out_specs=[vmem] * 2,
        compiler_params=pltpu.CompilerParams(vmem_limit_bytes=24 * 1024 * 1024),
        name="finish",
    )(own, left, right)


def place_kernel(grp_ref, *refs):
    ins, out_ref = refs[:16], refs[16]
    step = pl.program_id(0)
    for d in range(8):
        @pl.when(step == d)
        def _():
            out_ref[0, : QS // 2] = ins[2 * d][...]
            out_ref[0, QS // 2 :] = ins[2 * d + 1][...]


def put_in_place(grp, pieces):
    return pl.pallas_call(
        place_kernel,
        out_shape=jax.ShapeDtypeStruct((ROWS, QS, LAT), BF),
        grid_spec=pltpu.PrefetchScalarGridSpec(
            num_scalar_prefetch=1,
            grid=(ROWS,),
            in_specs=[pl.BlockSpec(memory_space=pltpu.VMEM)] * 16,
            out_specs=pl.BlockSpec((1, QS, LAT), lambda i, g: (lax.rem(g[0] + i, GRP), 0, 0)),
        ),
        compiler_params=pltpu.CompilerParams(vmem_limit_bytes=16 * 1024 * 1024),
        name="place",
    )(grp, *pieces)


def attention(turn, grp, place, filled, meta, table, queries, fresh, here, there):
    keys_here, top_here = keys_and_top(meta, place, filled, table, queries, fresh, here)
    keys_there, top_there = keys_and_top(meta, place, filled, table, queries, fresh, there)
    keys, top = (keys_here, keys_there), jnp.maximum(top_here, top_there)

    every = jnp.broadcast_to(top[None], (GRP,) + top.shape)
    top = jnp.max(lax.all_to_all(every, "grp", 0, 0, tiled=True), axis=0)

    part = lambda *places: sums(places, grp, meta, keys, queries, fresh, top)
    far_top, far_bottom = part(4)
    up3, down3 = part(3, 5)
    up2, down2 = part(2, 6)
    up1, down1, own = part(1, 7, 0)

    cut = QS // 2
    up, down = turn(far_top, 1), turn(far_bottom, -1)
    up = turn(jnp.concatenate([up3[:cut] + up, up3[cut:]]), 1)
    down = turn(jnp.concatenate([down3[:cut], down3[cut:] + down]), -1)
    up, down = turn(up2 + up, 1), turn(down2 + down, -1)
    up, down = turn(up1 + up, 1), turn(down1 + down, -1)
    top_half, bottom_half = finish(own, up, down)

    got = [[top_half, bottom_half]] + [[None, None] for _ in range(7)]
    for d in (1, 2, 3):
        for h in range(2):
            got[8 - d][h] = turn(got[(9 - d) % 8][h], 1)
            got[d][h] = turn(got[d - 1][h], -1)
    got[4] = [turn(got[5][0], 1), turn(got[3][1], -1)]
    return put_in_place(grp[None], [half for pieces in got for half in pieces])


def body(coeffs, lengths, owners, row_pick, queries, new_latent):
    stored = coeffs[0, 0, 0]
    pair = lax.axis_index("pair").astype(I32)
    grp = lax.axis_index("grp").astype(I32)
    place = jnp.stack([pair // 4, pair % 4])

    owner = owners[:, 0]
    requests = jnp.arange(owner.shape[0], dtype=I32)
    mine = (owner == pair).astype(I32)
    before = jnp.sum(jnp.where(requests[None, :] < requests[:, None], mine[None, :], 0), axis=1)
    wanted = row_pick % jnp.sum(mine)
    hit = mine[None, :] * (before[None, :] == wanted[:, None]).astype(I32)
    request = jnp.sum(hit * requests[None, :], axis=1)
    flags = jnp.max(hit.reshape(ROWS, 16, 4), axis=(0, 2))

    filled = flags * jnp.sum(jnp.where(owner.reshape(16, 4) == pair, lengths, 0), axis=1)
    flag_block = jnp.zeros((1, QUARTER, KV), BF).at[0, :, :16].set(flags.astype(BF)[None, :])
    quarter = lambda i: stored[:, i * QUARTER : (i + 1) * QUARTER]
    flagged = lambda v: jnp.concatenate([v, flag_block], axis=0)
    a_lo, a_hi = flagged(quarter(0)), quarter(1)
    b_lo, b_hi = flagged(quarter(2)), quarter(3)

    send = lambda v, perm: lax.ppermute(v, "pair", perm)

    def gather_line(lo, hi, perm):
        from_prev = send(lo, perm(1)), send(hi, perm(1))
        from_next = send(lo, perm(-1)), send(hi, perm(-1))
        return (lo, hi) + from_next + from_prev, from_prev[0], from_next[1]

    line_a, a_prev_lo, a_next_hi = gather_line(a_lo, a_hi, x_perm)
    line_b, b_prev_lo, b_next_hi = gather_line(b_lo, b_hi, y_perm)

    named = owner.reshape(16, 4)[:, :, None] == jnp.arange(16, dtype=I32)[None, None, :]
    earlier = jnp.arange(4)[None, :] < jnp.arange(4)[:, None]
    offsets = jnp.sum(jnp.where(earlier[None], lengths[:, None, :], 0), axis=2)
    len_of = jnp.sum(jnp.where(named, lengths[:, :, None], 0), axis=1)
    off_of = jnp.sum(jnp.where(named, offsets[:, :, None], 0), axis=1)
    request_len = jnp.sum(
        jnp.where(request[:, None] == requests[None, :], lengths.reshape(1, -1), 0), axis=1
    )
    meta = jnp.concatenate([request // 4, request_len])
    fresh = jnp.concatenate([new_latent, jnp.zeros((ROWS, QUARTER - STEPS, KV), BF)], axis=1)
    table = spread_table()

    a_prev_lo, b_prev_lo, place, len_of, off_of, filled, meta, fresh, table = (
        lax.optimization_barrier(
            (a_prev_lo, b_prev_lo, place, len_of, off_of, filled, meta, fresh, table)
        )
    )
    line_a = line_a + (send(a_prev_lo, x_perm(1)), send(a_next_hi, x_perm(-1)))
    line_b = line_b + (send(b_prev_lo, y_perm(1)), send(b_next_hi, y_perm(-1)))

    heard = lambda v: v[FLAG, 0, :16]
    all_flags = jnp.stack([heard(v) for v in line_b[::2] + line_a[::2]]).astype(I32)
    packed = pack(place, all_flags, len_of, off_of, line_a + line_b)

    across = lambda v: lax.ppermute(v, "side", [(0, 1), (1, 0)])

    def second_hop(own, nxt, prv, opp, perm):
        return own, send(prv, perm(-1)), send(nxt, perm(1)), send(opp, perm(2))

    here = second_hop(*packed[:4], y_perm) + second_hop(*packed[4:], x_perm)
    there = tuple(across(v) for v in here)
    turn = lambda v, shift: lax.ppermute(v, "grp", ring(shift))
    flat_queries = queries.reshape(ROWS, QS, KV)
    out = attention(turn, grp, place, filled, meta, table, flat_queries, fresh, here, there)
    return out.reshape(ROWS, STEPS, HEADS, LAT)


def solution(mesh):
    return jax.shard_map(
        body,
        mesh=mesh,
        in_specs=(
            P("pair", "side", "grp", None, None, None),
            P(),
            P(),
            P("pair"),
            P("pair", None, "side", None),
            P("pair", None, None),
        ),
        out_specs=P("pair", None, "side", None),
        check_vma=False,
    )
```

```python
import functools
import math

import jax
import jax.numpy as jnp
import numpy as np
from jax import lax
from jax.experimental import pallas as pl
from jax.experimental.pallas import tpu as pltpu
from jax.sharding import PartitionSpec as P

LAT = 512
KV = 576
BLK = 64
HALF = 32
QUARTER = 16
STEPS = 4
MOST_M = 8
STORE = 20
ROWS = 8
HEADS = 64
QS = STEPS * HEADS
SIDE_LEN = 4
MOST_CAP = SIDE_LEN * MOST_M
USUAL_CAP = 24
GRP = 8
GROUP = 4
CHUNK = GROUP * BLK
VMEM_LIMIT = 56 * 1024 * 1024
RED = QS + 8
FLAG = STORE

score_scale = 192.0 ** (-0.5)
BF = jnp.bfloat16
F32 = jnp.float32
I32 = jnp.int32
RELS = (0, 1, 3, 2)


def spread_table():
    frequency = np.arange(BLK, dtype=np.float64)[:, None]
    position = np.arange(BLK, dtype=np.float64)[None, :]
    factor = np.sqrt(np.where(frequency > 0, 2.0, 1.0) / BLK)
    table = factor * np.cos(math.pi * (2.0 * position + 1.0) * frequency / (2.0 * BLK))
    table = table.reshape(2, HALF, BLK)
    spread = np.einsum("bc,hft->bthcf", np.eye(GROUP), table).reshape(CHUNK, CHUNK)
    return jnp.asarray(spread, BF)


def x_perm(shift):
    return [(y * 4 + x, y * 4 + (x + shift) % 4) for y in range(4) for x in range(4)]


def y_perm(shift):
    return [(y * 4 + x, (y + shift) % 4 * 4 + x) for y in range(4) for x in range(4)]


def ring(shift):
    return [(i, (i + shift) % GRP) for i in range(GRP)]


def pick4(index, values):
    out = values[3]
    for i in (2, 1, 0):
        out = jnp.where(index == i, values[i], out)
    return out


ANY = pl.BlockSpec(memory_space=pl.ANY)


def routes_kernel(pair_ref, owner_ref, len_ref, pick_ref, flag_ref, meta_ref, filled_ref):
    pair = pair_ref[0]
    mine = [(owner_ref[r] == pair).astype(I32) for r in range(64)]
    owned = functools.reduce(lambda a, b: a + b, mine)
    wanted = [lax.rem(pick_ref[n], owned) for n in range(ROWS)]
    request = [jnp.int32(0)] * ROWS
    rank = jnp.int32(0)
    for r in range(64):
        for n in range(ROWS):
            request[n] = jnp.where((mine[r] == 1) & (rank == wanted[n]), r, request[n])
        rank = rank + mine[r]
    source = [request[n] // 4 for n in range(ROWS)]
    blocks = [len_ref[source[n], lax.rem(request[n], 4)] for n in range(ROWS)]
    for n in range(ROWS):
        meta_ref[n] = source[n]
        meta_ref[ROWS + n] = blocks[n]
    filled = []
    lane = lax.broadcasted_iota(I32, (QUARTER, KV), 1)
    told = jnp.zeros((QUARTER, KV), F32)
    for p in range(16):
        total = jnp.int32(0)
        for n in range(ROWS):
            total = jnp.where(source[n] == p, blocks[n], total)
        filled.append(total)
        filled_ref[p] = total
        told = told + jnp.where((lane == p) & (total > 0), 1.0, 0.0)
    most = jnp.int32(0)
    for i in range(4):
        most = jnp.maximum(most, sum(filled[4 * i + 1 : 4 * i + 4], filled[4 * i]))
        most = jnp.maximum(most, sum(filled[i + 4 :: 4], filled[i]))
    told = told + jnp.where((lane == 16) & (most > USUAL_CAP), 1.0, 0.0)
    flag_ref[0] = told.astype(BF)


def routes(pair, owner, lengths, row_pick):
    smem = pl.BlockSpec(memory_space=pltpu.SMEM)
    return pl.pallas_call(
        routes_kernel,
        out_shape=[
            jax.ShapeDtypeStruct((1, QUARTER, KV), BF),
            jax.ShapeDtypeStruct((2 * ROWS,), I32),
            jax.ShapeDtypeStruct((16,), I32),
        ],
        in_specs=[smem] * 4,
        out_specs=[pl.BlockSpec(memory_space=pltpu.VMEM), smem, smem],
        name="routes",
    )(pair, owner, lengths, row_pick)


def overflow_kernel(own_ref, *refs):
    ins, out_ref, hold, sems = refs[:3], refs[3], refs[4], refs[5]
    copies = [
        pltpu.make_async_copy(
            ref.at[USUAL_CAP, pl.ds(0, QUARTER), pl.ds(0, 128)], hold.at[i], sems.at[i]
        )
        for i, ref in enumerate(ins)
    ]
    for copy in copies:
        copy.start()
    for copy in copies:
        copy.wait()
    most = jnp.maximum(jnp.maximum(hold[0], hold[1]), jnp.maximum(hold[2], own_ref[:, :128]))
    out_ref[...] = most.astype(F32)


def overflow(own, arrays):
    vmem = pl.BlockSpec(memory_space=pltpu.VMEM)
    return pl.pallas_call(
        overflow_kernel,
        out_shape=jax.ShapeDtypeStruct((QUARTER, 128), F32),
        in_specs=[vmem] + [ANY] * 3,
        out_specs=vmem,
        scratch_shapes=[pltpu.VMEM((3, QUARTER, 128), BF), pltpu.SemaphoreType.DMA((3,))],
        name="overflow",
    )(own, *arrays)


def pack_kernel(cap, place_ref, flags_ref, len_ref, off_ref, over_ref, *refs):
    ins, outs = refs[:16], refs[16:24]
    y, x = place_ref[0], place_ref[1]
    low, high = pl.ds(0, QUARTER), pl.ds(QUARTER, QUARTER)
    for path in range(2):
        sources = ins[path * 8 : path * 8 + 8]
        for out in outs[path * 4 + 1 : path * 4 + 4]:
            out[cap, low] = over_ref[...]
        along, across = (x, y) if path == 0 else (y, x)
        for kd, shift in enumerate(RELS):
            there = lax.rem(across + shift, 4)
            dest = there * 4 + x if path == 0 else y * 4 + there
            counts, offsets, starts = [], [], []
            total = jnp.int32(0)
            for s in range(4):
                p = y * 4 + s if path == 0 else s * 4 + x
                n = flags_ref[path * 4 + kd, p] * len_ref[p, dest]
                counts.append(n)
                offsets.append(off_ref[p, dest])
                starts.append(total)
                total = total + n
            for ks, near in enumerate(RELS):
                s = lax.rem(along + near, 4)
                n, o, d = pick4(s, counts), pick4(s, offsets), pick4(s, starts)
                source_lo, source_hi = sources[2 * ks : 2 * ks + 2]

                def move(i, carry):
                    out = outs[path * 4 + kd]
                    out[d + i, low] = source_lo[o + i]
                    out[d + i, high] = source_hi[o + i]
                    return carry

                lax.fori_loop(0, jnp.minimum(n, jnp.maximum(cap - d, 0)), move, 0)


def pack(cap, place, flags, len_of, off_of, over, arrays):
    own = jax.ShapeDtypeStruct((cap, HALF, KV), BF)
    sent = jax.ShapeDtypeStruct((cap + 1, HALF, KV), BF)
    smem = pl.BlockSpec(memory_space=pltpu.SMEM)
    vmem = pl.BlockSpec(memory_space=pltpu.VMEM)
    return pl.pallas_call(
        functools.partial(pack_kernel, cap),
        out_shape=[own, sent, sent, sent] * 2,
        in_specs=[smem] * 4 + [vmem] * 17,
        out_specs=[vmem] * 8,
        compiler_params=pltpu.CompilerParams(vmem_limit_bytes=40 * 1024 * 1024),
        name="pack",
    )(place, flags, len_of, off_of, over, *arrays)


def column_of(row, width=128):
    return jnp.transpose(jnp.broadcast_to(row, (width, QS)))


def row_of(column):
    return jnp.transpose(jnp.broadcast_to(column, (QS, 128)))[:8]


def draft_scores(query, fresh):
    raw = (
        lax.dot_general(query, fresh, (((1,), (1,)), ((), ())), preferred_element_type=F32)
        * score_scale
    )
    step = lax.broadcasted_iota(I32, raw.shape, 0) // HEADS
    token = lax.broadcasted_iota(I32, raw.shape, 1)
    return jnp.where(token <= step, raw, -jnp.inf)


def bias_row(group, filled):
    token = lax.rem(lax.broadcasted_iota(I32, (1, 2 * CHUNK), 1), CHUNK)
    return jnp.where(token // BLK + group * GROUP < filled, 0.0, -jnp.inf)


def products(query, keys):
    return lax.dot_general(query, keys, (((1,), (1,)), ((), ())), preferred_element_type=F32)


def fold(op, wide):
    return op(op(wide[:, :128], wide[:, 128:256]), op(wide[:, 256:384], wide[:, 384:]))


def keys_kernel(cap, meta_ref, place_ref, filled_ref, table_ref, query_ref, fresh_ref, *refs):
    ins = refs[:16]
    keys_ref, top_ref, hold, best, sems = refs[16:]
    row = pl.program_id(0)
    y, x = place_ref[0], place_ref[1]

    def spots(n):
        p = meta_ref[n]
        sy, sx = p // 4, lax.rem(p, 4)
        found = []
        for path in range(2):
            line, inner = (sy, sx) if path == 0 else (sx, sy)
            start = jnp.int32(0)
            for s in range(3):
                other = sy * 4 + s if path == 0 else s * 4 + sx
                start = start + jnp.where(s < inner, filled_ref[other], 0)
            rel = lax.rem(line - (y if path == 0 else x) + 4, 4)
            first = jnp.minimum(start, cap - MOST_M)
            found.append((rel, first, start - first))
        return found

    def each_copy(n, act):
        slot = lax.rem(n, 2)
        found = spots(n)
        for side in range(2):
            for path in range(2):
                rel, first, _ = found[path]
                at = (side * 2 + path) * 4
                for ref, shift in zip(ins[at : at + 4], RELS):
                    @pl.when(rel == shift)
                    def _():
                        act(
                            pltpu.make_async_copy(
                                ref.at[pl.ds(first, MOST_M)],
                                hold.at[slot, side, path, pl.ds(0, MOST_M)],
                                sems.at[slot, side, path],
                            )
                        )

    @pl.when(row == 0)
    def _():
        each_copy(jnp.int32(0), lambda c: c.start())

    @pl.when(row + 1 < ROWS)
    def _():
        each_copy(row + 1, lambda c: c.start())

    each_copy(row, lambda c: c.wait())
    slot = lax.rem(row, 2)
    found = spots(row)
    filled = meta_ref[ROWS + row]
    query = query_ref[0]
    draft = draft_scores(query, fresh_ref[0])
    best[...] = jnp.full((QS, 128), -jnp.inf, F32)
    for group in range(2):
        @pl.when(group * GROUP < filled)
        def _():
            for side in range(2):
                parts = []
                for path in range(2):
                    at = found[path][2] + group * GROUP
                    for i in range(GROUP):
                        block = hold[slot, side, path, at + i]
                        live = i + group * GROUP < filled
                        parts.append(jnp.where(live, block, jnp.zeros_like(block)))
                packed = jnp.concatenate(parts, axis=0)
                keys_ref[0, group, side * CHUNK : side * CHUNK + CHUNK] = jnp.dot(
                    table_ref[...], packed, preferred_element_type=F32
                ).astype(BF)
            raw = products(query, keys_ref[0, group]) + bias_row(group, filled)
            best[...] = jnp.maximum(best[...], fold(jnp.maximum, raw))
    cached = jnp.max(best[...], axis=1, keepdims=True) * score_scale
    top_ref[0] = row_of(jnp.maximum(cached, jnp.max(draft, axis=1, keepdims=True)))[:1]


def keys_and_top(cap, meta, place, filled, table, queries, fresh, arrays):
    row = lambda *tail: pl.BlockSpec((1,) + tail, lambda i, *_: (i,) + (0,) * len(tail))
    return pl.pallas_call(
        functools.partial(keys_kernel, cap),
        out_shape=[
            jax.ShapeDtypeStruct((ROWS, 2, 2 * CHUNK, KV), BF),
            jax.ShapeDtypeStruct((ROWS, 1, QS), F32),
        ],
        grid_spec=pltpu.PrefetchScalarGridSpec(
            num_scalar_prefetch=3,
            grid=(ROWS,),
            in_specs=[
                pl.BlockSpec((CHUNK, CHUNK), lambda i, *_: (0, 0)),
                row(QS, KV),
                row(QUARTER, KV),
            ]
            + [ANY] * 16,
            out_specs=[row(2, 2 * CHUNK, KV), row(1, QS)],
            scratch_shapes=[
                pltpu.VMEM((2, 2, 2, 2 * MOST_M, HALF, KV), BF),
                pltpu.VMEM((QS, 128), F32),
                pltpu.SemaphoreType.DMA((2, 2, 2)),
            ],
        ),
        compiler_params=pltpu.CompilerParams(vmem_limit_bytes=VMEM_LIMIT),
        name="keys",
    )(meta, place, filled, table, queries, fresh, *arrays)


def sums_kernel(places, meta_ref, order_ref, keys_ref, query_ref, fresh_ref, *refs):
    top_ref, outs, acc, total = refs[0], refs[1:-2], refs[-2], refs[-1]
    step = pl.program_id(0)
    row = order_ref[step]
    filled = meta_ref[ROWS + row]
    query = query_ref[0]
    peak = column_of(top_ref[0])
    for group in range(2):
        def add():
            keys = keys_ref[0, group]
            raw = products(query, keys) * score_scale + bias_row(group, filled)
            weights = jnp.exp(raw - jnp.concatenate([peak] * 4, axis=1))
            part = jnp.dot(weights.astype(BF), keys[:, :LAT], preferred_element_type=F32)
            if group == 0:
                total[...] = fold(jnp.add, weights)
                acc[...] = part
            else:
                total[...] += fold(jnp.add, weights)
                acc[...] += part

        if group == 0:
            add()
        else:
            pl.when(group * GROUP < filled)(add)

    if places[-1] == 0:
        @pl.when(step == len(places) - 1)
        def _():
            fresh = fresh_ref[0]
            weights = jnp.exp(draft_scores(query, fresh) - peak[:, :QUARTER])
            acc[...] += jnp.dot(weights.astype(BF), fresh[:, :LAT], preferred_element_type=F32)
            lane = lax.broadcasted_iota(I32, (QS, 128), 1)
            extra = jnp.sum(weights, axis=1, keepdims=True)
            total[...] += jnp.where(lane == 0, extra, 0.0)

    shares = row_of(jnp.sum(total[...], axis=1, keepdims=True))
    if len(places) == 1:
        cut = QS // 2
        outs[0][...] = acc[:cut]
        outs[1][:cut] = acc[cut:]
        outs[1][cut:, :QS] = shares
        outs[1][cut:, QS:] = jnp.zeros((RED - QS, LAT - QS), F32)
        return
    for i in range(len(places)):
        @pl.when(step == i)
        def _():
            outs[i][:QS] = acc[...]
            outs[i][QS:, :QS] = shares
            outs[i][QS:, QS:] = jnp.zeros((RED - QS, LAT - QS), F32)


def sums(places, grp, meta, keys, queries, fresh, top):
    count = len(places)
    heights = [QS // 2, RED - QS // 2] if count == 1 else [RED] * count
    order = (grp + jnp.array(places, I32)) % ROWS
    row = lambda *tail: pl.BlockSpec((1,) + tail, lambda i, m, o: (o[i],) + (0,) * len(tail))
    return pl.pallas_call(
        functools.partial(sums_kernel, places),
        out_shape=[jax.ShapeDtypeStruct((n, LAT), F32) for n in heights],
        grid_spec=pltpu.PrefetchScalarGridSpec(
            num_scalar_prefetch=2,
            grid=(count,),
            in_specs=[row(2, 2 * CHUNK, KV), row(QS, KV), row(QUARTER, KV)]
            + [row(1, QS)],
            out_specs=[pl.BlockSpec((n, LAT), lambda i, m, o: (0, 0)) for n in heights],
            scratch_shapes=[pltpu.VMEM((QS, LAT), F32), pltpu.VMEM((QS, 128), F32)],
        ),
        compiler_params=pltpu.CompilerParams(vmem_limit_bytes=VMEM_LIMIT),
        name="sums",
    )(meta, order, keys, queries, fresh, top)


def finish_kernel(a_ref, b_ref, c_ref, top_ref, bottom_ref):
    whole = a_ref[...] + (b_ref[...] + c_ref[...])
    total = jnp.transpose(jnp.broadcast_to(whole[QS : QS + 1, :QS], (128, QS)))
    total = jnp.concatenate([total] * 4, axis=1)
    out = (whole[:QS] / total).astype(BF)
    top_ref[...] = out[: QS // 2]
    bottom_ref[...] = out[QS // 2 :]


def finish(own, left, right):
    vmem = pl.BlockSpec(memory_space=pltpu.VMEM)
    return pl.pallas_call(
        finish_kernel,
        out_shape=[jax.ShapeDtypeStruct((QS // 2, LAT), BF)] * 2,
        in_specs=[vmem] * 3,
        out_specs=[vmem] * 2,
        compiler_params=pltpu.CompilerParams(vmem_limit_bytes=24 * 1024 * 1024),
        name="finish",
    )(own, left, right)


def place_kernel(grp_ref, *refs):
    ins, out_ref = refs[:16], refs[16]
    step = pl.program_id(0)
    for d in range(8):
        @pl.when(step == d)
        def _():
            out_ref[0, : QS // 2] = ins[2 * d][...]
            out_ref[0, QS // 2 :] = ins[2 * d + 1][...]


def put_in_place(grp, pieces):
    return pl.pallas_call(
        place_kernel,
        out_shape=jax.ShapeDtypeStruct((ROWS, QS, LAT), BF),
        grid_spec=pltpu.PrefetchScalarGridSpec(
            num_scalar_prefetch=1,
            grid=(ROWS,),
            in_specs=[pl.BlockSpec(memory_space=pltpu.VMEM)] * 16,
            out_specs=pl.BlockSpec((1, QS, LAT), lambda i, g: (lax.rem(g[0] + i, GRP), 0, 0)),
        ),
        compiler_params=pltpu.CompilerParams(vmem_limit_bytes=16 * 1024 * 1024),
        name="place",
    )(grp, *pieces)


def attention(cap, turn, grp, place, filled, meta, table, queries, fresh, arrays):
    keys, top = keys_and_top(cap, meta, place, filled, table, queries, fresh, arrays)

    every = jnp.broadcast_to(top[None], (GRP,) + top.shape)
    top = jnp.max(lax.all_to_all(every, "grp", 0, 0, tiled=True), axis=0)

    part = lambda *places: sums(places, grp, meta, keys, queries, fresh, top)
    far_top, far_bottom = part(4)
    up3, down3 = part(3, 5)
    up2, down2 = part(2, 6)
    up1, down1, own = part(1, 7, 0)

    cut = QS // 2
    up, down = turn(far_top, 1), turn(far_bottom, -1)
    up = turn(jnp.concatenate([up3[:cut] + up, up3[cut:]]), 1)
    down = turn(jnp.concatenate([down3[:cut], down3[cut:] + down]), -1)
    up, down = turn(up2 + up, 1), turn(down2 + down, -1)
    up, down = turn(up1 + up, 1), turn(down1 + down, -1)
    top_half, bottom_half = finish(own, up, down)

    got = [[top_half, bottom_half]] + [[None, None] for _ in range(7)]
    for d in (1, 2, 3):
        for h in range(2):
            got[8 - d][h] = turn(got[(9 - d) % 8][h], 1)
            got[d][h] = turn(got[d - 1][h], -1)
    got[4] = [turn(got[5][0], 1), turn(got[3][1], -1)]
    return put_in_place(grp[None], [half for pieces in got for half in pieces])


def body(coeffs, lengths, owners, row_pick, queries, new_latent):
    stored = coeffs[0, 0, 0]
    pair = lax.axis_index("pair").astype(I32)
    grp = lax.axis_index("grp").astype(I32)
    place = jnp.stack([pair // 4, pair % 4])

    owner = owners[:, 0]
    flag_block, meta, filled = routes(pair[None], owner, lengths, row_pick)
    quarter = lambda i: stored[:, i * QUARTER : (i + 1) * QUARTER]
    flagged = lambda v: jnp.concatenate([v, flag_block], axis=0)
    a_lo, a_hi = flagged(quarter(0)), quarter(1)
    b_lo, b_hi = flagged(quarter(2)), quarter(3)

    send = lambda v, perm: lax.ppermute(v, "pair", perm)

    def gather_line(lo, hi, perm):
        from_prev = send(lo, perm(1)), send(hi, perm(1))
        from_next = send(lo, perm(-1)), send(hi, perm(-1))
        return (lo, hi) + from_next + from_prev, from_prev[0], from_next[1]

    line_a, a_prev_lo, a_next_hi = gather_line(a_lo, a_hi, x_perm)
    line_b, b_prev_lo, b_next_hi = gather_line(b_lo, b_hi, y_perm)

    named = owner.reshape(16, 4)[:, :, None] == jnp.arange(16, dtype=I32)[None, None, :]
    earlier = jnp.arange(4)[None, :] < jnp.arange(4)[:, None]
    offsets = jnp.sum(jnp.where(earlier[None], lengths[:, None, :], 0), axis=2)
    len_of = jnp.sum(jnp.where(named, lengths[:, :, None], 0), axis=1)
    off_of = jnp.sum(jnp.where(named, offsets[:, :, None], 0), axis=1)
    fresh = jnp.concatenate([new_latent, jnp.zeros((ROWS, QUARTER - STEPS, KV), BF)], axis=1)
    table = spread_table()

    a_prev_lo, b_prev_lo, place, len_of, off_of, fresh, table = (
        lax.optimization_barrier(
            (a_prev_lo, b_prev_lo, place, len_of, off_of, fresh, table)
        )
    )
    line_a = line_a + (send(a_prev_lo, x_perm(1)), send(a_next_hi, x_perm(-1)))
    line_b = line_b + (send(b_prev_lo, y_perm(1)), send(b_next_hi, y_perm(-1)))

    heard = lambda v: v[FLAG, 0, :17]
    told = jnp.stack([heard(v) for v in line_b[::2] + line_a[::2]])
    all_flags = told[:, :16].astype(I32)
    line_over = jnp.broadcast_to(jnp.max(told[4:, 16]), (QUARTER, KV))

    across = lambda v: lax.ppermute(v, "side", [(0, 1), (1, 0)])

    def second_hop(own, nxt, prv, opp, perm):
        return own, send(prv, perm(-1)), send(nxt, perm(1)), send(opp, perm(2))

    def exchange(cap):
        packed = pack(cap, place, all_flags, len_of, off_of, line_over, line_a + line_b)
        here = second_hop(*packed[:4], y_perm) + second_hop(*packed[4:], x_perm)
        return here + tuple(across(v) for v in here)

    arrays = exchange(USUAL_CAP)
    seen = overflow(line_over, arrays[1:4])
    turn = lambda v, shift: lax.ppermute(v, "grp", ring(shift))
    flat_queries = queries.reshape(ROWS, QS, KV)

    def attend(cap, arrays):
        return attention(
            cap, turn, grp, place, filled, meta, table, flat_queries, fresh, arrays
        )

    out = lax.cond(
        seen[0, 0] > 0,
        lambda: attend(MOST_CAP, exchange(MOST_CAP)),
        lambda: attend(USUAL_CAP, arrays),
    )
    return out.reshape(ROWS, STEPS, HEADS, LAT)


def solution(mesh):
    return jax.shard_map(
        body,
        mesh=mesh,
        in_specs=(
            P("pair", "side", "grp", None, None, None),
            P(),
            P(),
            P("pair"),
            P("pair", None, "side", None),
            P("pair", None, None),
        ),
        out_specs=P("pair", None, "side", None),
        check_vma=False,
    )
```

```python
import functools
import math

import jax
import jax.numpy as jnp
import numpy as np
from jax import lax
from jax.experimental import pallas as pl
from jax.experimental.pallas import tpu as pltpu
from jax.sharding import PartitionSpec as P

LAT = 512
KV = 576
BLK = 64
HALF = 32
QUARTER = 16
STEPS = 4
MOST_M = 8
STORE = 20
ROWS = 8
HEADS = 64
QS = STEPS * HEADS
SIDE_LEN = 4
MOST_CAP = SIDE_LEN * MOST_M
USUAL_CAP = 24
GRP = 8
GROUP = 4
CHUNK = GROUP * BLK
VMEM_LIMIT = 56 * 1024 * 1024
RED = QS + 8
FLAG = STORE

score_scale = 192.0 ** (-0.5)
BF = jnp.bfloat16
F32 = jnp.float32
I32 = jnp.int32
RELS = (0, 1, 3, 2)


def spread_table():
    frequency = np.arange(BLK, dtype=np.float64)[:, None]
    position = np.arange(BLK, dtype=np.float64)[None, :]
    factor = np.sqrt(np.where(frequency > 0, 2.0, 1.0) / BLK)
    table = factor * np.cos(math.pi * (2.0 * position + 1.0) * frequency / (2.0 * BLK))
    table = table.reshape(2, HALF, BLK)
    spread = np.einsum("bc,hft->bthcf", np.eye(GROUP), table).reshape(CHUNK, CHUNK)
    return jnp.asarray(spread, BF)


def x_perm(shift):
    return [(y * 4 + x, y * 4 + (x + shift) % 4) for y in range(4) for x in range(4)]


def y_perm(shift):
    return [(y * 4 + x, (y + shift) % 4 * 4 + x) for y in range(4) for x in range(4)]


def ring(shift):
    return [(i, (i + shift) % GRP) for i in range(GRP)]


def pick4(index, values):
    out = values[3]
    for i in (2, 1, 0):
        out = jnp.where(index == i, values[i], out)
    return out


ANY = pl.BlockSpec(memory_space=pl.ANY)


def routes_kernel(pair_ref, owner_ref, len_ref, pick_ref, flag_ref, meta_ref, filled_ref):
    pair = pair_ref[0]
    mine = [(owner_ref[r] == pair).astype(I32) for r in range(64)]
    owned = functools.reduce(lambda a, b: a + b, mine)
    wanted = [lax.rem(pick_ref[n], owned) for n in range(ROWS)]
    request = [jnp.int32(0)] * ROWS
    rank = jnp.int32(0)
    for r in range(64):
        for n in range(ROWS):
            request[n] = jnp.where((mine[r] == 1) & (rank == wanted[n]), r, request[n])
        rank = rank + mine[r]
    source = [request[n] // 4 for n in range(ROWS)]
    blocks = [len_ref[source[n], lax.rem(request[n], 4)] for n in range(ROWS)]
    for n in range(ROWS):
        meta_ref[n] = source[n]
        meta_ref[ROWS + n] = blocks[n]
    filled = []
    lane = lax.broadcasted_iota(I32, (QUARTER, KV), 1)
    told = jnp.zeros((QUARTER, KV), F32)
    for p in range(16):
        total = jnp.int32(0)
        for n in range(ROWS):
            total = jnp.where(source[n] == p, blocks[n], total)
        filled.append(total)
        filled_ref[p] = total
        told = told + jnp.where((lane == p) & (total > 0), 1.0, 0.0)
    most = jnp.int32(0)
    for i in range(4):
        most = jnp.maximum(most, sum(filled[4 * i + 1 : 4 * i + 4], filled[4 * i]))
        most = jnp.maximum(most, sum(filled[i + 4 :: 4], filled[i]))
    told = told + jnp.where((lane == 16) & (most > USUAL_CAP), 1.0, 0.0)
    flag_ref[0] = told.astype(BF)


def routes(pair, owner, lengths, row_pick):
    smem = pl.BlockSpec(memory_space=pltpu.SMEM)
    return pl.pallas_call(
        routes_kernel,
        out_shape=[
            jax.ShapeDtypeStruct((1, QUARTER, KV), BF),
            jax.ShapeDtypeStruct((2 * ROWS,), I32),
            jax.ShapeDtypeStruct((16,), I32),
        ],
        in_specs=[smem] * 4,
        out_specs=[pl.BlockSpec(memory_space=pltpu.VMEM), smem, smem],
        name="routes",
    )(pair, owner, lengths, row_pick)


def overflow_kernel(own_ref, *refs):
    ins, out_ref, hold, sems = refs[:3], refs[3], refs[4], refs[5]
    copies = [
        pltpu.make_async_copy(
            ref.at[USUAL_CAP, pl.ds(0, QUARTER), pl.ds(0, 128)], hold.at[i], sems.at[i]
        )
        for i, ref in enumerate(ins)
    ]
    for copy in copies:
        copy.start()
    for copy in copies:
        copy.wait()
    most = jnp.maximum(jnp.maximum(hold[0], hold[1]), jnp.maximum(hold[2], own_ref[:, :128]))
    out_ref[0] = jnp.max(most.astype(F32)).astype(I32)


def overflow(own, arrays):
    vmem = pl.BlockSpec(memory_space=pltpu.VMEM)
    return pl.pallas_call(
        overflow_kernel,
        out_shape=jax.ShapeDtypeStruct((1,), I32),
        in_specs=[vmem] + [ANY] * 3,
        out_specs=pl.BlockSpec(memory_space=pltpu.SMEM),
        scratch_shapes=[pltpu.VMEM((3, QUARTER, 128), BF), pltpu.SemaphoreType.DMA((3,))],
        name="overflow",
    )(own, *arrays)


def pack_kernel(cap, place_ref, flags_ref, len_ref, off_ref, over_ref, *refs):
    ins, outs = refs[:16], refs[16:23]
    y, x = place_ref[0], place_ref[1]
    low, high, tail = pl.ds(0, QUARTER), pl.ds(QUARTER, QUARTER), pl.ds(HALF, QUARTER)
    for path in range(2):
        sources = ins[path * 8 : path * 8 + 8]
        if path == 0:
            for out in outs[1:4]:
                out[cap, low] = over_ref[...]
        along, across = (x, y) if path == 0 else (y, x)
        for kd, shift in enumerate(RELS):
            there = lax.rem(across + shift, 4)
            dest = there * 4 + x if path == 0 else y * 4 + there
            counts, offsets, starts = [], [], []
            total = jnp.int32(0)
            for s in range(4):
                p = y * 4 + s if path == 0 else s * 4 + x
                n = flags_ref[path * 4 + kd, p] * len_ref[p, dest]
                counts.append(n)
                offsets.append(off_ref[p, dest])
                starts.append(total)
                total = total + n
            for ks, near in enumerate(RELS):
                s = lax.rem(along + near, 4)
                n, o, d = pick4(s, counts), pick4(s, offsets), pick4(s, starts)
                source_lo, source_hi = sources[2 * ks : 2 * ks + 2]

                def move(i, carry):
                    first, second = source_lo[o + i], source_hi[o + i]
                    if path == 1 and kd == 3:
                        outs[5][d + i, tail] = first
                        outs[6][d + i, tail] = second
                    else:
                        outs[path * 4 + kd][d + i, low] = first
                        outs[path * 4 + kd][d + i, high] = second
                    return carry

                lax.fori_loop(0, jnp.minimum(n, jnp.maximum(cap - d, 0)), move, 0)


def pack(cap, place, flags, len_of, off_of, over, arrays):
    own = jax.ShapeDtypeStruct((cap, HALF, KV), BF)
    sent = jax.ShapeDtypeStruct((cap + 1, HALF, KV), BF)
    more = jax.ShapeDtypeStruct((cap, HALF + QUARTER, KV), BF)
    smem = pl.BlockSpec(memory_space=pltpu.SMEM)
    vmem = pl.BlockSpec(memory_space=pltpu.VMEM)
    return pl.pallas_call(
        functools.partial(pack_kernel, cap),
        out_shape=[own, sent, sent, sent, own, more, more],
        in_specs=[smem] * 4 + [vmem] * 17,
        out_specs=[vmem] * 7,
        compiler_params=pltpu.CompilerParams(vmem_limit_bytes=40 * 1024 * 1024),
        name="pack",
    )(place, flags, len_of, off_of, over, *arrays)


def column_of(row, width=128):
    return jnp.transpose(jnp.broadcast_to(row, (width, QS)))


def row_of(column):
    return jnp.transpose(jnp.broadcast_to(column, (QS, 128)))[:8]


def draft_scores(query, fresh):
    raw = (
        lax.dot_general(query, fresh, (((1,), (1,)), ((), ())), preferred_element_type=F32)
        * score_scale
    )
    step = lax.broadcasted_iota(I32, raw.shape, 0) // HEADS
    token = lax.broadcasted_iota(I32, raw.shape, 1)
    return jnp.where(token <= step, raw, -jnp.inf)


def bias_row(group, filled):
    token = lax.rem(lax.broadcasted_iota(I32, (1, 2 * CHUNK), 1), CHUNK)
    return jnp.where(token // BLK + group * GROUP < filled, 0.0, -jnp.inf)


def products(query, keys):
    return lax.dot_general(query, keys, (((1,), (1,)), ((), ())), preferred_element_type=F32)


def fold(op, wide):
    return op(op(wide[:, :128], wide[:, 128:256]), op(wide[:, 256:384], wide[:, 384:]))


def keys_kernel(cap, meta_ref, place_ref, filled_ref, table_ref, query_ref, fresh_ref, *refs):
    ins = refs[:18]
    keys_ref, top_ref, hold, best, sems = refs[18:]
    row = pl.program_id(0)
    y, x = place_ref[0], place_ref[1]

    def spots(n):
        p = meta_ref[n]
        sy, sx = p // 4, lax.rem(p, 4)
        found = []
        for path in range(2):
            line, inner = (sy, sx) if path == 0 else (sx, sy)
            start = jnp.int32(0)
            for s in range(3):
                other = sy * 4 + s if path == 0 else s * 4 + sx
                start = start + jnp.where(s < inner, filled_ref[other], 0)
            rel = lax.rem(line - (y if path == 0 else x) + 4, 4)
            first = jnp.minimum(start, cap - MOST_M)
            found.append((rel, first, start - first))
        return found

    def each_copy(n, act):
        slot = lax.rem(n, 2)
        found = spots(n)
        for side in range(2):
            for path in range(2):
                rel, first, _ = found[path]
                at = side * 9 + path * 4
                there = hold.at[slot, side, path, pl.ds(0, MOST_M)]
                block = pl.ds(first, MOST_M)
                for ref, shift in zip(ins[at : at + 4 - path], RELS):
                    @pl.when(rel == shift)
                    def _():
                        act(
                            pltpu.make_async_copy(
                                ref.at[block, pl.ds(0, HALF)], there, sems.at[slot, side, path, 0]
                            )
                        )

                if path == 1:
                    @pl.when(rel == 2)
                    def _():
                        for part, ref in enumerate(ins[at + 3 : at + 5]):
                            act(
                                pltpu.make_async_copy(
                                    ref.at[block],
                                    there.at[:, pl.ds(part * QUARTER, QUARTER)],
                                    sems.at[slot, side, path, part],
                                )
                            )

    @pl.when(row == 0)
    def _():
        each_copy(jnp.int32(0), lambda c: c.start())

    @pl.when(row + 1 < ROWS)
    def _():
        each_copy(row + 1, lambda c: c.start())

    each_copy(row, lambda c: c.wait())
    slot = lax.rem(row, 2)
    found = spots(row)
    filled = meta_ref[ROWS + row]
    query = query_ref[0]
    draft = draft_scores(query, fresh_ref[0])
    best[...] = jnp.full((QS, 128), -jnp.inf, F32)
    for group in range(2):
        @pl.when(group * GROUP < filled)
        def _():
            for side in range(2):
                parts = []
                for path in range(2):
                    at = found[path][2] + group * GROUP
                    for i in range(GROUP):
                        block = hold[slot, side, path, at + i]
                        live = i + group * GROUP < filled
                        parts.append(jnp.where(live, block, jnp.zeros_like(block)))
                packed = jnp.concatenate(parts, axis=0)
                keys_ref[0, group, side * CHUNK : side * CHUNK + CHUNK] = jnp.dot(
                    table_ref[...], packed, preferred_element_type=F32
                ).astype(BF)
            raw = products(query, keys_ref[0, group]) + bias_row(group, filled)
            best[...] = jnp.maximum(best[...], fold(jnp.maximum, raw))
    cached = jnp.max(best[...], axis=1, keepdims=True) * score_scale
    peak = row_of(jnp.maximum(cached, jnp.max(draft, axis=1, keepdims=True)))
    top_ref[pl.ds(row, 1)] = peak[:1]


def keys_and_top(cap, meta, place, filled, table, queries, fresh, arrays):
    row = lambda *tail: pl.BlockSpec((1,) + tail, lambda i, *_: (i,) + (0,) * len(tail))
    return pl.pallas_call(
        functools.partial(keys_kernel, cap),
        out_shape=[
            jax.ShapeDtypeStruct((ROWS, 2, 2 * CHUNK, KV), BF),
            jax.ShapeDtypeStruct((ROWS, QS), F32),
        ],
        grid_spec=pltpu.PrefetchScalarGridSpec(
            num_scalar_prefetch=3,
            grid=(ROWS,),
            in_specs=[
                pl.BlockSpec((CHUNK, CHUNK), lambda i, *_: (0, 0)),
                row(QS, KV),
                row(QUARTER, KV),
            ]
            + [ANY] * 18,
            out_specs=[
                row(2, 2 * CHUNK, KV),
                pl.BlockSpec((ROWS, QS), lambda i, *_: (0, 0)),
            ],
            scratch_shapes=[
                pltpu.VMEM((2, 2, 2, 2 * MOST_M, HALF, KV), BF),
                pltpu.VMEM((QS, 128), F32),
                pltpu.SemaphoreType.DMA((2, 2, 2, 2)),
            ],
        ),
        compiler_params=pltpu.CompilerParams(vmem_limit_bytes=VMEM_LIMIT),
        name="keys",
    )(meta, place, filled, table, queries, fresh, *arrays)


def sums_kernel(places, meta_ref, order_ref, keys_ref, query_ref, fresh_ref, *refs):
    top_ref, outs, acc, total = refs[0], refs[1:-2], refs[-2], refs[-1]
    step = pl.program_id(0)
    row = order_ref[step]
    filled = meta_ref[ROWS + row]
    query = query_ref[0]
    peak = column_of(top_ref[pl.ds(row, 1)])
    for group in range(2):
        def add():
            keys = keys_ref[0, group]
            raw = products(query, keys) * score_scale + bias_row(group, filled)
            weights = jnp.exp(raw - jnp.concatenate([peak] * 4, axis=1))
            part = jnp.dot(weights.astype(BF), keys[:, :LAT], preferred_element_type=F32)
            if group == 0:
                total[...] = fold(jnp.add, weights)
                acc[...] = part
            else:
                total[...] += fold(jnp.add, weights)
                acc[...] += part

        if group == 0:
            add()
        else:
            pl.when(group * GROUP < filled)(add)

    if places[-1] == 0:
        @pl.when(step == len(places) - 1)
        def _():
            fresh = fresh_ref[0]
            weights = jnp.exp(draft_scores(query, fresh) - peak[:, :QUARTER])
            acc[...] += jnp.dot(weights.astype(BF), fresh[:, :LAT], preferred_element_type=F32)
            lane = lax.broadcasted_iota(I32, (QS, 128), 1)
            extra = jnp.sum(weights, axis=1, keepdims=True)
            total[...] += jnp.where(lane == 0, extra, 0.0)

    shares = row_of(jnp.sum(total[...], axis=1, keepdims=True))
    if len(places) == 1:
        cut = QS // 2
        outs[0][...] = acc[:cut]
        outs[1][:cut] = acc[cut:]
        outs[1][cut:, :QS] = shares
        outs[1][cut:, QS:] = jnp.zeros((RED - QS, LAT - QS), F32)
        return
    for i in range(len(places)):
        @pl.when(step == i)
        def _():
            outs[i][:QS] = acc[...]
            outs[i][QS:, :QS] = shares
            outs[i][QS:, QS:] = jnp.zeros((RED - QS, LAT - QS), F32)


def sums(places, grp, meta, keys, queries, fresh, top):
    count = len(places)
    heights = [QS // 2, RED - QS // 2] if count == 1 else [RED] * count
    order = (grp + jnp.array(places, I32)) % ROWS
    row = lambda *tail: pl.BlockSpec((1,) + tail, lambda i, m, o: (o[i],) + (0,) * len(tail))
    return pl.pallas_call(
        functools.partial(sums_kernel, places),
        out_shape=[jax.ShapeDtypeStruct((n, LAT), F32) for n in heights],
        grid_spec=pltpu.PrefetchScalarGridSpec(
            num_scalar_prefetch=2,
            grid=(count,),
            in_specs=[row(2, 2 * CHUNK, KV), row(QS, KV), row(QUARTER, KV)]
            + [pl.BlockSpec((ROWS, QS), lambda i, m, o: (0, 0))],
            out_specs=[pl.BlockSpec((n, LAT), lambda i, m, o: (0, 0)) for n in heights],
            scratch_shapes=[pltpu.VMEM((QS, LAT), F32), pltpu.VMEM((QS, 128), F32)],
        ),
        compiler_params=pltpu.CompilerParams(vmem_limit_bytes=VMEM_LIMIT),
        name="sums",
    )(meta, order, keys, queries, fresh, top)


def finish_kernel(a_ref, b_ref, c_ref, top_ref, bottom_ref):
    whole = a_ref[...] + (b_ref[...] + c_ref[...])
    total = jnp.transpose(jnp.broadcast_to(whole[QS : QS + 1, :QS], (128, QS)))
    total = jnp.concatenate([total] * 4, axis=1)
    out = (whole[:QS] / total).astype(BF)
    top_ref[...] = out[: QS // 2]
    bottom_ref[...] = out[QS // 2 :]


def finish(own, left, right):
    vmem = pl.BlockSpec(memory_space=pltpu.VMEM)
    return pl.pallas_call(
        finish_kernel,
        out_shape=[jax.ShapeDtypeStruct((QS // 2, LAT), BF)] * 2,
        in_specs=[vmem] * 3,
        out_specs=[vmem] * 2,
        compiler_params=pltpu.CompilerParams(vmem_limit_bytes=24 * 1024 * 1024),
        name="finish",
    )(own, left, right)


def place_kernel(grp_ref, *refs):
    ins, out_ref = refs[:16], refs[16]
    step = pl.program_id(0)
    for d in range(8):
        @pl.when(step == d)
        def _():
            out_ref[0, : QS // 2] = ins[2 * d][...]
            out_ref[0, QS // 2 :] = ins[2 * d + 1][...]


def put_in_place(grp, pieces):
    return pl.pallas_call(
        place_kernel,
        out_shape=jax.ShapeDtypeStruct((ROWS, QS, LAT), BF),
        grid_spec=pltpu.PrefetchScalarGridSpec(
            num_scalar_prefetch=1,
            grid=(ROWS,),
            in_specs=[pl.BlockSpec(memory_space=pltpu.VMEM)] * 16,
            out_specs=pl.BlockSpec((1, QS, LAT), lambda i, g: (lax.rem(g[0] + i, GRP), 0, 0)),
        ),
        compiler_params=pltpu.CompilerParams(vmem_limit_bytes=16 * 1024 * 1024),
        name="place",
    )(grp, *pieces)


def attention(cap, turn, grp, place, filled, meta, table, queries, fresh, arrays):
    keys, top = keys_and_top(cap, meta, place, filled, table, queries, fresh, arrays)

    every = jnp.broadcast_to(top[None], (GRP,) + top.shape)
    top = jnp.max(lax.all_to_all(every, "grp", 0, 0, tiled=True), axis=0)

    part = lambda *places: sums(places, grp, meta, keys, queries, fresh, top)
    far_top, far_bottom = part(4)
    up3, down3 = part(3, 5)
    up2, down2 = part(2, 6)
    up1, down1, own = part(1, 7, 0)

    cut = QS // 2
    up, down = turn(far_top, 1), turn(far_bottom, -1)
    up = turn(jnp.concatenate([up3[:cut] + up, up3[cut:]]), 1)
    down = turn(jnp.concatenate([down3[:cut], down3[cut:] + down]), -1)
    up, down = turn(up2 + up, 1), turn(down2 + down, -1)
    up, down = turn(up1 + up, 1), turn(down1 + down, -1)
    top_half, bottom_half = finish(own, up, down)

    got = [[top_half, bottom_half]] + [[None, None] for _ in range(7)]
    for d in (1, 2, 3):
        for h in range(2):
            got[8 - d][h] = turn(got[(9 - d) % 8][h], 1)
            got[d][h] = turn(got[d - 1][h], -1)
    got[4] = [turn(got[5][0], 1), turn(got[3][1], -1)]
    return [half for pieces in got for half in pieces]


def body(coeffs, lengths, owners, row_pick, queries, new_latent):
    stored = coeffs[0, 0, 0]
    pair = lax.axis_index("pair").astype(I32)
    grp = lax.axis_index("grp").astype(I32)
    place = jnp.stack([pair // 4, pair % 4])

    owner = owners[:, 0]
    flag_block, meta, filled = routes(pair[None], owner, lengths, row_pick)
    quarter = lambda i: stored[:, i * QUARTER : (i + 1) * QUARTER]
    flagged = lambda v: jnp.concatenate([v, flag_block], axis=0)
    a_lo, a_hi = flagged(quarter(0)), quarter(1)
    b_lo, b_hi = flagged(quarter(2)), quarter(3)

    send = lambda v, perm: lax.ppermute(v, "pair", perm)

    def gather_line(lo, hi, perm):
        from_prev = send(lo, perm(1)), send(hi, perm(1))
        from_next = send(lo, perm(-1)), send(hi, perm(-1))
        return (lo, hi) + from_next + from_prev, from_prev[0], from_next[1]

    line_a, a_prev_lo, a_next_hi = gather_line(a_lo, a_hi, x_perm)
    line_b, b_prev_lo, b_next_hi = gather_line(b_lo, b_hi, y_perm)

    named = owner.reshape(16, 4)[:, :, None] == jnp.arange(16, dtype=I32)[None, None, :]
    earlier = jnp.arange(4)[None, :] < jnp.arange(4)[:, None]
    offsets = jnp.sum(jnp.where(earlier[None], lengths[:, None, :], 0), axis=2)
    len_of = jnp.sum(jnp.where(named, lengths[:, :, None], 0), axis=1)
    off_of = jnp.sum(jnp.where(named, offsets[:, :, None], 0), axis=1)
    fresh = jnp.concatenate([new_latent, jnp.zeros((ROWS, QUARTER - STEPS, KV), BF)], axis=1)
    table = spread_table()

    a_prev_lo, b_prev_lo, place, len_of, off_of, fresh, table = (
        lax.optimization_barrier(
            (a_prev_lo, b_prev_lo, place, len_of, off_of, fresh, table)
        )
    )
    line_a = line_a + (send(a_prev_lo, x_perm(1)), send(a_next_hi, x_perm(-1)))
    line_b = line_b + (send(b_prev_lo, y_perm(1)), send(b_next_hi, y_perm(-1)))

    heard = lambda v: v[FLAG, 0, :17]
    told = jnp.stack([heard(v) for v in line_b[::2] + line_a[::2]])
    all_flags = told[:, :16].astype(I32)
    line_over = jnp.broadcast_to(jnp.max(told[4:, 16]), (QUARTER, KV))

    across = lambda v: lax.ppermute(v, "side", [(0, 1), (1, 0)])

    def exchange(cap):
        packed = pack(cap, place, all_flags, len_of, off_of, line_over, line_a + line_b)
        own, nxt, prv, opp = packed[:4]
        here = own, send(prv, y_perm(-1)), send(nxt, y_perm(1)), send(opp, y_perm(2))
        own, nxt, prv = packed[4:]
        prv, nxt = send(nxt, x_perm(1)), send(prv, x_perm(-1))
        here += own, nxt, prv, send(prv[:, HALF:], x_perm(1)), send(nxt[:, HALF:], x_perm(-1))
        return here + tuple(across(v) for v in here)

    arrays = exchange(USUAL_CAP)
    seen = overflow(line_over, arrays[1:4])
    turn = lambda v, shift: lax.ppermute(v, "grp", ring(shift))
    flat_queries = queries.reshape(ROWS, QS, KV)

    def attend(cap, arrays):
        return attention(
            cap, turn, grp, place, filled, meta, table, flat_queries, fresh, arrays
        )

    pieces = lax.cond(
        seen[0] > 0,
        lambda: attend(MOST_CAP, exchange(MOST_CAP)),
        lambda: attend(USUAL_CAP, arrays),
    )
    return put_in_place(grp[None], pieces).reshape(ROWS, STEPS, HEADS, LAT)


def solution(mesh):
    return jax.shard_map(
        body,
        mesh=mesh,
        in_specs=(
            P("pair", "side", "grp", None, None, None),
            P(),
            P(),
            P("pair"),
            P("pair", None, "side", None),
            P("pair", None, None),
        ),
        out_specs=P("pair", None, "side", None),
        check_vma=False,
    )
```

```python
import functools
import math

import jax
import jax.numpy as jnp
import numpy as np
from jax import lax
from jax.experimental import pallas as pl
from jax.experimental.pallas import tpu as pltpu
from jax.sharding import PartitionSpec as P

LAT = 512
KV = 576
BLK = 64
HALF = 32
QUARTER = 16
STEPS = 4
MOST_M = 8
STORE = 20
ROWS = 8
HEADS = 64
QS = STEPS * HEADS
SIDE_LEN = 4
MOST_CAP = SIDE_LEN * MOST_M
USUAL_CAP = 24
GRP = 8
GROUP = 4
CHUNK = GROUP * BLK
VMEM_LIMIT = 56 * 1024 * 1024
RED = QS + 8
FLAG = STORE

score_scale = 192.0 ** (-0.5)
BF = jnp.bfloat16
F32 = jnp.float32
I32 = jnp.int32
RELS = (0, 1, 3, 2)


def spread_table():
    frequency = np.arange(BLK, dtype=np.float64)[:, None]
    position = np.arange(BLK, dtype=np.float64)[None, :]
    factor = np.sqrt(np.where(frequency > 0, 2.0, 1.0) / BLK)
    table = factor * np.cos(math.pi * (2.0 * position + 1.0) * frequency / (2.0 * BLK))
    table = table.reshape(2, HALF, BLK)
    spread = np.einsum("bc,hft->bthcf", np.eye(GROUP), table).reshape(CHUNK, CHUNK)
    return jnp.asarray(spread, BF)


def x_perm(shift):
    return [(y * 4 + x, y * 4 + (x + shift) % 4) for y in range(4) for x in range(4)]


def y_perm(shift):
    return [(y * 4 + x, (y + shift) % 4 * 4 + x) for y in range(4) for x in range(4)]


def ring(shift):
    return [(i, (i + shift) % GRP) for i in range(GRP)]


def pick4(index, values):
    out = values[3]
    for i in (2, 1, 0):
        out = jnp.where(index == i, values[i], out)
    return out


ANY = pl.BlockSpec(memory_space=pl.ANY)


def routes_kernel(pair_ref, owner_ref, len_ref, pick_ref, flag_ref, meta_ref, filled_ref):
    pair = pair_ref[0]
    mine = [(owner_ref[r] == pair).astype(I32) for r in range(64)]
    owned = functools.reduce(lambda a, b: a + b, mine)
    wanted = [lax.rem(pick_ref[n], owned) for n in range(ROWS)]
    request = [jnp.int32(0)] * ROWS
    rank = jnp.int32(0)
    for r in range(64):
        for n in range(ROWS):
            request[n] = jnp.where((mine[r] == 1) & (rank == wanted[n]), r, request[n])
        rank = rank + mine[r]
    source = [request[n] // 4 for n in range(ROWS)]
    blocks = [len_ref[source[n], lax.rem(request[n], 4)] for n in range(ROWS)]
    for n in range(ROWS):
        meta_ref[n] = source[n]
        meta_ref[ROWS + n] = blocks[n]
    filled = []
    lane = lax.broadcasted_iota(I32, (QUARTER, KV), 1)
    told = jnp.zeros((QUARTER, KV), F32)
    for p in range(16):
        total = jnp.int32(0)
        for n in range(ROWS):
            total = jnp.where(source[n] == p, blocks[n], total)
        filled.append(total)
        filled_ref[p] = total
        told = told + jnp.where((lane == p) & (total > 0), 1.0, 0.0)
    most = jnp.int32(0)
    for i in range(4):
        most = jnp.maximum(most, sum(filled[4 * i + 1 : 4 * i + 4], filled[4 * i]))
        most = jnp.maximum(most, sum(filled[i + 4 :: 4], filled[i]))
    told = told + jnp.where((lane == 16) & (most > USUAL_CAP), 1.0, 0.0)
    flag_ref[0] = told.astype(BF)


def routes(pair, owner, lengths, row_pick):
    smem = pl.BlockSpec(memory_space=pltpu.SMEM)
    return pl.pallas_call(
        routes_kernel,
        out_shape=[
            jax.ShapeDtypeStruct((1, QUARTER, KV), BF),
            jax.ShapeDtypeStruct((2 * ROWS,), I32),
            jax.ShapeDtypeStruct((16,), I32),
        ],
        in_specs=[smem] * 4,
        out_specs=[pl.BlockSpec(memory_space=pltpu.VMEM), smem, smem],
        name="routes",
    )(pair, owner, lengths, row_pick)


def overflow_kernel(own_ref, *refs):
    ins, out_ref, hold, sems = refs[:3], refs[3], refs[4], refs[5]
    copies = [
        pltpu.make_async_copy(
            ref.at[USUAL_CAP, pl.ds(0, QUARTER), pl.ds(0, 128)], hold.at[i], sems.at[i]
        )
        for i, ref in enumerate(ins)
    ]
    for copy in copies:
        copy.start()
    for copy in copies:
        copy.wait()
    most = jnp.maximum(jnp.maximum(hold[0], hold[1]), jnp.maximum(hold[2], own_ref[:, :128]))
    out_ref[0] = jnp.max(most.astype(F32)).astype(I32)


def overflow(own, arrays):
    vmem = pl.BlockSpec(memory_space=pltpu.VMEM)
    return pl.pallas_call(
        overflow_kernel,
        out_shape=jax.ShapeDtypeStruct((1,), I32),
        in_specs=[vmem] + [ANY] * 3,
        out_specs=pl.BlockSpec(memory_space=pltpu.SMEM),
        scratch_shapes=[pltpu.VMEM((3, QUARTER, 128), BF), pltpu.SemaphoreType.DMA((3,))],
        name="overflow",
    )(own, *arrays)


def pack_kernel(cap, place_ref, flags_ref, len_ref, off_ref, over_ref, *refs):
    ins, outs = refs[:16], refs[16:24]
    y, x = place_ref[0], place_ref[1]
    low, high = pl.ds(0, QUARTER), pl.ds(QUARTER, QUARTER)
    for path in range(2):
        sources = ins[path * 8 : path * 8 + 8]
        for out in outs[path * 4 + 1 : path * 4 + 4]:
            out[cap, low] = over_ref[...]
        along, across = (x, y) if path == 0 else (y, x)
        for kd, shift in enumerate(RELS):
            there = lax.rem(across + shift, 4)
            dest = there * 4 + x if path == 0 else y * 4 + there
            counts, offsets, starts = [], [], []
            total = jnp.int32(0)
            for s in range(4):
                p = y * 4 + s if path == 0 else s * 4 + x
                n = flags_ref[path * 4 + kd, p] * len_ref[p, dest]
                counts.append(n)
                offsets.append(off_ref[p, dest])
                starts.append(total)
                total = total + n
            for ks, near in enumerate(RELS):
                s = lax.rem(along + near, 4)
                n, o, d = pick4(s, counts), pick4(s, offsets), pick4(s, starts)
                source_lo, source_hi = sources[2 * ks : 2 * ks + 2]

                def move(i, carry):
                    out = outs[path * 4 + kd]
                    out[d + i, low] = source_lo[o + i]
                    out[d + i, high] = source_hi[o + i]
                    return carry

                lax.fori_loop(0, jnp.minimum(n, jnp.maximum(cap - d, 0)), move, 0)


def pack(cap, place, flags, len_of, off_of, over, arrays):
    own = jax.ShapeDtypeStruct((cap, HALF, KV), BF)
    sent = jax.ShapeDtypeStruct((cap + 1, HALF, KV), BF)
    smem = pl.BlockSpec(memory_space=pltpu.SMEM)
    vmem = pl.BlockSpec(memory_space=pltpu.VMEM)
    return pl.pallas_call(
        functools.partial(pack_kernel, cap),
        out_shape=[own, sent, sent, sent] * 2,
        in_specs=[smem] * 4 + [vmem] * 17,
        out_specs=[vmem] * 8,
        compiler_params=pltpu.CompilerParams(vmem_limit_bytes=40 * 1024 * 1024),
        name="pack",
    )(place, flags, len_of, off_of, over, *arrays)


def column_of(row, width=128):
    return jnp.transpose(jnp.broadcast_to(row, (width, QS)))


def row_of(column):
    return jnp.transpose(jnp.broadcast_to(column, (QS, 128)))[:8]


def draft_scores(query, fresh):
    raw = (
        lax.dot_general(query, fresh, (((1,), (1,)), ((), ())), preferred_element_type=F32)
        * score_scale
    )
    step = lax.broadcasted_iota(I32, raw.shape, 0) // HEADS
    token = lax.broadcasted_iota(I32, raw.shape, 1)
    return jnp.where(token <= step, raw, -jnp.inf)


def bias_row(group, filled):
    token = lax.rem(lax.broadcasted_iota(I32, (1, 2 * CHUNK), 1), CHUNK)
    return jnp.where(token // BLK + group * GROUP < filled, 0.0, -jnp.inf)


def products(query, keys):
    return lax.dot_general(query, keys, (((1,), (1,)), ((), ())), preferred_element_type=F32)


def fold(op, wide):
    return op(op(wide[:, :128], wide[:, 128:256]), op(wide[:, 256:384], wide[:, 384:]))


def keys_kernel(cap, meta_ref, place_ref, filled_ref, table_ref, query_ref, fresh_ref, *refs):
    ins = refs[:16]
    keys_ref, top_ref, hold, best, sems = refs[16:]
    row = pl.program_id(0)
    y, x = place_ref[0], place_ref[1]

    def spots(n):
        p = meta_ref[n]
        sy, sx = p // 4, lax.rem(p, 4)
        found = []
        for path in range(2):
            line, inner = (sy, sx) if path == 0 else (sx, sy)
            start = jnp.int32(0)
            for s in range(3):
                other = sy * 4 + s if path == 0 else s * 4 + sx
                start = start + jnp.where(s < inner, filled_ref[other], 0)
            rel = lax.rem(line - (y if path == 0 else x) + 4, 4)
            first = jnp.minimum(start, cap - MOST_M)
            found.append((rel, first, start - first))
        return found

    def each_copy(n, act):
        slot = lax.rem(n, 2)
        found = spots(n)
        for side in range(2):
            for path in range(2):
                rel, first, _ = found[path]
                at = (side * 2 + path) * 4
                for ref, shift in zip(ins[at : at + 4], RELS):
                    @pl.when(rel == shift)
                    def _():
                        act(
                            pltpu.make_async_copy(
                                ref.at[pl.ds(first, MOST_M)],
                                hold.at[slot, side, path, pl.ds(0, MOST_M)],
                                sems.at[slot, side, path],
                            )
                        )

    @pl.when(row == 0)
    def _():
        each_copy(jnp.int32(0), lambda c: c.start())

    @pl.when(row + 1 < ROWS)
    def _():
        each_copy(row + 1, lambda c: c.start())

    each_copy(row, lambda c: c.wait())
    slot = lax.rem(row, 2)
    found = spots(row)
    filled = meta_ref[ROWS + row]
    query = query_ref[0]
    draft = draft_scores(query, fresh_ref[0])
    best[...] = jnp.full((QS, 128), -jnp.inf, F32)
    for group in range(2):
        @pl.when(group * GROUP < filled)
        def _():
            for side in range(2):
                parts = []
                for path in range(2):
                    at = found[path][2] + group * GROUP
                    for i in range(GROUP):
                        block = hold[slot, side, path, at + i]
                        live = i + group * GROUP < filled
                        parts.append(jnp.where(live, block, jnp.zeros_like(block)))
                packed = jnp.concatenate(parts, axis=0)
                keys_ref[0, group, side * CHUNK : side * CHUNK + CHUNK] = jnp.dot(
                    table_ref[...], packed, preferred_element_type=F32
                ).astype(BF)
            raw = products(query, keys_ref[0, group]) + bias_row(group, filled)
            best[...] = jnp.maximum(best[...], fold(jnp.maximum, raw))
    cached = jnp.max(best[...], axis=1, keepdims=True) * score_scale
    peak = row_of(jnp.maximum(cached, jnp.max(draft, axis=1, keepdims=True)))
    top_ref[pl.ds(row, 1)] = peak[:1]


def keys_and_top(cap, meta, place, filled, table, queries, fresh, arrays):
    row = lambda *tail: pl.BlockSpec((1,) + tail, lambda i, *_: (i,) + (0,) * len(tail))
    return pl.pallas_call(
        functools.partial(keys_kernel, cap),
        out_shape=[
            jax.ShapeDtypeStruct((ROWS, 2, 2 * CHUNK, KV), BF),
            jax.ShapeDtypeStruct((ROWS, QS), F32),
        ],
        grid_spec=pltpu.PrefetchScalarGridSpec(
            num_scalar_prefetch=3,
            grid=(ROWS,),
            in_specs=[
                pl.BlockSpec((CHUNK, CHUNK), lambda i, *_: (0, 0)),
                row(QS, KV),
                row(QUARTER, KV),
            ]
            + [ANY] * 16,
            out_specs=[
                row(2, 2 * CHUNK, KV),
                pl.BlockSpec((ROWS, QS), lambda i, *_: (0, 0)),
            ],
            scratch_shapes=[
                pltpu.VMEM((2, 2, 2, 2 * MOST_M, HALF, KV), BF),
                pltpu.VMEM((QS, 128), F32),
                pltpu.SemaphoreType.DMA((2, 2, 2)),
            ],
        ),
        compiler_params=pltpu.CompilerParams(vmem_limit_bytes=VMEM_LIMIT),
        name="keys",
    )(meta, place, filled, table, queries, fresh, *arrays)


def sums_kernel(places, meta_ref, order_ref, keys_ref, query_ref, fresh_ref, *refs):
    top_ref, outs, acc, total = refs[0], refs[1:-2], refs[-2], refs[-1]
    step = pl.program_id(0)
    row = order_ref[step]
    filled = meta_ref[ROWS + row]
    query = query_ref[0]
    peak = column_of(top_ref[pl.ds(row, 1)])
    for group in range(2):
        def add():
            keys = keys_ref[0, group]
            raw = products(query, keys) * score_scale + bias_row(group, filled)
            weights = jnp.exp(raw - jnp.concatenate([peak] * 4, axis=1))
            part = jnp.dot(weights.astype(BF), keys[:, :LAT], preferred_element_type=F32)
            if group == 0:
                total[...] = fold(jnp.add, weights)
                acc[...] = part
            else:
                total[...] += fold(jnp.add, weights)
                acc[...] += part

        if group == 0:
            add()
        else:
            pl.when(group * GROUP < filled)(add)

    if places[-1] == 0:
        @pl.when(step == len(places) - 1)
        def _():
            fresh = fresh_ref[0]
            weights = jnp.exp(draft_scores(query, fresh) - peak[:, :QUARTER])
            acc[...] += jnp.dot(weights.astype(BF), fresh[:, :LAT], preferred_element_type=F32)
            lane = lax.broadcasted_iota(I32, (QS, 128), 1)
            extra = jnp.sum(weights, axis=1, keepdims=True)
            total[...] += jnp.where(lane == 0, extra, 0.0)

    shares = row_of(jnp.sum(total[...], axis=1, keepdims=True))
    if len(places) == 1:
        cut = QS // 2
        outs[0][...] = acc[:cut]
        outs[1][:cut] = acc[cut:]
        outs[1][cut:, :QS] = shares
        outs[1][cut:, QS:] = jnp.zeros((RED - QS, LAT - QS), F32)
        return
    for i in range(len(places)):
        @pl.when(step == i)
        def _():
            outs[i][:QS] = acc[...]
            outs[i][QS:, :QS] = shares
            outs[i][QS:, QS:] = jnp.zeros((RED - QS, LAT - QS), F32)


def sums(places, grp, meta, keys, queries, fresh, top):
    count = len(places)
    heights = [QS // 2, RED - QS // 2] if count == 1 else [RED] * count
    order = (grp + jnp.array(places, I32)) % ROWS
    row = lambda *tail: pl.BlockSpec((1,) + tail, lambda i, m, o: (o[i],) + (0,) * len(tail))
    return pl.pallas_call(
        functools.partial(sums_kernel, places),
        out_shape=[jax.ShapeDtypeStruct((n, LAT), F32) for n in heights],
        grid_spec=pltpu.PrefetchScalarGridSpec(
            num_scalar_prefetch=2,
            grid=(count,),
            in_specs=[row(2, 2 * CHUNK, KV), row(QS, KV), row(QUARTER, KV)]
            + [pl.BlockSpec((ROWS, QS), lambda i, m, o: (0, 0))],
            out_specs=[pl.BlockSpec((n, LAT), lambda i, m, o: (0, 0)) for n in heights],
            scratch_shapes=[pltpu.VMEM((QS, LAT), F32), pltpu.VMEM((QS, 128), F32)],
        ),
        compiler_params=pltpu.CompilerParams(vmem_limit_bytes=VMEM_LIMIT),
        name="sums",
    )(meta, order, keys, queries, fresh, top)


def finish_kernel(a_ref, b_ref, c_ref, top_ref, bottom_ref):
    whole = a_ref[...] + (b_ref[...] + c_ref[...])
    total = jnp.transpose(jnp.broadcast_to(whole[QS : QS + 1, :QS], (128, QS)))
    total = jnp.concatenate([total] * 4, axis=1)
    out = (whole[:QS] / total).astype(BF)
    top_ref[...] = out[: QS // 2]
    bottom_ref[...] = out[QS // 2 :]


def finish(own, left, right):
    vmem = pl.BlockSpec(memory_space=pltpu.VMEM)
    return pl.pallas_call(
        finish_kernel,
        out_shape=[jax.ShapeDtypeStruct((QS // 2, LAT), BF)] * 2,
        in_specs=[vmem] * 3,
        out_specs=[vmem] * 2,
        compiler_params=pltpu.CompilerParams(vmem_limit_bytes=24 * 1024 * 1024),
        name="finish",
    )(own, left, right)


def place_kernel(grp_ref, *refs):
    ins, out_ref = refs[:16], refs[16]
    step = pl.program_id(0)
    for d in range(8):
        @pl.when(step == d)
        def _():
            out_ref[0, : QS // 2] = ins[2 * d][...]
            out_ref[0, QS // 2 :] = ins[2 * d + 1][...]


def put_in_place(grp, pieces):
    return pl.pallas_call(
        place_kernel,
        out_shape=jax.ShapeDtypeStruct((ROWS, QS, LAT), BF),
        grid_spec=pltpu.PrefetchScalarGridSpec(
            num_scalar_prefetch=1,
            grid=(ROWS,),
            in_specs=[pl.BlockSpec(memory_space=pltpu.VMEM)] * 16,
            out_specs=pl.BlockSpec((1, QS, LAT), lambda i, g: (lax.rem(g[0] + i, GRP), 0, 0)),
        ),
        compiler_params=pltpu.CompilerParams(vmem_limit_bytes=16 * 1024 * 1024),
        name="place",
    )(grp, *pieces)


def attention(cap, turn, grp, place, filled, meta, table, queries, fresh, arrays):
    keys, top = keys_and_top(cap, meta, place, filled, table, queries, fresh, arrays)

    every = jnp.broadcast_to(top[None], (GRP,) + top.shape)
    top = jnp.max(lax.all_to_all(every, "grp", 0, 0, tiled=True), axis=0)

    part = lambda *places: sums(places, grp, meta, keys, queries, fresh, top)
    far_top, far_bottom = part(4)
    up3, down3 = part(3, 5)
    up2, down2 = part(2, 6)
    up1, down1, own = part(1, 7, 0)

    cut = QS // 2
    up, down = turn(far_top, 1), turn(far_bottom, -1)
    up = turn(jnp.concatenate([up3[:cut] + up, up3[cut:]]), 1)
    down = turn(jnp.concatenate([down3[:cut], down3[cut:] + down]), -1)
    up, down = turn(up2 + up, 1), turn(down2 + down, -1)
    up, down = turn(up1 + up, 1), turn(down1 + down, -1)
    top_half, bottom_half = finish(own, up, down)

    got = [[top_half, bottom_half]] + [[None, None] for _ in range(7)]
    for d in (1, 2, 3):
        for h in range(2):
            got[8 - d][h] = turn(got[(9 - d) % 8][h], 1)
            got[d][h] = turn(got[d - 1][h], -1)
    got[4] = [turn(got[5][0], 1), turn(got[3][1], -1)]
    return put_in_place(grp[None], [half for pieces in got for half in pieces])


def body(coeffs, lengths, owners, row_pick, queries, new_latent):
    stored = coeffs[0, 0, 0]
    pair = lax.axis_index("pair").astype(I32)
    grp = lax.axis_index("grp").astype(I32)
    place = jnp.stack([pair // 4, pair % 4])

    owner = owners[:, 0]
    flag_block, meta, filled = routes(pair[None], owner, lengths, row_pick)
    quarter = lambda i: stored[:, i * QUARTER : (i + 1) * QUARTER]
    flagged = lambda v: jnp.concatenate([v, flag_block], axis=0)
    a_lo, a_hi = flagged(quarter(0)), quarter(1)
    b_lo, b_hi = flagged(quarter(2)), quarter(3)

    send = lambda v, perm: lax.ppermute(v, "pair", perm)

    def gather_line(lo, hi, perm):
        from_prev = send(lo, perm(1)), send(hi, perm(1))
        from_next = send(lo, perm(-1)), send(hi, perm(-1))
        return (lo, hi) + from_next + from_prev, from_prev[0], from_next[1]

    line_a, a_prev_lo, a_next_hi = gather_line(a_lo, a_hi, x_perm)
    line_b, b_prev_lo, b_next_hi = gather_line(b_lo, b_hi, y_perm)

    named = owner.reshape(16, 4)[:, :, None] == jnp.arange(16, dtype=I32)[None, None, :]
    earlier = jnp.arange(4)[None, :] < jnp.arange(4)[:, None]
    offsets = jnp.sum(jnp.where(earlier[None], lengths[:, None, :], 0), axis=2)
    len_of = jnp.sum(jnp.where(named, lengths[:, :, None], 0), axis=1)
    off_of = jnp.sum(jnp.where(named, offsets[:, :, None], 0), axis=1)
    fresh = jnp.concatenate([new_latent, jnp.zeros((ROWS, QUARTER - STEPS, KV), BF)], axis=1)
    table = spread_table()

    a_prev_lo, b_prev_lo, place, len_of, off_of, fresh, table = (
        lax.optimization_barrier(
            (a_prev_lo, b_prev_lo, place, len_of, off_of, fresh, table)
        )
    )
    line_a = line_a + (send(a_prev_lo, x_perm(1)), send(a_next_hi, x_perm(-1)))
    line_b = line_b + (send(b_prev_lo, y_perm(1)), send(b_next_hi, y_perm(-1)))

    heard = lambda v: v[FLAG, 0, :17]
    told = jnp.stack([heard(v) for v in line_b[::2] + line_a[::2]])
    all_flags = told[:, :16].astype(I32)
    line_over = jnp.broadcast_to(jnp.max(told[4:, 16]), (QUARTER, KV))

    across = lambda v: lax.ppermute(v, "side", [(0, 1), (1, 0)])

    def second_hop(own, nxt, prv, opp, perm):
        return own, send(prv, perm(-1)), send(nxt, perm(1)), send(opp, perm(2))

    def exchange(cap):
        packed = pack(cap, place, all_flags, len_of, off_of, line_over, line_a + line_b)
        here = second_hop(*packed[:4], y_perm) + second_hop(*packed[4:], x_perm)
        return here + tuple(across(v) for v in here)

    arrays = exchange(USUAL_CAP)
    seen = overflow(line_over, arrays[1:4])
    turn = lambda v, shift: lax.ppermute(v, "grp", ring(shift))
    flat_queries = queries.reshape(ROWS, QS, KV)

    def attend(cap, arrays):
        return attention(
            cap, turn, grp, place, filled, meta, table, flat_queries, fresh, arrays
        )

    out = lax.cond(
        seen[0] > 0,
        lambda: attend(MOST_CAP, exchange(MOST_CAP)),
        lambda: attend(USUAL_CAP, arrays),
    )
    return out.reshape(ROWS, STEPS, HEADS, LAT)


def solution(mesh):
    return jax.shard_map(
        body,
        mesh=mesh,
        in_specs=(
            P("pair", "side", "grp", None, None, None),
            P(),
            P(),
            P("pair"),
            P("pair", None, "side", None),
            P("pair", None, None),
        ),
        out_specs=P("pair", None, "side", None),
        check_vma=False,
    )
```

```python
import functools
import math

import jax
import jax.numpy as jnp
import numpy as np
from jax import lax
from jax.experimental import pallas as pl
from jax.experimental.pallas import tpu as pltpu
from jax.sharding import PartitionSpec as P

LAT = 512
KV = 576
BLK = 64
HALF = 32
QUARTER = 16
STEPS = 4
MOST_M = 8
STORE = 20
ROWS = 8
HEADS = 64
QS = STEPS * HEADS
SIDE_LEN = 4
MOST_CAP = SIDE_LEN * MOST_M
USUAL_CAP = 24
GRP = 8
GROUP = 4
CHUNK = GROUP * BLK
VMEM_LIMIT = 56 * 1024 * 1024
RED = QS + 8
FLAG = STORE
FOLD = HALF * KV // 128
SPLIT = 10

score_scale = 192.0 ** (-0.5)
BF = jnp.bfloat16
F32 = jnp.float32
I32 = jnp.int32
RELS = (0, 1, 3, 2)


def spread_table():
    frequency = np.arange(BLK, dtype=np.float64)[:, None]
    position = np.arange(BLK, dtype=np.float64)[None, :]
    factor = np.sqrt(np.where(frequency > 0, 2.0, 1.0) / BLK)
    table = factor * np.cos(math.pi * (2.0 * position + 1.0) * frequency / (2.0 * BLK))
    table = table.reshape(2, HALF, BLK)
    spread = np.einsum("bc,hft->bthcf", np.eye(GROUP), table).reshape(CHUNK, CHUNK)
    return jnp.asarray(spread, BF)


def x_perm(shift):
    return [(y * 4 + x, y * 4 + (x + shift) % 4) for y in range(4) for x in range(4)]


def y_perm(shift):
    return [(y * 4 + x, (y + shift) % 4 * 4 + x) for y in range(4) for x in range(4)]


def ring(shift):
    return [(i, (i + shift) % GRP) for i in range(GRP)]


def pick4(index, values):
    out = values[3]
    for i in (2, 1, 0):
        out = jnp.where(index == i, values[i], out)
    return out


ANY = pl.BlockSpec(memory_space=pl.ANY)


def routes_kernel(pair_ref, owner_ref, len_ref, pick_ref, stored_ref, low_ref, high_ref, meta_ref, filled_ref):
    pair = pair_ref[0]
    mine = [(owner_ref[r] == pair).astype(I32) for r in range(64)]
    owned = functools.reduce(lambda a, b: a + b, mine)
    wanted = [lax.rem(pick_ref[n], owned) for n in range(ROWS)]
    request = [jnp.int32(0)] * ROWS
    rank = jnp.int32(0)
    for r in range(64):
        for n in range(ROWS):
            request[n] = jnp.where((mine[r] == 1) & (rank == wanted[n]), r, request[n])
        rank = rank + mine[r]
    source = [request[n] // 4 for n in range(ROWS)]
    blocks = [len_ref[source[n], lax.rem(request[n], 4)] for n in range(ROWS)]
    for n in range(ROWS):
        meta_ref[n] = source[n]
        meta_ref[ROWS + n] = blocks[n]
    filled = []
    lane = lax.broadcasted_iota(I32, (QUARTER, 128), 1)
    told = jnp.zeros((QUARTER, 128), F32)
    for p in range(16):
        total = jnp.int32(0)
        for n in range(ROWS):
            total = jnp.where(source[n] == p, blocks[n], total)
        filled.append(total)
        filled_ref[p] = total
        told = told + jnp.where((lane == p) & (total > 0), 1.0, 0.0)
    most = jnp.int32(0)
    for i in range(4):
        most = jnp.maximum(most, sum(filled[4 * i + 1 : 4 * i + 4], filled[4 * i]))
        most = jnp.maximum(most, sum(filled[i + 4 :: 4], filled[i]))
    told = told + jnp.where((lane == 16) & (most > USUAL_CAP), 1.0, 0.0)
    for half, out in enumerate((low_ref, high_ref)):
        out[FLAG] = jnp.zeros((FOLD, 128), BF)
        out[FLAG, :QUARTER] = told.astype(BF)

        def fold_block(i, carry):
            rows = stored_ref[i, half * HALF : half * HALF + HALF]
            for k in range(4):
                out[i, k * HALF : k * HALF + HALF] = rows[:, k * 128 : k * 128 + 128]
            rest = rows[:, LAT:]
            out[i, 4 * HALF :] = jnp.concatenate([rest[:QUARTER], rest[QUARTER:]], axis=1)
            return carry

        lax.fori_loop(0, STORE, fold_block, 0)


def routes(pair, owner, lengths, row_pick, stored):
    smem = pl.BlockSpec(memory_space=pltpu.SMEM)
    vmem = pl.BlockSpec(memory_space=pltpu.VMEM)
    return pl.pallas_call(
        routes_kernel,
        out_shape=[
            jax.ShapeDtypeStruct((STORE + 1, FOLD, 128), BF),
            jax.ShapeDtypeStruct((STORE + 1, FOLD, 128), BF),
            jax.ShapeDtypeStruct((2 * ROWS,), I32),
            jax.ShapeDtypeStruct((16,), I32),
        ],
        in_specs=[smem] * 4 + [vmem],
        out_specs=[vmem, vmem, smem, smem],
        compiler_params=pltpu.CompilerParams(vmem_limit_bytes=16 * 1024 * 1024),
        name="routes",
    )(pair, owner, lengths, row_pick, stored)


def overflow_kernel(own_ref, *refs):
    ins, out_ref, hold, sems = refs[:3], refs[3], refs[4], refs[5]
    copies = [
        pltpu.make_async_copy(
            ref.at[USUAL_CAP, pl.ds(0, QUARTER), pl.ds(0, 128)], hold.at[i], sems.at[i]
        )
        for i, ref in enumerate(ins)
    ]
    for copy in copies:
        copy.start()
    for copy in copies:
        copy.wait()
    most = jnp.maximum(jnp.maximum(hold[0], hold[1]), jnp.maximum(hold[2], own_ref[...]))
    out_ref[0] = jnp.max(most.astype(F32)).astype(I32)


def overflow(own, arrays):
    vmem = pl.BlockSpec(memory_space=pltpu.VMEM)
    return pl.pallas_call(
        overflow_kernel,
        out_shape=jax.ShapeDtypeStruct((1,), I32),
        in_specs=[vmem] + [ANY] * 3,
        out_specs=pl.BlockSpec(memory_space=pltpu.SMEM),
        scratch_shapes=[pltpu.VMEM((3, QUARTER, 128), BF), pltpu.SemaphoreType.DMA((3,))],
        name="overflow",
    )(own, *arrays)


def pack_kernel(cap, place_ref, flags_ref, len_ref, off_ref, over_ref, *refs):
    ins, outs = refs[:10], refs[10:18]
    y, x = place_ref[0], place_ref[1]
    for path in range(2):
        sources = ins[path * 5 : path * 5 + 5]
        for out in outs[path * 4 + 1 : path * 4 + 4]:
            out[cap, :QUARTER] = over_ref[...]
        along, across = (x, y) if path == 0 else (y, x)
        for kd, shift in enumerate(RELS):
            there = lax.rem(across + shift, 4)
            dest = there * 4 + x if path == 0 else y * 4 + there
            counts, offsets, starts = [], [], []
            total = jnp.int32(0)
            for s in range(4):
                p = y * 4 + s if path == 0 else s * 4 + x
                n = flags_ref[path * 4 + kd, p] * len_ref[p, dest]
                counts.append(n)
                offsets.append(off_ref[p, dest])
                starts.append(total)
                total = total + n
            for ks, near in enumerate(RELS):
                s = lax.rem(along + near, 4)
                n, o, d = pick4(s, counts), pick4(s, offsets), pick4(s, starts)
                n = jnp.minimum(n, jnp.maximum(cap - d, 0))

                def move_from(source, shift):
                    def move(i, carry):
                        outs[path * 4 + kd][d + i] = source[o + i - shift]
                        return carry

                    return move

                if ks < 3:
                    lax.fori_loop(0, n, move_from(sources[ks], 0), 0)
                else:
                    early = jnp.clip(SPLIT + 1 - o, 0, n)
                    lax.fori_loop(0, early, move_from(sources[3], 0), 0)
                    lax.fori_loop(early, n, move_from(sources[4], SPLIT), 0)


def pack(cap, place, flags, len_of, off_of, over, arrays):
    own = jax.ShapeDtypeStruct((cap, FOLD, 128), BF)
    sent = jax.ShapeDtypeStruct((cap + 1, FOLD, 128), BF)
    smem = pl.BlockSpec(memory_space=pltpu.SMEM)
    vmem = pl.BlockSpec(memory_space=pltpu.VMEM)
    return pl.pallas_call(
        functools.partial(pack_kernel, cap),
        out_shape=[own, sent, sent, sent] * 2,
        in_specs=[smem] * 4 + [vmem] * 11,
        out_specs=[vmem] * 8,
        compiler_params=pltpu.CompilerParams(vmem_limit_bytes=40 * 1024 * 1024),
        name="pack",
    )(place, flags, len_of, off_of, over, *arrays)


def column_of(row, width=128):
    return jnp.transpose(jnp.broadcast_to(row, (width, QS)))


def row_of(column):
    return jnp.transpose(jnp.broadcast_to(column, (QS, 128)))[:8]


def draft_scores(query, fresh):
    raw = (
        lax.dot_general(query, fresh, (((1,), (1,)), ((), ())), preferred_element_type=F32)
        * score_scale
    )
    step = lax.broadcasted_iota(I32, raw.shape, 0) // HEADS
    token = lax.broadcasted_iota(I32, raw.shape, 1)
    return jnp.where(token <= step, raw, -jnp.inf)


def bias_row(group, filled):
    token = lax.rem(lax.broadcasted_iota(I32, (1, 2 * CHUNK), 1), CHUNK)
    return jnp.where(token // BLK + group * GROUP < filled, 0.0, -jnp.inf)


def products(query, keys):
    return lax.dot_general(query, keys, (((1,), (1,)), ((), ())), preferred_element_type=F32)


def fold(op, wide):
    return op(op(wide[:, :128], wide[:, 128:256]), op(wide[:, 256:384], wide[:, 384:]))


def unfold(folded):
    tiles = [folded[k * HALF : k * HALF + HALF] for k in range(4)]
    rest = folded[4 * HALF :]
    rest = jnp.concatenate([rest[:, :64], rest[:, 64:]], axis=0)
    return jnp.concatenate(tiles + [rest], axis=1)


def keys_kernel(cap, meta_ref, place_ref, filled_ref, table_ref, query_ref, fresh_ref, *refs):
    ins = refs[:16]
    keys_ref, top_ref, hold, best, sems = refs[16:]
    row = pl.program_id(0)
    y, x = place_ref[0], place_ref[1]

    def spots(n):
        p = meta_ref[n]
        sy, sx = p // 4, lax.rem(p, 4)
        found = []
        for path in range(2):
            line, inner = (sy, sx) if path == 0 else (sx, sy)
            start = jnp.int32(0)
            for s in range(3):
                other = sy * 4 + s if path == 0 else s * 4 + sx
                start = start + jnp.where(s < inner, filled_ref[other], 0)
            rel = lax.rem(line - (y if path == 0 else x) + 4, 4)
            first = jnp.minimum(start, cap - MOST_M)
            found.append((rel, first, start - first))
        return found

    def each_copy(n, act):
        slot = lax.rem(n, 2)
        found = spots(n)
        for side in range(2):
            for path in range(2):
                rel, first, _ = found[path]
                at = (side * 2 + path) * 4
                for ref, shift in zip(ins[at : at + 4], RELS):
                    @pl.when(rel == shift)
                    def _():
                        act(
                            pltpu.make_async_copy(
                                ref.at[pl.ds(first, MOST_M)],
                                hold.at[slot, side, path, pl.ds(0, MOST_M)],
                                sems.at[slot, side, path],
                            )
                        )

    @pl.when(row == 0)
    def _():
        each_copy(jnp.int32(0), lambda c: c.start())

    @pl.when(row + 1 < ROWS)
    def _():
        each_copy(row + 1, lambda c: c.start())

    each_copy(row, lambda c: c.wait())
    slot = lax.rem(row, 2)
    found = spots(row)
    filled = meta_ref[ROWS + row]
    query = query_ref[0]
    draft = draft_scores(query, fresh_ref[0])
    best[...] = jnp.full((QS, 128), -jnp.inf, F32)
    for group in range(2):
        @pl.when(group * GROUP < filled)
        def _():
            for side in range(2):
                parts = []
                for path in range(2):
                    at = found[path][2] + group * GROUP
                    for i in range(GROUP):
                        block = unfold(hold[slot, side, path, at + i])
                        live = i + group * GROUP < filled
                        parts.append(jnp.where(live, block, jnp.zeros_like(block)))
                packed = jnp.concatenate(parts, axis=0)
                keys_ref[0, group, side * CHUNK : side * CHUNK + CHUNK] = jnp.dot(
                    table_ref[...], packed, preferred_element_type=F32
                ).astype(BF)
            raw = products(query, keys_ref[0, group]) + bias_row(group, filled)
            best[...] = jnp.maximum(best[...], fold(jnp.maximum, raw))
    cached = jnp.max(best[...], axis=1, keepdims=True) * score_scale
    peak = row_of(jnp.maximum(cached, jnp.max(draft, axis=1, keepdims=True)))
    top_ref[pl.ds(row, 1)] = peak[:1]


def keys_and_top(cap, meta, place, filled, table, queries, fresh, arrays):
    row = lambda *tail: pl.BlockSpec((1,) + tail, lambda i, *_: (i,) + (0,) * len(tail))
    return pl.pallas_call(
        functools.partial(keys_kernel, cap),
        out_shape=[
            jax.ShapeDtypeStruct((ROWS, 2, 2 * CHUNK, KV), BF),
            jax.ShapeDtypeStruct((ROWS, QS), F32),
        ],
        grid_spec=pltpu.PrefetchScalarGridSpec(
            num_scalar_prefetch=3,
            grid=(ROWS,),
            in_specs=[
                pl.BlockSpec((CHUNK, CHUNK), lambda i, *_: (0, 0)),
                row(QS, KV),
                row(QUARTER, KV),
            ]
            + [ANY] * 16,
            out_specs=[
                row(2, 2 * CHUNK, KV),
                pl.BlockSpec((ROWS, QS), lambda i, *_: (0, 0)),
            ],
            scratch_shapes=[
                pltpu.VMEM((2, 2, 2, 2 * MOST_M, FOLD, 128), BF),
                pltpu.VMEM((QS, 128), F32),
                pltpu.SemaphoreType.DMA((2, 2, 2)),
            ],
        ),
        compiler_params=pltpu.CompilerParams(vmem_limit_bytes=VMEM_LIMIT),
        name="keys",
    )(meta, place, filled, table, queries, fresh, *arrays)


def sums_kernel(places, meta_ref, order_ref, keys_ref, query_ref, fresh_ref, *refs):
    top_ref, outs, acc, total = refs[0], refs[1:-2], refs[-2], refs[-1]
    step = pl.program_id(0)
    row = order_ref[step]
    filled = meta_ref[ROWS + row]
    query = query_ref[0]
    peak = column_of(top_ref[pl.ds(row, 1)])
    for group in range(2):
        def add():
            keys = keys_ref[0, group]
            raw = products(query, keys) * score_scale + bias_row(group, filled)
            weights = jnp.exp(raw - jnp.concatenate([peak] * 4, axis=1))
            part = jnp.dot(weights.astype(BF), keys[:, :LAT], preferred_element_type=F32)
            if group == 0:
                total[...] = fold(jnp.add, weights)
                acc[...] = part
            else:
                total[...] += fold(jnp.add, weights)
                acc[...] += part

        if group == 0:
            add()
        else:
            pl.when(group * GROUP < filled)(add)

    if places[-1] == 0:
        @pl.when(step == len(places) - 1)
        def _():
            fresh = fresh_ref[0]
            weights = jnp.exp(draft_scores(query, fresh) - peak[:, :QUARTER])
            acc[...] += jnp.dot(weights.astype(BF), fresh[:, :LAT], preferred_element_type=F32)
            lane = lax.broadcasted_iota(I32, (QS, 128), 1)
            extra = jnp.sum(weights, axis=1, keepdims=True)
            total[...] += jnp.where(lane == 0, extra, 0.0)

    shares = row_of(jnp.sum(total[...], axis=1, keepdims=True))
    if len(places) == 1:
        cut = QS // 2
        outs[0][...] = acc[:cut]
        outs[1][:cut] = acc[cut:]
        outs[1][cut:, :QS] = shares
        outs[1][cut:, QS:] = jnp.zeros((RED - QS, LAT - QS), F32)
        return
    for i in range(len(places)):
        @pl.when(step == i)
        def _():
            outs[i][:QS] = acc[...]
            outs[i][QS:, :QS] = shares
            outs[i][QS:, QS:] = jnp.zeros((RED - QS, LAT - QS), F32)


def sums(places, grp, meta, keys, queries, fresh, top):
    count = len(places)
    heights = [QS // 2, RED - QS // 2] if count == 1 else [RED] * count
    order = (grp + jnp.array(places, I32)) % ROWS
    row = lambda *tail: pl.BlockSpec((1,) + tail, lambda i, m, o: (o[i],) + (0,) * len(tail))
    return pl.pallas_call(
        functools.partial(sums_kernel, places),
        out_shape=[jax.ShapeDtypeStruct((n, LAT), F32) for n in heights],
        grid_spec=pltpu.PrefetchScalarGridSpec(
            num_scalar_prefetch=2,
            grid=(count,),
            in_specs=[row(2, 2 * CHUNK, KV), row(QS, KV), row(QUARTER, KV)]
            + [pl.BlockSpec((ROWS, QS), lambda i, m, o: (0, 0))],
            out_specs=[pl.BlockSpec((n, LAT), lambda i, m, o: (0, 0)) for n in heights],
            scratch_shapes=[pltpu.VMEM((QS, LAT), F32), pltpu.VMEM((QS, 128), F32)],
        ),
        compiler_params=pltpu.CompilerParams(vmem_limit_bytes=VMEM_LIMIT),
        name="sums",
    )(meta, order, keys, queries, fresh, top)


def finish_kernel(a_ref, b_ref, c_ref, top_ref, bottom_ref):
    whole = a_ref[...] + (b_ref[...] + c_ref[...])
    total = jnp.transpose(jnp.broadcast_to(whole[QS : QS + 1, :QS], (128, QS)))
    total = jnp.concatenate([total] * 4, axis=1)
    out = (whole[:QS] / total).astype(BF)
    top_ref[...] = out[: QS // 2]
    bottom_ref[...] = out[QS // 2 :]


def finish(own, left, right):
    vmem = pl.BlockSpec(memory_space=pltpu.VMEM)
    return pl.pallas_call(
        finish_kernel,
        out_shape=[jax.ShapeDtypeStruct((QS // 2, LAT), BF)] * 2,
        in_specs=[vmem] * 3,
        out_specs=[vmem] * 2,
        compiler_params=pltpu.CompilerParams(vmem_limit_bytes=24 * 1024 * 1024),
        name="finish",
    )(own, left, right)


def place_kernel(grp_ref, *refs):
    ins, out_ref = refs[:16], refs[16]
    step = pl.program_id(0)
    for d in range(8):
        @pl.when(step == d)
        def _():
            out_ref[0, : QS // 2] = ins[2 * d][...]
            out_ref[0, QS // 2 :] = ins[2 * d + 1][...]


def put_in_place(grp, pieces):
    return pl.pallas_call(
        place_kernel,
        out_shape=jax.ShapeDtypeStruct((ROWS, QS, LAT), BF),
        grid_spec=pltpu.PrefetchScalarGridSpec(
            num_scalar_prefetch=1,
            grid=(ROWS,),
            in_specs=[pl.BlockSpec(memory_space=pltpu.VMEM)] * 16,
            out_specs=pl.BlockSpec((1, QS, LAT), lambda i, g: (lax.rem(g[0] + i, GRP), 0, 0)),
        ),
        compiler_params=pltpu.CompilerParams(vmem_limit_bytes=16 * 1024 * 1024),
        name="place",
    )(grp, *pieces)


def attention(cap, turn, grp, place, filled, meta, table, queries, fresh, arrays):
    keys, top = keys_and_top(cap, meta, place, filled, table, queries, fresh, arrays)

    every = jnp.broadcast_to(top[None], (GRP,) + top.shape)
    top = jnp.max(lax.all_to_all(every, "grp", 0, 0, tiled=True), axis=0)

    part = lambda *places: sums(places, grp, meta, keys, queries, fresh, top)
    far_top, far_bottom = part(4)
    up3, down3 = part(3, 5)
    up2, down2 = part(2, 6)
    up1, down1, own = part(1, 7, 0)

    cut = QS // 2
    up, down = turn(far_top, 1), turn(far_bottom, -1)
    up = turn(jnp.concatenate([up3[:cut] + up, up3[cut:]]), 1)
    down = turn(jnp.concatenate([down3[:cut], down3[cut:] + down]), -1)
    up, down = turn(up2 + up, 1), turn(down2 + down, -1)
    up, down = turn(up1 + up, 1), turn(down1 + down, -1)
    top_half, bottom_half = finish(own, up, down)

    got = [[top_half, bottom_half]] + [[None, None] for _ in range(7)]
    for d in (1, 2, 3):
        for h in range(2):
            got[8 - d][h] = turn(got[(9 - d) % 8][h], 1)
            got[d][h] = turn(got[d - 1][h], -1)
    got[4] = [turn(got[5][0], 1), turn(got[3][1], -1)]
    return put_in_place(grp[None], [half for pieces in got for half in pieces])


def body(coeffs, lengths, owners, row_pick, queries, new_latent):
    stored = coeffs[0, 0, 0]
    pair = lax.axis_index("pair").astype(I32)
    grp = lax.axis_index("grp").astype(I32)
    place = jnp.stack([pair // 4, pair % 4])

    owner = owners[:, 0]
    a_own, b_own, meta, filled = routes(pair[None], owner, lengths, row_pick, stored)

    send = lambda v, perm: lax.ppermute(v, "pair", perm)
    a_prev, a_next = send(a_own, x_perm(1)), send(a_own, x_perm(-1))
    b_prev, b_next = send(b_own, y_perm(1)), send(b_own, y_perm(-1))

    named = owner.reshape(16, 4)[:, :, None] == jnp.arange(16, dtype=I32)[None, None, :]
    earlier = jnp.arange(4)[None, :] < jnp.arange(4)[:, None]
    offsets = jnp.sum(jnp.where(earlier[None], lengths[:, None, :], 0), axis=2)
    len_of = jnp.sum(jnp.where(named, lengths[:, :, None], 0), axis=1)
    off_of = jnp.sum(jnp.where(named, offsets[:, :, None], 0), axis=1)
    fresh = jnp.concatenate([new_latent, jnp.zeros((ROWS, QUARTER - STEPS, KV), BF)], axis=1)
    table = spread_table()

    a_prev, b_prev, place, len_of, off_of, fresh, table = (
        lax.optimization_barrier(
            (a_prev, b_prev, place, len_of, off_of, fresh, table)
        )
    )

    def relay(prv, nxt, perm):
        return send(prv[: SPLIT + 1], perm(1)), send(nxt[SPLIT:], perm(-1))

    line_a = (a_own, a_next, a_prev) + relay(a_prev, a_next, x_perm)
    line_b = (b_own, b_next, b_prev) + relay(b_prev, b_next, y_perm)

    heard = lambda v: [w[FLAG, 0, :17] for w in v[:3]] + [v[4][FLAG - SPLIT, 0, :17]]
    told = jnp.stack(heard(line_b) + heard(line_a))
    all_flags = told[:, :16].astype(I32)
    line_over = jnp.broadcast_to(jnp.max(told[4:, 16]), (QUARTER, 128))

    across = lambda v: lax.ppermute(v, "side", [(0, 1), (1, 0)])

    def second_hop(own, nxt, prv, opp, perm):
        return own, send(prv, perm(-1)), send(nxt, perm(1)), send(opp, perm(2))

    def exchange(cap):
        packed = pack(cap, place, all_flags, len_of, off_of, line_over, line_a + line_b)
        here = second_hop(*packed[:4], y_perm) + second_hop(*packed[4:], x_perm)
        return here + tuple(across(v) for v in here)

    arrays = exchange(USUAL_CAP)
    seen = overflow(line_over, arrays[1:4])
    turn = lambda v, shift: lax.ppermute(v, "grp", ring(shift))
    flat_queries = queries.reshape(ROWS, QS, KV)

    def attend(cap, arrays):
        return attention(
            cap, turn, grp, place, filled, meta, table, flat_queries, fresh, arrays
        )

    out = lax.cond(
        seen[0] > 0,
        lambda: attend(MOST_CAP, exchange(MOST_CAP)),
        lambda: attend(USUAL_CAP, arrays),
    )
    return out.reshape(ROWS, STEPS, HEADS, LAT)


def solution(mesh):
    return jax.shard_map(
        body,
        mesh=mesh,
        in_specs=(
            P("pair", "side", "grp", None, None, None),
            P(),
            P(),
            P("pair"),
            P("pair", None, "side", None),
            P("pair", None, None),
        ),
        out_specs=P("pair", None, "side", None),
        check_vma=False,
    )
```

```python
import functools
import math

import jax
import jax.numpy as jnp
import numpy as np
from jax import lax
from jax.experimental import pallas as pl
from jax.experimental.pallas import tpu as pltpu
from jax.sharding import PartitionSpec as P

LAT = 512
KV = 576
BLK = 64
HALF = 32
QUARTER = 16
STEPS = 4
MOST_M = 8
STORE = 20
ROWS = 8
HEADS = 64
QS = STEPS * HEADS
SIDE_LEN = 4
MOST_CAP = SIDE_LEN * MOST_M
USUAL_CAP = 24
GRP = 8
GROUP = 4
CHUNK = GROUP * BLK
VMEM_LIMIT = 56 * 1024 * 1024
RED = QS + 8
FLAG = STORE
FOLD = HALF * KV // 128
SPLIT = 10

score_scale = 192.0 ** (-0.5)
BF = jnp.bfloat16
F32 = jnp.float32
I32 = jnp.int32
RELS = (0, 1, 3, 2)


def spread_table():
    frequency = np.arange(BLK, dtype=np.float64)[:, None]
    position = np.arange(BLK, dtype=np.float64)[None, :]
    factor = np.sqrt(np.where(frequency > 0, 2.0, 1.0) / BLK)
    table = factor * np.cos(math.pi * (2.0 * position + 1.0) * frequency / (2.0 * BLK))
    table = table.reshape(2, HALF, BLK)
    spread = np.einsum("bc,hft->bthcf", np.eye(GROUP), table).reshape(CHUNK, CHUNK)
    return jnp.asarray(spread, BF)


def x_perm(shift):
    return [(y * 4 + x, y * 4 + (x + shift) % 4) for y in range(4) for x in range(4)]


def y_perm(shift):
    return [(y * 4 + x, (y + shift) % 4 * 4 + x) for y in range(4) for x in range(4)]


def ring(shift):
    return [(i, (i + shift) % GRP) for i in range(GRP)]


def pick4(index, values):
    out = values[3]
    for i in (2, 1, 0):
        out = jnp.where(index == i, values[i], out)
    return out


ANY = pl.BlockSpec(memory_space=pl.ANY)


def routes_kernel(pair_ref, owner_ref, len_ref, pick_ref, stored_ref, low_ref, high_ref, meta_ref, filled_ref):
    pair = pair_ref[0]
    mine = [(owner_ref[r] == pair).astype(I32) for r in range(64)]
    owned = functools.reduce(lambda a, b: a + b, mine)
    wanted = [lax.rem(pick_ref[n], owned) for n in range(ROWS)]
    request = [jnp.int32(0)] * ROWS
    rank = jnp.int32(0)
    for r in range(64):
        for n in range(ROWS):
            request[n] = jnp.where((mine[r] == 1) & (rank == wanted[n]), r, request[n])
        rank = rank + mine[r]
    source = [request[n] // 4 for n in range(ROWS)]
    blocks = [len_ref[source[n], lax.rem(request[n], 4)] for n in range(ROWS)]
    for n in range(ROWS):
        meta_ref[n] = source[n]
        meta_ref[ROWS + n] = blocks[n]
    filled = []
    lane = lax.broadcasted_iota(I32, (QUARTER, 128), 1)
    told = jnp.zeros((QUARTER, 128), F32)
    for p in range(16):
        total = jnp.int32(0)
        for n in range(ROWS):
            total = jnp.where(source[n] == p, blocks[n], total)
        filled.append(total)
        filled_ref[p] = total
        told = told + jnp.where((lane == p) & (total > 0), 1.0, 0.0)
    most = jnp.int32(0)
    for i in range(4):
        most = jnp.maximum(most, sum(filled[4 * i + 1 : 4 * i + 4], filled[4 * i]))
        most = jnp.maximum(most, sum(filled[i + 4 :: 4], filled[i]))
    told = told + jnp.where((lane == 16) & (most > USUAL_CAP), 1.0, 0.0)
    for half, out in enumerate((low_ref, high_ref)):
        out[FLAG] = jnp.zeros((FOLD, 128), BF)
        out[FLAG, :QUARTER] = told.astype(BF)

        def fold_block(i, carry):
            rows = stored_ref[i, half * HALF : half * HALF + HALF]
            for k in range(4):
                out[i, k * HALF : k * HALF + HALF] = rows[:, k * 128 : k * 128 + 128]
            rest = rows[:, LAT:]
            out[i, 4 * HALF :] = jnp.concatenate([rest[:QUARTER], rest[QUARTER:]], axis=1)
            return carry

        lax.fori_loop(0, STORE, fold_block, 0)


def routes(pair, owner, lengths, row_pick, stored):
    smem = pl.BlockSpec(memory_space=pltpu.SMEM)
    vmem = pl.BlockSpec(memory_space=pltpu.VMEM)
    return pl.pallas_call(
        routes_kernel,
        out_shape=[
            jax.ShapeDtypeStruct((STORE + 1, FOLD, 128), BF),
            jax.ShapeDtypeStruct((STORE + 1, FOLD, 128), BF),
            jax.ShapeDtypeStruct((2 * ROWS,), I32),
            jax.ShapeDtypeStruct((16,), I32),
        ],
        in_specs=[smem] * 4 + [vmem],
        out_specs=[vmem, vmem, smem, smem],
        compiler_params=pltpu.CompilerParams(vmem_limit_bytes=16 * 1024 * 1024),
        name="routes",
    )(pair, owner, lengths, row_pick, stored)


def overflow_kernel(own_ref, *refs):
    ins, out_ref, hold, sems = refs[:3], refs[3], refs[4], refs[5]
    copies = [
        pltpu.make_async_copy(
            ref.at[USUAL_CAP, pl.ds(0, QUARTER), pl.ds(0, 128)], hold.at[i], sems.at[i]
        )
        for i, ref in enumerate(ins)
    ]
    for copy in copies:
        copy.start()
    for copy in copies:
        copy.wait()
    most = jnp.maximum(jnp.maximum(hold[0], hold[1]), jnp.maximum(hold[2], own_ref[...]))
    out_ref[0] = jnp.max(most.astype(F32)).astype(I32)


def overflow(own, arrays):
    vmem = pl.BlockSpec(memory_space=pltpu.VMEM)
    return pl.pallas_call(
        overflow_kernel,
        out_shape=jax.ShapeDtypeStruct((1,), I32),
        in_specs=[vmem] + [ANY] * 3,
        out_specs=pl.BlockSpec(memory_space=pltpu.SMEM),
        scratch_shapes=[pltpu.VMEM((3, QUARTER, 128), BF), pltpu.SemaphoreType.DMA((3,))],
        name="overflow",
    )(own, *arrays)


def pack_kernel(cap, place_ref, flags_ref, len_ref, off_ref, over_ref, *refs):
    ins, outs = refs[:10], refs[10:18]
    y, x = place_ref[0], place_ref[1]
    for path in range(2):
        sources = ins[path * 5 : path * 5 + 5]
        for out in outs[path * 4 + 1 : path * 4 + 4]:
            out[cap, :QUARTER] = over_ref[...]
        along, across = (x, y) if path == 0 else (y, x)
        for kd, shift in enumerate(RELS):
            there = lax.rem(across + shift, 4)
            dest = there * 4 + x if path == 0 else y * 4 + there
            counts, offsets, starts = [], [], []
            total = jnp.int32(0)
            for s in range(4):
                p = y * 4 + s if path == 0 else s * 4 + x
                n = flags_ref[path * 4 + kd, p] * len_ref[p, dest]
                counts.append(n)
                offsets.append(off_ref[p, dest])
                starts.append(total)
                total = total + n
            for ks, near in enumerate(RELS):
                s = lax.rem(along + near, 4)
                n, o, d = pick4(s, counts), pick4(s, offsets), pick4(s, starts)
                n = jnp.minimum(n, jnp.maximum(cap - d, 0))

                def move_from(source, shift):
                    def move(i, carry):
                        outs[path * 4 + kd][d + i] = source[o + i - shift]
                        return carry

                    return move

                if ks < 3:
                    lax.fori_loop(0, n, move_from(sources[ks], 0), 0)
                else:
                    early = jnp.clip(SPLIT + 1 - o, 0, n)
                    lax.fori_loop(0, early, move_from(sources[3], 0), 0)
                    lax.fori_loop(early, n, move_from(sources[4], SPLIT), 0)


def pack(cap, place, flags, len_of, off_of, over, arrays):
    own = jax.ShapeDtypeStruct((cap, FOLD, 128), BF)
    sent = jax.ShapeDtypeStruct((cap + 1, FOLD, 128), BF)
    smem = pl.BlockSpec(memory_space=pltpu.SMEM)
    vmem = pl.BlockSpec(memory_space=pltpu.VMEM)
    return pl.pallas_call(
        functools.partial(pack_kernel, cap),
        out_shape=[own, sent, sent, sent] * 2,
        in_specs=[smem] * 4 + [vmem] * 11,
        out_specs=[vmem] * 8,
        compiler_params=pltpu.CompilerParams(vmem_limit_bytes=40 * 1024 * 1024),
        name="pack",
    )(place, flags, len_of, off_of, over, *arrays)


def column_of(row, width=128):
    return jnp.transpose(jnp.broadcast_to(row, (width, QS)))


def row_of(column):
    return jnp.transpose(jnp.broadcast_to(column, (QS, 128)))[:8]


def draft_scores(query, fresh):
    raw = (
        lax.dot_general(query, fresh, (((1,), (1,)), ((), ())), preferred_element_type=F32)
        * score_scale
    )
    step = lax.broadcasted_iota(I32, raw.shape, 0) // HEADS
    token = lax.broadcasted_iota(I32, raw.shape, 1)
    return jnp.where(token <= step, raw, -jnp.inf)


def bias_row(group, filled):
    token = lax.rem(lax.broadcasted_iota(I32, (1, 2 * CHUNK), 1), CHUNK)
    return jnp.where(token // BLK + group * GROUP < filled, 0.0, -jnp.inf)


def products(query, keys):
    return lax.dot_general(query, keys, (((1,), (1,)), ((), ())), preferred_element_type=F32)


def fold(op, wide):
    return op(op(wide[:, :128], wide[:, 128:256]), op(wide[:, 256:384], wide[:, 384:]))


def unfold(folded):
    tiles = [folded[k * HALF : k * HALF + HALF] for k in range(4)]
    rest = folded[4 * HALF :]
    rest = jnp.concatenate([rest[:, :64], rest[:, 64:]], axis=0)
    return jnp.concatenate(tiles + [rest], axis=1)


def keys_kernel(cap, meta_ref, place_ref, filled_ref, table_ref, query_ref, fresh_ref, *refs):
    ins = refs[:16]
    keys_ref, top_ref, hold, best, sems = refs[16:]
    row = pl.program_id(0)
    y, x = place_ref[0], place_ref[1]

    def spots(n):
        p = meta_ref[n]
        sy, sx = p // 4, lax.rem(p, 4)
        found = []
        for path in range(2):
            line, inner = (sy, sx) if path == 0 else (sx, sy)
            start = jnp.int32(0)
            for s in range(3):
                other = sy * 4 + s if path == 0 else s * 4 + sx
                start = start + jnp.where(s < inner, filled_ref[other], 0)
            rel = lax.rem(line - (y if path == 0 else x) + 4, 4)
            first = jnp.minimum(start, cap - MOST_M)
            found.append((rel, first, start - first))
        return found

    def each_copy(n, act):
        slot = lax.rem(n, 2)
        found = spots(n)
        for side in range(2):
            for path in range(2):
                rel, first, _ = found[path]
                at = (side * 2 + path) * 4
                for ref, shift in zip(ins[at : at + 4], RELS):
                    @pl.when(rel == shift)
                    def _():
                        act(
                            pltpu.make_async_copy(
                                ref.at[pl.ds(first, MOST_M)],
                                hold.at[slot, side, path, pl.ds(0, MOST_M)],
                                sems.at[slot, side, path],
                            )
                        )

    @pl.when(row == 0)
    def _():
        each_copy(jnp.int32(0), lambda c: c.start())

    @pl.when(row + 1 < ROWS)
    def _():
        each_copy(row + 1, lambda c: c.start())

    each_copy(row, lambda c: c.wait())
    slot = lax.rem(row, 2)
    found = spots(row)
    filled = meta_ref[ROWS + row]
    query = query_ref[0]
    draft = draft_scores(query, fresh_ref[0])
    best[...] = jnp.full((QS, 128), -jnp.inf, F32)
    for group in range(2):
        @pl.when(group * GROUP < filled)
        def _():
            for side in range(2):
                parts = []
                for path in range(2):
                    at = found[path][2] + group * GROUP
                    for i in range(GROUP):
                        block = unfold(hold[slot, side, path, at + i])
                        live = i + group * GROUP < filled
                        parts.append(jnp.where(live, block, jnp.zeros_like(block)))
                packed = jnp.concatenate(parts, axis=0)
                keys_ref[0, group, side * CHUNK : side * CHUNK + CHUNK] = jnp.dot(
                    table_ref[...], packed, preferred_element_type=F32
                ).astype(BF)
            raw = products(query, keys_ref[0, group]) + bias_row(group, filled)
            best[...] = jnp.maximum(best[...], fold(jnp.maximum, raw))
    cached = jnp.max(best[...], axis=1, keepdims=True) * score_scale
    peak = row_of(jnp.maximum(cached, jnp.max(draft, axis=1, keepdims=True)))
    top_ref[:, pl.ds(row, 1)] = jnp.broadcast_to(peak[None, :1], (GRP, 1, QS))


def keys_and_top(cap, meta, place, filled, table, queries, fresh, arrays):
    row = lambda *tail: pl.BlockSpec((1,) + tail, lambda i, *_: (i,) + (0,) * len(tail))
    return pl.pallas_call(
        functools.partial(keys_kernel, cap),
        out_shape=[
            jax.ShapeDtypeStruct((ROWS, 2, 2 * CHUNK, KV), BF),
            jax.ShapeDtypeStruct((GRP, ROWS, QS), F32),
        ],
        grid_spec=pltpu.PrefetchScalarGridSpec(
            num_scalar_prefetch=3,
            grid=(ROWS,),
            in_specs=[
                pl.BlockSpec((CHUNK, CHUNK), lambda i, *_: (0, 0)),
                row(QS, KV),
                row(QUARTER, KV),
            ]
            + [ANY] * 16,
            out_specs=[
                row(2, 2 * CHUNK, KV),
                pl.BlockSpec((GRP, ROWS, QS), lambda i, *_: (0, 0, 0)),
            ],
            scratch_shapes=[
                pltpu.VMEM((2, 2, 2, 2 * MOST_M, FOLD, 128), BF),
                pltpu.VMEM((QS, 128), F32),
                pltpu.SemaphoreType.DMA((2, 2, 2)),
            ],
        ),
        compiler_params=pltpu.CompilerParams(vmem_limit_bytes=VMEM_LIMIT),
        name="keys",
    )(meta, place, filled, table, queries, fresh, *arrays)


def sums_kernel(places, meta_ref, order_ref, keys_ref, query_ref, fresh_ref, *refs):
    top_ref, outs, acc, total = refs[0], refs[1:-2], refs[-2], refs[-1]
    step = pl.program_id(0)
    row = order_ref[step]
    filled = meta_ref[ROWS + row]
    query = query_ref[0]
    peak = column_of(jnp.max(top_ref[:, pl.ds(row, 1)], axis=0))
    for group in range(2):
        def add():
            keys = keys_ref[0, group]
            raw = products(query, keys) * score_scale + bias_row(group, filled)
            weights = jnp.exp(raw - jnp.concatenate([peak] * 4, axis=1))
            part = jnp.dot(weights.astype(BF), keys[:, :LAT], preferred_element_type=F32)
            if group == 0:
                total[...] = fold(jnp.add, weights)
                acc[...] = part
            else:
                total[...] += fold(jnp.add, weights)
                acc[...] += part

        if group == 0:
            add()
        else:
            pl.when(group * GROUP < filled)(add)

    if places[-1] == 0:
        @pl.when(step == len(places) - 1)
        def _():
            fresh = fresh_ref[0]
            weights = jnp.exp(draft_scores(query, fresh) - peak[:, :QUARTER])
            acc[...] += jnp.dot(weights.astype(BF), fresh[:, :LAT], preferred_element_type=F32)
            lane = lax.broadcasted_iota(I32, (QS, 128), 1)
            extra = jnp.sum(weights, axis=1, keepdims=True)
            total[...] += jnp.where(lane == 0, extra, 0.0)

    shares = row_of(jnp.sum(total[...], axis=1, keepdims=True))
    if len(places) == 1:
        cut = QS // 2
        outs[0][...] = acc[:cut]
        outs[1][:cut] = acc[cut:]
        outs[1][cut:, :QS] = shares
        outs[1][cut:, QS:] = jnp.zeros((RED - QS, LAT - QS), F32)
        return
    for i in range(len(places)):
        @pl.when(step == i)
        def _():
            outs[i][:QS] = acc[...]
            outs[i][QS:, :QS] = shares
            outs[i][QS:, QS:] = jnp.zeros((RED - QS, LAT - QS), F32)


def sums(places, order, meta, keys, queries, fresh, top):
    count = len(places)
    heights = [QS // 2, RED - QS // 2] if count == 1 else [RED] * count
    row = lambda *tail: pl.BlockSpec((1,) + tail, lambda i, m, o: (o[i],) + (0,) * len(tail))
    return pl.pallas_call(
        functools.partial(sums_kernel, places),
        out_shape=[jax.ShapeDtypeStruct((n, LAT), F32) for n in heights],
        grid_spec=pltpu.PrefetchScalarGridSpec(
            num_scalar_prefetch=2,
            grid=(count,),
            in_specs=[row(2, 2 * CHUNK, KV), row(QS, KV), row(QUARTER, KV)]
            + [pl.BlockSpec((GRP, ROWS, QS), lambda i, m, o: (0, 0, 0))],
            out_specs=[pl.BlockSpec((n, LAT), lambda i, m, o: (0, 0)) for n in heights],
            scratch_shapes=[pltpu.VMEM((QS, LAT), F32), pltpu.VMEM((QS, 128), F32)],
        ),
        compiler_params=pltpu.CompilerParams(vmem_limit_bytes=VMEM_LIMIT),
        name="sums",
    )(meta, order, keys, queries, fresh, top)


def join_kernel(up_ref, top_ref, down_ref, bottom_ref, up_out, down_out):
    cut = QS // 2
    up_out[:cut] = up_ref[:cut] + top_ref[...]
    up_out[cut:] = up_ref[cut:]
    down_out[:cut] = down_ref[:cut]
    down_out[cut:] = down_ref[cut:] + bottom_ref[...]


def join(up, top, down, bottom):
    vmem = pl.BlockSpec(memory_space=pltpu.VMEM)
    return pl.pallas_call(
        join_kernel,
        out_shape=[jax.ShapeDtypeStruct((RED, LAT), F32)] * 2,
        in_specs=[vmem] * 4,
        out_specs=[vmem] * 2,
        compiler_params=pltpu.CompilerParams(vmem_limit_bytes=24 * 1024 * 1024),
        name="join",
    )(up, top, down, bottom)


def finish_kernel(a_ref, b_ref, c_ref, top_ref, bottom_ref):
    whole = a_ref[...] + (b_ref[...] + c_ref[...])
    total = jnp.transpose(jnp.broadcast_to(whole[QS : QS + 1, :QS], (128, QS)))
    total = jnp.concatenate([total] * 4, axis=1)
    out = (whole[:QS] / total).astype(BF)
    top_ref[...] = out[: QS // 2]
    bottom_ref[...] = out[QS // 2 :]


def finish(own, left, right):
    vmem = pl.BlockSpec(memory_space=pltpu.VMEM)
    return pl.pallas_call(
        finish_kernel,
        out_shape=[jax.ShapeDtypeStruct((QS // 2, LAT), BF)] * 2,
        in_specs=[vmem] * 3,
        out_specs=[vmem] * 2,
        compiler_params=pltpu.CompilerParams(vmem_limit_bytes=24 * 1024 * 1024),
        name="finish",
    )(own, left, right)


def place_kernel(grp_ref, *refs):
    ins, out_ref = refs[:16], refs[16]
    step = pl.program_id(0)
    for d in range(8):
        @pl.when(step == d)
        def _():
            out_ref[0, : QS // 2] = ins[2 * d][...]
            out_ref[0, QS // 2 :] = ins[2 * d + 1][...]


def put_in_place(grp, pieces):
    return pl.pallas_call(
        place_kernel,
        out_shape=jax.ShapeDtypeStruct((ROWS, QS, LAT), BF),
        grid_spec=pltpu.PrefetchScalarGridSpec(
            num_scalar_prefetch=1,
            grid=(ROWS,),
            in_specs=[pl.BlockSpec(memory_space=pltpu.VMEM)] * 16,
            out_specs=pl.BlockSpec((1, QS, LAT), lambda i, g: (lax.rem(g[0] + i, GRP), 0, 0)),
        ),
        compiler_params=pltpu.CompilerParams(vmem_limit_bytes=16 * 1024 * 1024),
        name="place",
    )(grp, *pieces)


def attention(cap, turn, grp, orders, place, filled, meta, table, queries, fresh, arrays):
    keys, top = keys_and_top(cap, meta, place, filled, table, queries, fresh, arrays)

    top = lax.all_to_all(top, "grp", 0, 0, tiled=True)

    part = lambda *places: sums(places, orders[places], meta, keys, queries, fresh, top)
    far_top, far_bottom = part(4)
    up3, down3 = part(3, 5)
    up2, down2 = part(2, 6)
    up1, down1, own = part(1, 7, 0)

    up, down = turn(far_top, 1), turn(far_bottom, -1)
    up, down = join(up3, up, down3, down)
    up, down = turn(up, 1), turn(down, -1)
    up, down = turn(up2 + up, 1), turn(down2 + down, -1)
    up, down = turn(up1 + up, 1), turn(down1 + down, -1)
    top_half, bottom_half = finish(own, up, down)

    got = [[top_half, bottom_half]] + [[None, None] for _ in range(7)]
    for d in (1, 2, 3):
        for h in range(2):
            got[8 - d][h] = turn(got[(9 - d) % 8][h], 1)
            got[d][h] = turn(got[d - 1][h], -1)
    got[4] = [turn(got[5][0], 1), turn(got[3][1], -1)]
    return put_in_place(grp[None], [half for pieces in got for half in pieces])


def body(coeffs, lengths, owners, row_pick, queries, new_latent):
    stored = coeffs[0, 0, 0]
    pair = lax.axis_index("pair").astype(I32)
    grp = lax.axis_index("grp").astype(I32)
    place = jnp.stack([pair // 4, pair % 4])

    owner = owners[:, 0]
    a_own, b_own, meta, filled = routes(pair[None], owner, lengths, row_pick, stored)

    send = lambda v, perm: lax.ppermute(v, "pair", perm)
    a_prev, a_next = send(a_own, x_perm(1)), send(a_own, x_perm(-1))
    b_prev, b_next = send(b_own, y_perm(1)), send(b_own, y_perm(-1))

    named = owner.reshape(16, 4)[:, :, None] == jnp.arange(16, dtype=I32)[None, None, :]
    earlier = jnp.arange(4)[None, :] < jnp.arange(4)[:, None]
    offsets = jnp.sum(jnp.where(earlier[None], lengths[:, None, :], 0), axis=2)
    len_of = jnp.sum(jnp.where(named, lengths[:, :, None], 0), axis=1)
    off_of = jnp.sum(jnp.where(named, offsets[:, :, None], 0), axis=1)
    fresh = jnp.concatenate([new_latent, jnp.zeros((ROWS, QUARTER - STEPS, KV), BF)], axis=1)
    table = spread_table()

    orders = {
        places: (grp + jnp.array(places, I32)) % ROWS
        for places in ((4,), (3, 5), (2, 6), (1, 7, 0))
    }
    a_prev, b_prev, place, len_of, off_of, fresh, table, orders = (
        lax.optimization_barrier(
            (a_prev, b_prev, place, len_of, off_of, fresh, table, orders)
        )
    )

    def relay(prv, nxt, perm):
        return send(prv[: SPLIT + 1], perm(1)), send(nxt[SPLIT:], perm(-1))

    line_a = (a_own, a_next, a_prev) + relay(a_prev, a_next, x_perm)
    line_b = (b_own, b_next, b_prev) + relay(b_prev, b_next, y_perm)

    heard = lambda v: [w[FLAG, 0, :17] for w in v[:3]] + [v[4][FLAG - SPLIT, 0, :17]]
    told = jnp.stack(heard(line_b) + heard(line_a))
    all_flags = told[:, :16].astype(I32)
    line_over = jnp.broadcast_to(jnp.max(told[4:, 16]), (QUARTER, 128))

    across = lambda v: lax.ppermute(v, "side", [(0, 1), (1, 0)])

    def second_hop(own, nxt, prv, opp, perm):
        return own, send(prv, perm(-1)), send(nxt, perm(1)), send(opp, perm(2))

    def exchange(cap):
        packed = pack(cap, place, all_flags, len_of, off_of, line_over, line_a + line_b)
        here = second_hop(*packed[:4], y_perm) + second_hop(*packed[4:], x_perm)
        return here + tuple(across(v) for v in here)

    arrays = exchange(USUAL_CAP)
    seen = overflow(line_over, arrays[1:4])
    turn = lambda v, shift: lax.ppermute(v, "grp", ring(shift))
    flat_queries = queries.reshape(ROWS, QS, KV)

    def attend(cap, arrays):
        return attention(
            cap, turn, grp, orders, place, filled, meta, table, flat_queries, fresh, arrays
        )

    out = lax.cond(
        seen[0] > 0,
        lambda: attend(MOST_CAP, exchange(MOST_CAP)),
        lambda: attend(USUAL_CAP, arrays),
    )
    return out.reshape(ROWS, STEPS, HEADS, LAT)


def solution(mesh):
    return jax.shard_map(
        body,
        mesh=mesh,
        in_specs=(
            P("pair", "side", "grp", None, None, None),
            P(),
            P(),
            P("pair"),
            P("pair", None, "side", None),
            P("pair", None, None),
        ),
        out_specs=P("pair", None, "side", None),
        check_vma=False,
    )
```
